32 devices in a mesh: win: 8 (over y, x, core), tok: 4 (over z).
Axes of the slice: x: 2, y: 2, z: 4, core: 2. Of those that a mesh axis runs over, the one named last changes fastest.
Arguments:
- field_tokens: bfloat16 [8, 40, 40, 1280], P('win', 'tok'), may hold values from -60 to 60
- lon_shift: int32 [4], replicated, may hold values from 1 to 20, as said below
- norm_gain: float32 [1280], replicated, may hold values from 0.1 to 1.9
- qkv_weight: bfloat16 [1280, 1920], replicated, may hold values from -1 to 1
- out_weight: bfloat16 [640, 1280], replicated, may hold values from -0.25 to 0.25
Outputs:
- result: bfloat16 [8, 40, 40, 1280], P('win', 'tok')
The draws below stay inside these ranges and needn't reach their ends.
Inputs may be any that keep to these rules, and one draw needn't show every extreme that they name: `lon_shift`: one entry is 20 and another is 1.
All inputs are finite; a program needn't handle non-finite values.
Results may differ from the reference program's by a relative error of at most 0.0046.
Values may be sent and summed in bfloat16 or wider, within the bound.
No kernel may reach another device: no remote copies, remote signals or barrier semaphores. Data moves between devices by JAX's collectives and lax.ppermute only.
A program may use at most 64 MiB of HBM per device.

```python
import jax
import jax.numpy as jnp
from jax import lax

D = 1280
HEADS = 8
HD = 80
WS = 40
LAT_WINDOWS = 4
WINDOWS = 8
N_WIN = 8


def draw_lon_shift(key, part):
    sample = jax.random.randint(jax.random.fold_in(key, 11), (LAT_WINDOWS,), 1, WS // 2 + 1)
    chosen = jax.random.permutation(jax.random.fold_in(key, 12), LAT_WINDOWS)
    sample = sample.at[chosen[0]].set(WS // 2)
    sample = sample.at[chosen[1]].set(1)
    return sample.astype(jnp.int32)


def draw_qkv_weight(key, part):
    width = HEADS * HD
    sample = jax.random.normal(jax.random.fold_in(key, 21), (D, 3 * width), jnp.float32) * (2.0 / D) ** 0.5
    return jnp.clip(sample, -1.0, 1.0).astype(jnp.bfloat16)


def draw_field_tokens(key, part):
    shape = (WINDOWS, WS, WS, D)
    sample = jnp.clip(jax.random.normal(jax.random.fold_in(key, 31), shape, jnp.float32), -6.0, 6.0)
    return sample.astype(jnp.bfloat16)


def scatter_about(key, dims, scale, reach, kind=jnp.bfloat16):
    array = jax.random.normal(key, dims, jnp.float32) * scale
    return jnp.minimum(jnp.maximum(array, -reach), reach).astype(kind)


def setup_inputs(seed: int = 0) -> dict:
    key_of = jax.random.split(jax.random.key(seed), 6)
    return {
        "field_tokens": draw_field_tokens(jax.random.fold_in(key_of[5], 71), 0),
        "lon_shift": draw_lon_shift(jax.random.fold_in(key_of[5], 71), 0),
        "norm_gain": jnp.clip(1.0 + 0.18 * jax.random.normal(key_of[2], (D,), jnp.float32), 0.1, 1.9),
        "qkv_weight": draw_qkv_weight(jax.random.fold_in(key_of[5], 71), 0),
        "out_weight": scatter_about(key_of[4], (HEADS * HD, D), (HEADS * HD) ** -0.5, 0.25),
    }


def window_block(window, norm_gain, qkv_weight, out_weight):
    count = WS * WS
    tokens = window.reshape(count, D)
    values = tokens.astype(jnp.float32)
    factor = lax.rsqrt(lax.optimization_barrier(jnp.mean(values * values, axis=-1, keepdims=True)) + 1e-06)
    normed = (values * factor * norm_gain.astype(jnp.float32)).astype(jnp.bfloat16)
    qkv = jnp.dot(normed, qkv_weight, preferred_element_type=jnp.float32).astype(jnp.bfloat16)
    qkv = qkv.reshape(count, 3, HEADS, HD)
    queries = qkv[:, 0].astype(jnp.float32)
    key_rows = qkv[:, 1].astype(jnp.float32)
    value_rows = qkv[:, 2].astype(jnp.float32)
    scores = jnp.einsum('qhd,khd->hqk', queries, key_rows) * HD ** (-0.5)
    row_top = lax.optimization_barrier(jnp.max(scores, axis=-1, keepdims=True))
    exponent = jnp.exp(scores - row_top)
    weights = (exponent / lax.optimization_barrier(jnp.sum(exponent, axis=-1, keepdims=True))).astype(jnp.bfloat16)
    attended = jnp.einsum('hqk,khd->qhd', weights.astype(jnp.float32), value_rows).astype(jnp.bfloat16)
    projected = jnp.dot(attended.reshape(count, HEADS * HD), out_weight, preferred_element_type=jnp.float32)
    return (values + projected).astype(jnp.bfloat16).reshape(WS, WS, D)

def to_band(windows):
    lon_count = N_WIN // LAT_WINDOWS
    band = windows.reshape(lon_count, LAT_WINDOWS, WS, WS, D).transpose(1, 2, 0, 3, 4)
    return band.reshape(LAT_WINDOWS, WS, lon_count * WS, D)

def from_band(band):
    lon_count = N_WIN // LAT_WINDOWS
    windows = band.reshape(LAT_WINDOWS, WS, lon_count, WS, D).transpose(2, 0, 1, 3, 4)
    return windows.reshape(N_WIN, WS, WS, D)

def reference(field_tokens, lon_shift, norm_gain, qkv_weight, out_weight):
    band = to_band(field_tokens)
    moved = jax.vmap(lambda band_rows, amount: jnp.roll(band_rows, -amount, axis=1))(band, lon_shift)
    windows = from_band(moved)
    mixed = lax.map(lambda window: window_block(window, norm_gain, qkv_weight, out_weight), windows)
    mixed_band = to_band(mixed)
    restored = jax.vmap(lambda band_rows, amount: jnp.roll(band_rows, amount, axis=1))(mixed_band, lon_shift)
    return from_band(restored)
```

```python
import functools

import jax
import jax.numpy as jnp
from jax import lax
from jax.experimental import pallas as pl
from jax.experimental.pallas import tpu as pltpu
from jax.sharding import PartitionSpec as P

HEADS = 8
HD = 80
LAT_WINDOWS = 4
LANES = 128
SUBLANES = 8
VMEM_BYTES = 48 * 1024 * 1024


def round_up(value, unit):
    return -(-value // unit) * unit


def shifted(block, axis, distance):
    count = lax.axis_size(axis)
    return lax.ppermute(block, axis, [(i, (i + distance) % count) for i in range(count)])


def project(place, tokens, gain, weight, slots, outs, width):
    groups = len(outs)
    count = tokens.shape[0]
    factor = lax.rsqrt(jnp.mean(tokens * tokens, axis=-1, keepdims=True) + 1e-06)
    normed = (tokens * factor * gain[...]).astype(jnp.bfloat16)
    qkv = jnp.dot(normed, weight[...], preferred_element_type=jnp.float32)
    tail = jnp.ones((count, slots.shape[2] - 3 * width), jnp.float32)
    for group in range(groups):
        columns = [
            qkv[:, (kind * groups + group) * width : (kind * groups + group + 1) * width]
            for kind in range(3)
        ]
        slot = lax.rem(group - place[0] + groups, groups)
        slots[slot] = jnp.concatenate(columns + [tail], axis=1).astype(jnp.bfloat16)
    for slot in range(groups):
        outs[slot][...] = slots[slot]


def kept_kernel(split, width, place, field, gain, weight, *refs):
    *outs, slots = refs
    rows, columns, features = field.shape
    tokens = field[...].astype(jnp.float32)[:, split:]
    tokens = tokens.reshape(rows * (columns - split), features)
    project(place, tokens, gain, weight, slots, outs, width)


def mixed_kernel(split, width, place, field, eastern, gain, weight, *refs):
    *outs, slots = refs
    rows, _, features = field.shape
    own = field[...].astype(jnp.float32)[:, :split]
    column = lax.broadcasted_iota(jnp.int32, own.shape, 1)
    tokens = jnp.where(column < place[1], eastern[...].astype(jnp.float32), own)
    project(place, tokens.reshape(rows * split, features), gain, weight, slots, outs, width)


def folded_rows(count, fold):
    return round_up(-(-count // fold), SUBLANES)


def attention_kernel(width, blocks, *refs):
    ins, outs = refs[:blocks], refs[blocks : 2 * blocks]
    held, keys, attended = refs[2 * blocks :]
    start = 0
    for block in ins:
        held[start : start + block.shape[0]] = block[...]
        start += block.shape[0]
    total = start
    span = 2 * LANES
    key_at = width // LANES * LANES
    value_at = 2 * width // LANES * LANES
    keys[...] = held[:, key_at : key_at + span].T
    factor = HD ** (-0.5) * 1.4426950408889634
    step = attended.shape[0] // 10

    def one_step(index, carry):
        at = pl.multiple_of(index * step, 16)
        queries = held[pl.ds(at, step), :span]
        queries = pltpu.roll(queries.astype(jnp.float32), width - key_at, axis=1)
        lane = lax.broadcasted_iota(jnp.int32, queries.shape, 1)
        value_lane = lax.broadcasted_iota(jnp.int32, (step, span), 1)
        result = None
        for head in range(width // HD):
            first = width - key_at + head * HD
            inside = (lane >= first) & (lane < first + HD)
            chosen = jnp.where(inside, queries, 0.0).astype(jnp.bfloat16)
            scores = jnp.dot(chosen, keys[...], preferred_element_type=jnp.float32)
            top = jnp.max(scores, axis=-1, keepdims=True)
            weights = jnp.exp2((scores - top) * factor).astype(jnp.bfloat16)
            mixed = jnp.dot(
                weights, held[:, value_at : value_at + span], preferred_element_type=jnp.float32
            )
            ones_at = 3 * width - value_at
            scaled = mixed / mixed[:, ones_at : ones_at + 1]
            first = 2 * width - value_at + head * HD
            result = scaled if result is None else jnp.where(value_lane < first, result, scaled)
        attended[pl.ds(at, step)] = pltpu.roll(result, span - (2 * width - value_at), axis=1)
        return carry

    lax.fori_loop(0, attended.shape[0] // step, one_step, 0)

    rest = width - LANES
    fold = LANES // rest
    start = 0
    for block, out in zip(ins, outs):
        count = block.shape[0]
        part = folded_rows(count, fold)
        lane = lax.broadcasted_iota(jnp.int32, (part, LANES), 1)
        packed = jnp.zeros((part, LANES), jnp.float32)
        for index in range(fold):
            size = min(part, count - index * part)
            piece = attended[start + index * part : start + index * part + size, LANES:]
            if size < part:
                piece = jnp.concatenate([piece, jnp.zeros((part - size, LANES), jnp.float32)], axis=0)
            if index:
                piece = pltpu.roll(piece, index * rest, axis=1)
            packed = jnp.where(lane // rest == index, piece, packed)
        out[...] = jnp.concatenate(
            [attended[start : start + count, :LANES], packed], axis=0
        ).astype(jnp.bfloat16)
        start += count


def unpack(blocks, count, rest):
    fold = LANES // rest
    part = folded_rows(count, fold)
    mains = [block[:count] for block in blocks]
    lane = lax.broadcasted_iota(jnp.int32, (part, LANES), 1)
    rests = []
    for index in range(fold):
        row = jnp.zeros((part, LANES), jnp.float32)
        for group, block in enumerate(blocks):
            turn = ((group - index) * rest) % LANES
            piece = block[count : count + part]
            piece = pltpu.roll(piece, turn, axis=1) if turn else piece
            row = jnp.where(lane // rest == group, piece, row)
        rests.append(row[: min(part, count - index * part)])
    return jnp.concatenate(mains + [jnp.concatenate(rests, axis=0)], axis=1)


def output_kernel(split, width, groups, place, field, weight, *refs):
    kept, mixed, western = refs[:groups], refs[groups : 2 * groups], refs[2 * groups : 3 * groups]
    out, ordered = refs[3 * groups :]
    rows, columns, features = field.shape
    rest = width - LANES
    fold = LANES // rest
    for slot in range(groups):
        group = lax.rem(place[0] + slot, groups)
        at = pl.multiple_of(group * width, rest)
        ordered[slot * LANES : (slot + 1) * LANES] = weight[pl.ds(at, LANES)]
        at = pl.multiple_of(group * width + LANES, rest)
        first = groups * LANES + slot * rest
        ordered[first : first + rest] = weight[pl.ds(at, rest)]
    tokens = field[...].astype(jnp.float32)

    count = rows * (columns - split)
    blocks = [block[...].astype(jnp.float32) for block in kept]
    attended = unpack(blocks, count, rest).astype(jnp.bfloat16)
    projected = jnp.dot(attended, ordered[...], preferred_element_type=jnp.float32)
    right = tokens[:, split:] + projected.reshape(rows, columns - split, features)

    count = rows * split
    part = folded_rows(count, fold)
    shape = mixed[0].shape
    row = lax.broadcasted_iota(jnp.int32, shape, 0)
    lane = lax.broadcasted_iota(jnp.int32, shape, 1)
    token = jnp.where(row < count, row, row - count + lane // rest * part)
    taken = lax.rem(token, split) < place[1]
    blocks = [
        jnp.where(taken, west[...].astype(jnp.float32), own[...].astype(jnp.float32))
        for own, west in zip(mixed, western)
    ]
    attended = unpack(blocks, count, rest).astype(jnp.bfloat16)
    projected = jnp.dot(attended, ordered[...], preferred_element_type=jnp.float32)
    left = tokens[:, :split] + projected.reshape(rows, split, features)
    out[...] = jnp.concatenate([left, right], axis=1).astype(jnp.bfloat16)


def whole(count):
    return [pl.BlockSpec(memory_space=pltpu.VMEM)] * count


def shards(field_tokens, lon_shift, norm_gain, qkv_weight, out_weight):
    _, rows, columns, features = field_tokens.shape
    groups = lax.axis_size("tok")
    width = HEADS // groups * HD
    padded = round_up(3 * width + 1, LANES)
    split = round_up(columns // 2, SUBLANES)
    latitude = lax.axis_index("win") % LAT_WINDOWS
    offset = lax.dynamic_index_in_dim(lon_shift, latitude, 0, keepdims=False)
    place = jnp.stack([lax.axis_index("tok").astype(jnp.int32), offset])
    field = field_tokens[0]
    gain = norm_gain.reshape(1, features)
    smem = pl.BlockSpec(memory_space=pltpu.SMEM)
    params = pltpu.CompilerParams(vmem_limit_bytes=VMEM_BYTES)

    def projection(kernel, count, *operands):
        block = jax.ShapeDtypeStruct((count, padded), jnp.bfloat16)
        return pl.pallas_call(
            functools.partial(kernel, split, width),
            out_shape=[block] * groups,
            in_specs=[smem] + whole(len(operands) + 2),
            out_specs=whole(groups),
            scratch_shapes=[pltpu.VMEM((groups, count, padded), jnp.bfloat16)],
            compiler_params=params,
            cost_estimate=pl.CostEstimate(
                flops=2 * count * features * 3 * HEADS * HD,
                bytes_accessed=2 * features * (3 * HEADS * HD + 2 * count),
                transcendentals=0,
            ),
        )(place, *operands, gain, qkv_weight)

    def spread(blocks, sign):
        return [blocks[0]] + [
            shifted(blocks[distance], "tok", sign * distance) for distance in range(1, groups)
        ]

    eastern = shifted(field[:, :split], "win", -LAT_WINDOWS)
    kept_count, mixed_count = rows * (columns - split), rows * split
    kept = spread(projection(kept_kernel, kept_count, field), 1)
    mixed = spread(projection(mixed_kernel, mixed_count, field, eastern), 1)

    total = groups * rows * columns
    fold = LANES // (width - LANES)
    packed = [
        jax.ShapeDtypeStruct((count + folded_rows(count, fold), LANES), jnp.bfloat16)
        for count in (kept_count, mixed_count)
        for _ in range(groups)
    ]
    attended = pl.pallas_call(
        functools.partial(attention_kernel, width, 2 * groups),
        out_shape=packed,
        in_specs=whole(2 * groups),
        out_specs=whole(2 * groups),
        scratch_shapes=[
            pltpu.VMEM((total, padded), jnp.bfloat16),
            pltpu.VMEM((2 * LANES, total), jnp.bfloat16),
            pltpu.VMEM((total, 2 * LANES), jnp.float32),
        ],
        compiler_params=params,
        cost_estimate=pl.CostEstimate(
            flops=4 * total * total * width,
            bytes_accessed=2 * total * (padded + width),
            transcendentals=total * total * (width // HD),
        ),
    )(*kept, *mixed)
    mixed_back = spread(attended[groups:], -1)
    western = [shifted(block, "win", LAT_WINDOWS) for block in mixed_back]
    kept_back = spread(attended[:groups], -1)

    result = pl.pallas_call(
        functools.partial(output_kernel, split, width, groups),
        out_shape=jax.ShapeDtypeStruct(field.shape, jnp.bfloat16),
        in_specs=[smem] + whole(2 + 3 * groups),
        out_specs=pl.BlockSpec(memory_space=pltpu.VMEM),
        scratch_shapes=[pltpu.VMEM(out_weight.shape, jnp.bfloat16)],
        compiler_params=params,
        cost_estimate=pl.CostEstimate(
            flops=2 * rows * columns * HEADS * HD * features,
            bytes_accessed=2 * features * (HEADS * HD + 2 * rows * columns),
            transcendentals=0,
        ),
    )(place, field, out_weight, *kept_back, *mixed_back, *western)
    return result[None]


def solution(mesh):
    placed = (P("win", "tok", None, None), P(), P(), P(), P())
    return jax.shard_map(
        shards, mesh=mesh, in_specs=placed, out_specs=P("win", "tok", None, None), check_vma=False
    )
```

```python
import functools

import jax
import jax.numpy as jnp
from jax import lax
from jax.experimental import pallas as pl
from jax.experimental.pallas import tpu as pltpu
from jax.sharding import PartitionSpec as P

HEADS = 8
HD = 80
LAT_WINDOWS = 4
LANES = 128
SUBLANES = 8
VMEM_BYTES = 48 * 1024 * 1024


def round_up(value, unit):
    return -(-value // unit) * unit


def shifted(block, axis, distance):
    count = lax.axis_size(axis)
    return lax.ppermute(block, axis, [(i, (i + distance) % count) for i in range(count)])


def column_offset(lon_shift):
    return lon_shift[lax.rem(lax.axis_index("win"), LAT_WINDOWS)]


def project(tokens, gain, weight, slots, outs):
    local = HEADS // slots.shape[0]
    groups = slots.shape[0]
    count, features = tokens.shape
    span = slots.shape[2] // local
    factor = lax.rsqrt(jnp.mean(tokens * tokens, axis=-1, keepdims=True) + 1e-06)
    normed = (tokens * factor * gain[...].reshape(1, features)).astype(jnp.bfloat16)
    qkv = jnp.dot(normed, weight[...], preferred_element_type=jnp.float32)
    tail = jnp.ones((count, span - 3 * HD), jnp.float32)
    place = lax.axis_index("tok")
    for group in range(groups):
        slot = lax.rem(group - place + groups, groups)
        columns = []
        for head in range(group * local, (group + 1) * local):
            columns += [
                qkv[:, (kind * HEADS + head) * HD : (kind * HEADS + head + 1) * HD]
                for kind in range(3)
            ] + [tail]
        slots[slot] = jnp.concatenate(columns, axis=1).astype(jnp.bfloat16)
    parts = len(outs) // groups
    for index, out in enumerate(outs):
        first = index // groups * out.shape[1]
        out[...] = slots[index % groups, :, first : first + out.shape[1]]


def kept_kernel(split, field, gain, weight, *refs):
    *outs, slots = refs
    rows, columns, features = field.shape
    tokens = field[...].astype(jnp.float32)[:, split:]
    project(tokens.reshape(rows * (columns - split), features), gain, weight, slots, outs)


def mixed_kernel(split, lon_shift, field, eastern, gain, weight, *refs):
    *outs, slots = refs
    rows, _, features = field.shape
    own = field[...].astype(jnp.float32)[:, :split]
    column = lax.broadcasted_iota(jnp.int32, own.shape, 1)
    tokens = jnp.where(column < column_offset(lon_shift), eastern[...].astype(jnp.float32), own)
    project(tokens.reshape(rows * split, features), gain, weight, slots, outs)


def folded_rows(count, fold):
    return round_up(-(-count // fold), SUBLANES)


def attend(head, kept, mixed, held, keys, scores, weights, attended):
    span = held.shape[1]
    start = 0
    for block in kept:
        held[start : start + block.shape[0]] = block[:, head * span : (head + 1) * span]
        start += block.shape[0]
    for block in mixed:
        held[start : start + block.shape[0]] = block[...]
        start += block.shape[0]
    keys[...] = held[...].T
    factor = HD ** (-0.5) * 1.4426950408889634
    step = scores[0].shape[0]
    chunk = 16

    def score(index, out):
        queries = held[index * step : (index + 1) * step].astype(jnp.float32)
        queries = pltpu.roll(queries, HD, axis=1)
        lane = lax.broadcasted_iota(jnp.int32, queries.shape, 1)
        queries = jnp.where((lane >= HD) & (lane < 2 * HD), queries, 0.0).astype(jnp.bfloat16)
        out[...] = jnp.dot(queries, keys[...], preferred_element_type=jnp.float32)

    steps = start // step
    score(0, scores[0])
    for index in range(steps):
        if index + 1 < steps:
            score(index + 1, scores[(index + 1) % 2])
        now, out = scores[index % 2], weights[index % 2]
        for first in range(0, step, chunk):
            part = now[first : first + chunk]
            top = jnp.max(part, axis=-1, keepdims=True)
            out[first : first + chunk] = jnp.exp2((part - top) * factor).astype(jnp.bfloat16)
        mixed_values = jnp.dot(out[...], held[...], preferred_element_type=jnp.float32)
        scaled = mixed_values / mixed_values[:, 3 * HD : 3 * HD + 1]
        attended[index * step : (index + 1) * step] = pltpu.roll(scaled, span - 2 * HD, axis=1)[
            :, :LANES
        ]


def first_head_kernel(groups, *refs):
    kept, mixed, out = refs[:groups], refs[groups : 2 * groups], refs[2 * groups]
    held, keys, *rest = refs[2 * groups + 1 :]
    attend(0, kept, mixed, held, keys, rest[:2], rest[2:4], rest[4])
    out[...] = rest[4][...].astype(jnp.bfloat16)


def second_head_kernel(groups, width, *refs):
    kept, mixed, other = refs[:groups], refs[groups : 2 * groups], refs[2 * groups]
    outs = refs[2 * groups + 1 : 4 * groups + 1]
    held, keys, *scratch = refs[4 * groups + 1 :]
    attended = scratch[4]
    attend(1, kept, mixed, held, keys, scratch[:2], scratch[2:4], attended)
    rest = width - LANES
    fold = LANES // rest
    start = 0
    for block, out in zip((*kept, *mixed), outs):
        count = block.shape[0]
        part = folded_rows(count, fold)
        lane = lax.broadcasted_iota(jnp.int32, (count, LANES), 1)
        second = pltpu.roll(attended[start : start + count], HD, axis=1)
        main = jnp.where(lane < HD, other[start : start + count].astype(jnp.float32), second)
        ends = attended[start : start + count]
        lane = lax.broadcasted_iota(jnp.int32, (part, LANES), 1)
        packed = jnp.zeros((part, LANES), jnp.float32)
        for index in range(fold):
            size = min(part, count - index * part)
            piece = ends[index * part : index * part + size]
            if size < part:
                piece = jnp.concatenate([piece, jnp.zeros((part - size, LANES), jnp.float32)], axis=0)
            piece = pltpu.roll(piece, (index * rest + HD) % LANES, axis=1)
            packed = jnp.where(lane // rest == index, piece, packed)
        out[...] = jnp.concatenate([main, packed], axis=0).astype(jnp.bfloat16)
        start += count


def unpack(blocks, count, rest):
    fold = LANES // rest
    part = folded_rows(count, fold)
    mains = [block[:count] for block in blocks]
    lane = lax.broadcasted_iota(jnp.int32, (part, LANES), 1)
    rests = []
    for index in range(fold):
        row = jnp.zeros((part, LANES), jnp.float32)
        for group, block in enumerate(blocks):
            turn = ((group - index) * rest) % LANES
            piece = block[count : count + part]
            piece = pltpu.roll(piece, turn, axis=1) if turn else piece
            row = jnp.where(lane // rest == group, piece, row)
        rests.append(row[: min(part, count - index * part)])
    return jnp.concatenate(mains + [jnp.concatenate(rests, axis=0)], axis=1)


def output_kernel(split, width, groups, lon_shift, field, weight, *refs):
    kept, mixed, western = refs[:groups], refs[groups : 2 * groups], refs[2 * groups : 3 * groups]
    out, ordered = refs[3 * groups :]
    rows, columns, features = field.shape
    rest = width - LANES
    fold = LANES // rest
    for slot in range(groups):
        group = lax.rem(lax.axis_index("tok") + slot, groups)
        at = pl.multiple_of(group * width, rest)
        ordered[slot * LANES : (slot + 1) * LANES] = weight[pl.ds(at, LANES)]
        at = pl.multiple_of(group * width + LANES, rest)
        first = groups * LANES + slot * rest
        ordered[first : first + rest] = weight[pl.ds(at, rest)]
    tokens = field[...].astype(jnp.float32)

    count = rows * (columns - split)
    blocks = [block[...].astype(jnp.float32) for block in kept]
    attended = unpack(blocks, count, rest).astype(jnp.bfloat16)
    projected = jnp.dot(attended, ordered[...], preferred_element_type=jnp.float32)
    right = tokens[:, split:] + projected.reshape(rows, columns - split, features)

    count = rows * split
    part = folded_rows(count, fold)
    shape = mixed[0].shape
    row = lax.broadcasted_iota(jnp.int32, shape, 0)
    lane = lax.broadcasted_iota(jnp.int32, shape, 1)
    token = jnp.where(row < count, row, row - count + lane // rest * part)
    taken = lax.rem(token, split) < column_offset(lon_shift)
    blocks = [
        jnp.where(taken, west[...].astype(jnp.float32), own[...].astype(jnp.float32))
        for own, west in zip(mixed, western)
    ]
    attended = unpack(blocks, count, rest).astype(jnp.bfloat16)
    projected = jnp.dot(attended, ordered[...], preferred_element_type=jnp.float32)
    left = tokens[:, :split] + projected.reshape(rows, split, features)
    out[...] = jnp.concatenate([left, right], axis=1).astype(jnp.bfloat16)


def whole(count):
    return [pl.BlockSpec(memory_space=pltpu.VMEM)] * count


def shards(field_tokens, lon_shift, norm_gain, qkv_weight, out_weight):
    _, rows, columns, features = field_tokens.shape
    groups = lax.axis_size("tok")
    local = HEADS // groups
    width = local * HD
    span = round_up(3 * HD + 1, LANES)
    split = round_up(columns // 2, SUBLANES)
    field = field_tokens[0]
    smem = pl.BlockSpec(memory_space=pltpu.SMEM)
    params = pltpu.CompilerParams(vmem_limit_bytes=VMEM_BYTES)
    kept_count, mixed_count = rows * (columns - split), rows * split

    def projection(kernel, count, parts, scalars, operands):
        block = jax.ShapeDtypeStruct((count, local * span // parts), jnp.bfloat16)
        return pl.pallas_call(
            functools.partial(kernel, split),
            out_shape=[block] * (parts * groups),
            in_specs=[smem] * len(scalars) + whole(len(operands) + 2),
            out_specs=whole(parts * groups),
            scratch_shapes=[pltpu.VMEM((groups, count, local * span), jnp.bfloat16)],
            compiler_params=params,
            cost_estimate=pl.CostEstimate(
                flops=2 * count * features * 3 * HEADS * HD,
                bytes_accessed=2 * features * (3 * HEADS * HD + 2 * count),
                transcendentals=0,
            ),
        )(*scalars, *operands, norm_gain, qkv_weight)

    def spread(blocks, sign):
        return [blocks[0]] + [
            shifted(blocks[distance], "tok", sign * distance) for distance in range(1, groups)
        ]

    eastern = shifted(field[:, :split], "win", -LAT_WINDOWS)
    kept = spread(projection(kept_kernel, kept_count, 1, [], [field]), 1)
    mixed = projection(mixed_kernel, mixed_count, local, [lon_shift], [field, eastern])
    first_mixed, second_mixed = spread(mixed[:groups], 1), spread(mixed[groups:], 1)

    total = groups * rows * columns
    step = total // 5
    fold = LANES // (width - LANES)
    packed = [
        jax.ShapeDtypeStruct((count + folded_rows(count, fold), LANES), jnp.bfloat16)
        for count in (kept_count, mixed_count)
        for _ in range(groups)
    ]

    def attention(kernel, out_shape, *operands):
        return pl.pallas_call(
            kernel,
            out_shape=out_shape,
            in_specs=whole(len(operands)),
            out_specs=whole(len(out_shape)),
            scratch_shapes=[
                pltpu.VMEM((total, span), jnp.bfloat16),
                pltpu.VMEM((span, total), jnp.bfloat16),
                pltpu.VMEM((step, total), jnp.float32),
                pltpu.VMEM((step, total), jnp.float32),
                pltpu.VMEM((step, total), jnp.bfloat16),
                pltpu.VMEM((step, total), jnp.bfloat16),
                pltpu.VMEM((total, LANES), jnp.float32),
            ],
            compiler_params=params,
            cost_estimate=pl.CostEstimate(
                flops=4 * total * total * span,
                bytes_accessed=2 * total * (span + LANES),
                transcendentals=total * total,
            ),
        )(*operands)

    (other,) = attention(
        functools.partial(first_head_kernel, groups),
        [jax.ShapeDtypeStruct((total, LANES), jnp.bfloat16)],
        *kept,
        *first_mixed,
    )
    attended = attention(
        functools.partial(second_head_kernel, groups, width), packed, *kept, *second_mixed, other
    )
    mixed_back = spread(attended[groups:], -1)
    western = [shifted(block, "win", LAT_WINDOWS) for block in mixed_back]
    kept_back = spread(attended[:groups], -1)

    result = pl.pallas_call(
        functools.partial(output_kernel, split, width, groups),
        out_shape=jax.ShapeDtypeStruct(field.shape, jnp.bfloat16),
        in_specs=[smem] + whole(2 + 3 * groups),
        out_specs=pl.BlockSpec(memory_space=pltpu.VMEM),
        scratch_shapes=[pltpu.VMEM(out_weight.shape, jnp.bfloat16)],
        compiler_params=params,
        cost_estimate=pl.CostEstimate(
            flops=2 * rows * columns * HEADS * HD * features,
            bytes_accessed=2 * features * (HEADS * HD + 2 * rows * columns),
            transcendentals=0,
        ),
    )(lon_shift, field, out_weight, *kept_back, *mixed_back, *western)
    return result[None]


def solution(mesh):
    placed = (P("win", "tok", None, None), P(), P(), P(), P())
    return jax.shard_map(
        shards, mesh=mesh, in_specs=placed, out_specs=P("win", "tok", None, None), check_vma=False
    )
```

```python
import functools

import jax
import jax.numpy as jnp
from jax import lax
from jax.experimental import pallas as pl
from jax.experimental.pallas import tpu as pltpu
from jax.sharding import PartitionSpec as P

HEADS = 8
HD = 80
LAT_WINDOWS = 4
LANES = 128
SUBLANES = 8
VMEM_BYTES = 48 * 1024 * 1024


def round_up(value, unit):
    return -(-value // unit) * unit


def shifted(block, axis, distance):
    count = lax.axis_size(axis)
    return lax.ppermute(block, axis, [(i, (i + distance) % count) for i in range(count)])


def after(blocks, arrived):
    return [blocks[0]] + [
        lax.optimization_barrier(pair)[0] for pair in zip(blocks[1:], arrived[1:])
    ]


def column_offset(lon_shift):
    return lon_shift[lax.rem(lax.axis_index("win"), LAT_WINDOWS)]


def project(tokens, gain, weight, slots, outs):
    local = HEADS // slots.shape[0]
    groups = slots.shape[0]
    count, features = tokens.shape
    span = slots.shape[2] // local
    factor = lax.rsqrt(jnp.mean(tokens * tokens, axis=-1, keepdims=True) + 1e-06)
    normed = (tokens * factor * gain[...].reshape(1, features)).astype(jnp.bfloat16)
    qkv = jnp.dot(normed, weight[...], preferred_element_type=jnp.float32)
    tail = jnp.ones((count, span - 3 * HD), jnp.float32)
    place = lax.axis_index("tok")
    for group in range(groups):
        slot = lax.rem(group - place + groups, groups)
        columns = []
        for head in range(group * local, (group + 1) * local):
            columns += [
                qkv[:, (kind * HEADS + head) * HD : (kind * HEADS + head + 1) * HD]
                for kind in range(3)
            ] + [tail]
        slots[slot] = jnp.concatenate(columns, axis=1).astype(jnp.bfloat16)
    parts = len(outs) // groups
    for index, out in enumerate(outs):
        first = index // groups * out.shape[1]
        out[...] = slots[index % groups, :, first : first + out.shape[1]]


def kept_kernel(split, field, gain, weight, *refs):
    *outs, slots = refs
    rows, columns, features = field.shape
    tokens = field[...].astype(jnp.float32)[:, split:]
    project(tokens.reshape(rows * (columns - split), features), gain, weight, slots, outs)


def mixed_kernel(split, lon_shift, field, eastern, gain, weight, *refs):
    *outs, slots = refs
    rows, _, features = field.shape
    own = field[...].astype(jnp.float32)[:, :split]
    column = lax.broadcasted_iota(jnp.int32, own.shape, 1)
    tokens = jnp.where(column < column_offset(lon_shift), eastern[...].astype(jnp.float32), own)
    project(tokens.reshape(rows * split, features), gain, weight, slots, outs)


def attention_kernel(head, groups, *refs):
    kept, mixed = refs[:groups], refs[groups : 2 * groups]
    kept_out, mixed_out, held, keys = refs[2 * groups : 2 * groups + 4]
    scores, weights = refs[2 * groups + 4 : 2 * groups + 6], refs[2 * groups + 6 :]
    span = held.shape[1]
    start = 0
    for block in kept:
        held[start : start + block.shape[0]] = block[:, head * span : (head + 1) * span]
        start += block.shape[0]
    for block in mixed:
        held[start : start + block.shape[0]] = block[...]
        start += block.shape[0]
    keys[...] = held[...].T
    factor = HD ** (-0.5) * 1.4426950408889634
    step = scores[0].shape[0]
    chunk = 16

    def score(index, out):
        queries = held[index * step : (index + 1) * step].astype(jnp.float32)
        queries = pltpu.roll(queries, HD, axis=1)
        lane = lax.broadcasted_iota(jnp.int32, queries.shape, 1)
        queries = jnp.where((lane >= HD) & (lane < 2 * HD), queries, 0.0).astype(jnp.bfloat16)
        out[...] = jnp.dot(queries, keys[...], preferred_element_type=jnp.float32)

    steps = start // step
    score(0, scores[0])
    for index in range(steps):
        if index + 1 < steps:
            score(index + 1, scores[(index + 1) % 2])
        now, out = scores[index % 2], weights[index % 2]
        for first in range(0, step, chunk):
            part = now[first : first + chunk]
            top = jnp.max(part, axis=-1, keepdims=True)
            out[first : first + chunk] = jnp.exp2((part - top) * factor).astype(jnp.bfloat16)
        mixed_values = jnp.dot(out[...], held[...], preferred_element_type=jnp.float32)
        scaled = mixed_values / mixed_values[:, 3 * HD : 3 * HD + 1]
        values = pltpu.roll(scaled, span - 2 * HD, axis=1)[:, :LANES].astype(jnp.bfloat16)
        first = index * step
        if first < kept_out.shape[0]:
            kept_out[first : first + step] = values
        else:
            first -= kept_out.shape[0]
            mixed_out[first : first + step] = values


def pack_kernel(split, lon_shift, kept, mixed, western, *outs):
    groups = len(outs)
    half = LANES // 2
    rest = HD - half
    fold = LANES // rest
    kept_count, mixed_count = kept.shape[0] // groups, mixed.shape[0] // groups
    count = kept_count + mixed_count
    part = round_up(-(-count // fold), SUBLANES)
    shape = (mixed_count // split, split, LANES)
    taken = lax.broadcasted_iota(jnp.int32, shape, 1) < column_offset(lon_shift)
    for group, out in enumerate(outs):
        rows = slice(group * mixed_count, (group + 1) * mixed_count)
        own, west = mixed[rows].astype(jnp.float32), western[rows].astype(jnp.float32)
        chosen = jnp.where(taken, west.reshape(shape), own.reshape(shape)).reshape(own.shape)
        rows = kept[group * kept_count : (group + 1) * kept_count].astype(jnp.float32)
        rows = jnp.concatenate([rows, chosen], axis=0)
        lane = lax.broadcasted_iota(jnp.int32, (count // 2, LANES), 1)
        main = jnp.where(lane < half, rows[: count // 2], pltpu.roll(rows[count // 2 :], half, axis=1))
        lane = lax.broadcasted_iota(jnp.int32, (part, LANES), 1)
        rests = jnp.zeros((part, LANES), jnp.float32)
        for index in range(fold):
            piece = rows[index * part : (index + 1) * part]
            if piece.shape[0] < part:
                empty = jnp.zeros((part - piece.shape[0], LANES), jnp.float32)
                piece = jnp.concatenate([piece, empty], axis=0)
            piece = pltpu.roll(piece, (index * rest + half) % LANES, axis=1)
            rests = jnp.where(lane // rest == index, piece, rests)
        out[...] = jnp.concatenate([main, rests], axis=0).astype(jnp.bfloat16)


def unpack(blocks, count):
    half = LANES // 2
    rest = HD - half
    fold = LANES // rest
    part = round_up(-(-count // fold), SUBLANES)
    columns = []
    for block in blocks:
        block = block[...].astype(jnp.float32)
        main, rests = block[: count // 2], block[count // 2 :]
        main = jnp.concatenate([main, pltpu.roll(main, half, axis=1)], axis=0)
        pieces = []
        for index in range(fold):
            turn = (half - index * rest) % LANES
            piece = pltpu.roll(rests, turn, axis=1) if turn else rests
            pieces.append(piece[: min(part, count - index * part)])
        lane = lax.broadcasted_iota(jnp.int32, main.shape, 1)
        columns.append(jnp.where(lane < half, main, jnp.concatenate(pieces, axis=0)))
    return jnp.concatenate(columns, axis=1).astype(jnp.bfloat16)


def by_column(projected, rows, columns, split):
    kept_count = rows * (columns - split)
    right = projected[:kept_count].reshape(rows, columns - split, -1)
    left = projected[kept_count:].reshape(rows, split, -1)
    return jnp.concatenate([left, right], axis=1)


def first_output_kernel(split, groups, field, weight, *refs):
    blocks, (out, second, first) = refs[:groups], refs[groups:]
    rows, columns, features = field.shape
    for slot in range(groups):
        group = lax.rem(lax.axis_index("tok") + slot, groups)
        for head, ordered in enumerate((first, second)):
            at = pl.multiple_of((group * HEADS // groups + head) * HD, 16)
            ordered[slot * LANES : slot * LANES + HD] = weight[pl.ds(at, HD)]
            ordered[slot * LANES + HD : (slot + 1) * LANES] = jnp.zeros(
                (LANES - HD, features), jnp.bfloat16
            )
    attended = unpack(blocks, rows * columns)
    projected = jnp.dot(attended, first[...], preferred_element_type=jnp.float32)
    out[...] = field[...].astype(jnp.float32) + by_column(projected, rows, columns, split)


def second_output_kernel(split, partial, weight, *refs):
    *blocks, out = refs
    rows, columns, _ = partial.shape
    attended = unpack(blocks, rows * columns)
    projected = jnp.dot(attended, weight[...], preferred_element_type=jnp.float32)
    out[...] = (partial[...] + by_column(projected, rows, columns, split)).astype(jnp.bfloat16)


def whole(count):
    return [pl.BlockSpec(memory_space=pltpu.VMEM)] * count


def shards(field_tokens, lon_shift, norm_gain, qkv_weight, out_weight):
    _, rows, columns, features = field_tokens.shape
    groups = lax.axis_size("tok")
    local = HEADS // groups
    width = local * HD
    span = round_up(3 * HD + 1, LANES)
    split = round_up(columns // 2, SUBLANES)
    field = field_tokens[0]
    smem = pl.BlockSpec(memory_space=pltpu.SMEM)
    params = pltpu.CompilerParams(vmem_limit_bytes=VMEM_BYTES)
    kept_count, mixed_count = rows * (columns - split), rows * split

    def projection(kernel, count, parts, scalars, operands):
        block = jax.ShapeDtypeStruct((count, local * span // parts), jnp.bfloat16)
        return pl.pallas_call(
            functools.partial(kernel, split),
            out_shape=[block] * (parts * groups),
            in_specs=[smem] * len(scalars) + whole(len(operands) + 2),
            out_specs=whole(parts * groups),
            scratch_shapes=[pltpu.VMEM((groups, count, local * span), jnp.bfloat16)],
            compiler_params=params,
            cost_estimate=pl.CostEstimate(
                flops=2 * count * features * 3 * HEADS * HD,
                bytes_accessed=2 * features * (3 * HEADS * HD + 2 * count),
                transcendentals=0,
            ),
        )(*scalars, *operands, norm_gain, qkv_weight)

    def spread(blocks, sign):
        return [blocks[0]] + [
            shifted(blocks[distance], "tok", sign * distance) for distance in range(1, groups)
        ]

    eastern = shifted(field[:, :split], "win", -LAT_WINDOWS)
    kept = spread(projection(kept_kernel, kept_count, 1, [], [field]), 1)
    mixed = projection(mixed_kernel, mixed_count, local, [lon_shift], [field, eastern])
    first_mixed = spread(after(mixed[:groups], kept), 1)
    second_mixed = spread(after(mixed[groups:], first_mixed), 1)

    total = groups * rows * columns
    step = total // 5
    packed_rows = round_up(rows * columns // 2 + -(-rows * columns * (HD - LANES // 2) // LANES), 16)

    def attention(head, blocks):
        return pl.pallas_call(
            functools.partial(attention_kernel, head, groups),
            out_shape=[
                jax.ShapeDtypeStruct((groups * count, LANES), jnp.bfloat16)
                for count in (kept_count, mixed_count)
            ],
            in_specs=whole(len(blocks)),
            out_specs=whole(2),
            scratch_shapes=[
                pltpu.VMEM((total, span), jnp.bfloat16),
                pltpu.VMEM((span, total), jnp.bfloat16),
                pltpu.VMEM((step, total), jnp.float32),
                pltpu.VMEM((step, total), jnp.float32),
                pltpu.VMEM((step, total), jnp.bfloat16),
                pltpu.VMEM((step, total), jnp.bfloat16),
            ],
            compiler_params=params,
            cost_estimate=pl.CostEstimate(
                flops=4 * total * total * span,
                bytes_accessed=2 * total * (span + LANES),
                transcendentals=total * total,
            ),
        )(*blocks)

    def back(kept_values, mixed_values):
        western = shifted(mixed_values, "win", LAT_WINDOWS)
        packed = pl.pallas_call(
            functools.partial(pack_kernel, split),
            out_shape=[jax.ShapeDtypeStruct((packed_rows, LANES), jnp.bfloat16)] * groups,
            in_specs=[smem] + whole(3),
            out_specs=whole(groups),
            compiler_params=params,
            cost_estimate=pl.CostEstimate(
                flops=total * LANES * 20, bytes_accessed=8 * total * LANES, transcendentals=0
            ),
        )(lon_shift, kept_values, mixed_values, western)
        return spread(packed, -1)

    first = back(*attention(0, [*kept, *first_mixed]))
    second = back(*attention(1, [*kept, *second_mixed]))

    cost = pl.CostEstimate(
        flops=2 * rows * columns * groups * LANES * features,
        bytes_accessed=features * (HEADS * HD + 6 * rows * columns),
        transcendentals=0,
    )
    ordered = (groups * LANES, features)
    partial, weight = pl.pallas_call(
        functools.partial(first_output_kernel, split, groups),
        out_shape=[
            jax.ShapeDtypeStruct(field.shape, jnp.float32),
            jax.ShapeDtypeStruct(ordered, jnp.bfloat16),
        ],
        in_specs=whole(2 + groups),
        out_specs=whole(2),
        scratch_shapes=[pltpu.VMEM(ordered, jnp.bfloat16)],
        compiler_params=params,
        cost_estimate=cost,
    )(field, out_weight, *first)
    result = pl.pallas_call(
        functools.partial(second_output_kernel, split),
        out_shape=jax.ShapeDtypeStruct(field.shape, jnp.bfloat16),
        in_specs=whole(2 + groups),
        out_specs=pl.BlockSpec(memory_space=pltpu.VMEM),
        compiler_params=params,
        cost_estimate=cost,
    )(partial, weight, *second)
    return result[None]


def solution(mesh):
    placed = (P("win", "tok", None, None), P(), P(), P(), P())
    return jax.shard_map(
        shards, mesh=mesh, in_specs=placed, out_specs=P("win", "tok", None, None), check_vma=False
    )
```

```python
import functools

import jax
import jax.numpy as jnp
from jax import lax
from jax.experimental import pallas as pl
from jax.experimental.pallas import tpu as pltpu
from jax.sharding import PartitionSpec as P

HEADS = 8
HD = 80
LAT_WINDOWS = 4
LANES = 128
SUBLANES = 8
VMEM_BYTES = 48 * 1024 * 1024


def round_up(value, unit):
    return -(-value // unit) * unit


def shifted(block, axis, distance):
    count = lax.axis_size(axis)
    return lax.ppermute(block, axis, [(i, (i + distance) % count) for i in range(count)])


def exchanged(blocks):
    return lax.all_to_all(blocks, "tok", split_axis=0, concat_axis=0, tiled=True)


def column_offset(lon_shift):
    return lon_shift[lax.rem(lax.axis_index("win"), LAT_WINDOWS)]


def project(tokens, gain, weight, outs):
    groups = outs[0].shape[0]
    local = HEADS // groups
    count, features = tokens.shape
    span = outs[0].shape[2] * len(outs) // local
    factor = lax.rsqrt(jnp.mean(tokens * tokens, axis=-1, keepdims=True) + 1e-06)
    normed = (tokens * factor * gain[...].reshape(1, features)).astype(jnp.bfloat16)
    qkv = jnp.dot(normed, weight[...], preferred_element_type=jnp.float32)
    tail = jnp.ones((count, span - 3 * HD), jnp.float32)
    for index in range(HEADS):
        group, head = index // local, index % local
        columns = [
            qkv[:, (kind * HEADS + index) * HD : (kind * HEADS + index + 1) * HD]
            for kind in range(3)
        ]
        block = jnp.concatenate(columns + [tail], axis=1).astype(jnp.bfloat16)
        if len(outs) == 1:
            outs[0][group, :, head * span : (head + 1) * span] = block
        else:
            outs[head][group] = block


def kept_kernel(split, field, gain, weight, *outs):
    rows, columns, features = field.shape
    tokens = field[...].astype(jnp.float32)[:, split:]
    project(tokens.reshape(rows * (columns - split), features), gain, weight, outs)


def mixed_kernel(split, lon_shift, field, eastern, gain, weight, *outs):
    rows, _, features = field.shape
    own = field[...].astype(jnp.float32)[:, :split]
    column = lax.broadcasted_iota(jnp.int32, own.shape, 1)
    tokens = jnp.where(column < column_offset(lon_shift), eastern[...].astype(jnp.float32), own)
    project(tokens.reshape(rows * split, features), gain, weight, outs)


def attention_kernel(head, kept, mixed, kept_out, mixed_out, held, keys, *refs):
    scores, weights = refs[:2], refs[2:]
    span = held.shape[1]
    start = 0
    for group in range(kept.shape[0]):
        held[start : start + kept.shape[1]] = kept[group, :, head * span : (head + 1) * span]
        start += kept.shape[1]
    for group in range(mixed.shape[0]):
        held[start : start + mixed.shape[1]] = mixed[group]
        start += mixed.shape[1]
    keys[...] = held[...].T
    factor = HD ** (-0.5) * 1.4426950408889634
    step = scores[0].shape[0]
    chunk = 16

    def score(index, out):
        queries = held[index * step : (index + 1) * step].astype(jnp.float32)
        queries = pltpu.roll(queries, HD, axis=1)
        lane = lax.broadcasted_iota(jnp.int32, queries.shape, 1)
        queries = jnp.where((lane >= HD) & (lane < 2 * HD), queries, 0.0).astype(jnp.bfloat16)
        out[...] = jnp.dot(queries, keys[...], preferred_element_type=jnp.float32)

    steps = start // step
    score(0, scores[0])
    for index in range(steps):
        if index + 1 < steps:
            score(index + 1, scores[(index + 1) % 2])
        now, out = scores[index % 2], weights[index % 2]
        for first in range(0, step, chunk):
            part = now[first : first + chunk]
            top = jnp.max(part, axis=-1, keepdims=True)
            out[first : first + chunk] = jnp.exp2((part - top) * factor).astype(jnp.bfloat16)
        mixed_values = jnp.dot(out[...], held[...], preferred_element_type=jnp.float32)
        scaled = mixed_values / mixed_values[:, 3 * HD : 3 * HD + 1]
        values = pltpu.roll(scaled, span - 2 * HD, axis=1)[:, :LANES].astype(jnp.bfloat16)
        first = index * step
        if first < kept_out.shape[0]:
            kept_out[first : first + step] = values
        else:
            first -= kept_out.shape[0]
            mixed_out[first : first + step] = values


def pack_kernel(split, lon_shift, kept, mixed, western, out):
    groups = out.shape[0]
    half = LANES // 2
    rest = HD - half
    fold = LANES // rest
    kept_count, mixed_count = kept.shape[0] // groups, mixed.shape[0] // groups
    count = kept_count + mixed_count
    part = round_up(-(-count // fold), SUBLANES)
    shape = (mixed_count // split, split, LANES)
    taken = lax.broadcasted_iota(jnp.int32, shape, 1) < column_offset(lon_shift)
    for group in range(groups):
        rows = slice(group * mixed_count, (group + 1) * mixed_count)
        own, west = mixed[rows].astype(jnp.float32), western[rows].astype(jnp.float32)
        chosen = jnp.where(taken, west.reshape(shape), own.reshape(shape)).reshape(own.shape)
        rows = kept[group * kept_count : (group + 1) * kept_count].astype(jnp.float32)
        rows = jnp.concatenate([rows, chosen], axis=0)
        lane = lax.broadcasted_iota(jnp.int32, (count // 2, LANES), 1)
        main = jnp.where(lane < half, rows[: count // 2], pltpu.roll(rows[count // 2 :], half, axis=1))
        lane = lax.broadcasted_iota(jnp.int32, (part, LANES), 1)
        rests = jnp.zeros((part, LANES), jnp.float32)
        for index in range(fold):
            piece = rows[index * part : (index + 1) * part]
            if piece.shape[0] < part:
                empty = jnp.zeros((part - piece.shape[0], LANES), jnp.float32)
                piece = jnp.concatenate([piece, empty], axis=0)
            piece = pltpu.roll(piece, (index * rest + half) % LANES, axis=1)
            rests = jnp.where(lane // rest == index, piece, rests)
        out[group] = jnp.concatenate([main, rests], axis=0).astype(jnp.bfloat16)


def unpack(blocks, count):
    half = LANES // 2
    rest = HD - half
    fold = LANES // rest
    part = round_up(-(-count // fold), SUBLANES)
    columns = []
    for group in range(blocks.shape[0]):
        block = blocks[group].astype(jnp.float32)
        main, rests = block[: count // 2], block[count // 2 :]
        main = jnp.concatenate([main, pltpu.roll(main, half, axis=1)], axis=0)
        pieces = []
        for index in range(fold):
            turn = (half - index * rest) % LANES
            piece = pltpu.roll(rests, turn, axis=1) if turn else rests
            pieces.append(piece[: min(part, count - index * part)])
        lane = lax.broadcasted_iota(jnp.int32, main.shape, 1)
        columns.append(jnp.where(lane < half, main, jnp.concatenate(pieces, axis=0)))
    return jnp.concatenate(columns, axis=1).astype(jnp.bfloat16)


def by_column(projected, rows, columns, split):
    kept_count = rows * (columns - split)
    right = projected[:kept_count].reshape(rows, columns - split, -1)
    left = projected[kept_count:].reshape(rows, split, -1)
    return jnp.concatenate([left, right], axis=1)


def first_output_kernel(split, groups, field, weight, blocks, out, second, first):
    rows, columns, features = field.shape
    for group in range(groups):
        for head, ordered in enumerate((first, second)):
            at = (group * HEADS // groups + head) * HD
            ordered[group * LANES : group * LANES + HD] = weight[at : at + HD]
            ordered[group * LANES + HD : (group + 1) * LANES] = jnp.zeros(
                (LANES - HD, features), jnp.bfloat16
            )
    attended = unpack(blocks, rows * columns)
    projected = jnp.dot(attended, first[...], preferred_element_type=jnp.float32)
    out[...] = field[...].astype(jnp.float32) + by_column(projected, rows, columns, split)


def second_output_kernel(split, partial, weight, blocks, out):
    rows, columns, _ = partial.shape
    attended = unpack(blocks, rows * columns)
    projected = jnp.dot(attended, weight[...], preferred_element_type=jnp.float32)
    out[...] = (partial[...] + by_column(projected, rows, columns, split)).astype(jnp.bfloat16)


def whole(count):
    return [pl.BlockSpec(memory_space=pltpu.VMEM)] * count


def shards(field_tokens, lon_shift, norm_gain, qkv_weight, out_weight):
    _, rows, columns, features = field_tokens.shape
    groups = lax.axis_size("tok")
    local = HEADS // groups
    width = local * HD
    span = round_up(3 * HD + 1, LANES)
    split = round_up(columns // 2, SUBLANES)
    field = field_tokens[0]
    smem = pl.BlockSpec(memory_space=pltpu.SMEM)
    params = pltpu.CompilerParams(vmem_limit_bytes=VMEM_BYTES)
    kept_count, mixed_count = rows * (columns - split), rows * split

    def projection(kernel, count, parts, scalars, operands):
        block = jax.ShapeDtypeStruct((groups, count, local * span // parts), jnp.bfloat16)
        return pl.pallas_call(
            functools.partial(kernel, split),
            out_shape=[block] * parts,
            in_specs=[smem] * len(scalars) + whole(len(operands) + 2),
            out_specs=whole(parts),
            compiler_params=params,
            cost_estimate=pl.CostEstimate(
                flops=2 * count * features * 3 * HEADS * HD,
                bytes_accessed=2 * features * (3 * HEADS * HD + 2 * count),
                transcendentals=0,
            ),
        )(*scalars, *operands, norm_gain, qkv_weight)

    eastern = shifted(field[:, :split], "win", -LAT_WINDOWS)
    kept = exchanged(projection(kept_kernel, kept_count, 1, [], [field])[0])
    mixed = projection(mixed_kernel, mixed_count, local, [lon_shift], [field, eastern])

    total = groups * rows * columns
    step = total // 5
    packed_rows = round_up(rows * columns // 2 + -(-rows * columns * (HD - LANES // 2) // LANES), 16)

    def attention(head, *blocks):
        return pl.pallas_call(
            functools.partial(attention_kernel, head),
            out_shape=[
                jax.ShapeDtypeStruct((groups * count, LANES), jnp.bfloat16)
                for count in (kept_count, mixed_count)
            ],
            in_specs=whole(len(blocks)),
            out_specs=whole(2),
            scratch_shapes=[
                pltpu.VMEM((total, span), jnp.bfloat16),
                pltpu.VMEM((span, total), jnp.bfloat16),
                pltpu.VMEM((step, total), jnp.float32),
                pltpu.VMEM((step, total), jnp.float32),
                pltpu.VMEM((step, total), jnp.bfloat16),
                pltpu.VMEM((step, total), jnp.bfloat16),
            ],
            compiler_params=params,
            cost_estimate=pl.CostEstimate(
                flops=4 * total * total * span,
                bytes_accessed=2 * total * (span + LANES),
                transcendentals=total * total,
            ),
        )(*blocks)

    def back(kept_values, mixed_values):
        western = shifted(mixed_values, "win", LAT_WINDOWS)
        packed = pl.pallas_call(
            functools.partial(pack_kernel, split),
            out_shape=jax.ShapeDtypeStruct((groups, packed_rows, LANES), jnp.bfloat16),
            in_specs=[smem] + whole(3),
            out_specs=pl.BlockSpec(memory_space=pltpu.VMEM),
            compiler_params=params,
            cost_estimate=pl.CostEstimate(
                flops=total * LANES * 20, bytes_accessed=8 * total * LANES, transcendentals=0
            ),
        )(lon_shift, kept_values, mixed_values, western)
        return exchanged(packed)

    first = back(*attention(0, kept, exchanged(mixed[0])))
    second = back(*attention(1, kept, exchanged(mixed[1])))

    cost = pl.CostEstimate(
        flops=2 * rows * columns * groups * LANES * features,
        bytes_accessed=features * (HEADS * HD + 6 * rows * columns),
        transcendentals=0,
    )
    ordered = (groups * LANES, features)
    partial, weight = pl.pallas_call(
        functools.partial(first_output_kernel, split, groups),
        out_shape=[
            jax.ShapeDtypeStruct(field.shape, jnp.float32),
            jax.ShapeDtypeStruct(ordered, jnp.bfloat16),
        ],
        in_specs=whole(3),
        out_specs=whole(2),
        scratch_shapes=[pltpu.VMEM(ordered, jnp.bfloat16)],
        compiler_params=params,
        cost_estimate=cost,
    )(field, out_weight, first)
    result = pl.pallas_call(
        functools.partial(second_output_kernel, split),
        out_shape=jax.ShapeDtypeStruct(field.shape, jnp.bfloat16),
        in_specs=whole(3),
        out_specs=pl.BlockSpec(memory_space=pltpu.VMEM),
        compiler_params=params,
        cost_estimate=cost,
    )(partial, weight, second)
    return result[None]


def solution(mesh):
    placed = (P("win", "tok", None, None), P(), P(), P(), P())
    return jax.shard_map(
        shards, mesh=mesh, in_specs=placed, out_specs=P("win", "tok", None, None), check_vma=False
    )
```

```python
import functools

import jax
import jax.numpy as jnp
from jax import lax
from jax.experimental import pallas as pl
from jax.experimental.pallas import tpu as pltpu
from jax.sharding import PartitionSpec as P

HEADS = 8
HD = 80
LAT_WINDOWS = 4
LANES = 128
SUBLANES = 8
MIB = 1024 * 1024
CHUNKS = 5


def round_up(value, unit):
    return -(-value // unit) * unit


def shifted(block, axis, distance):
    count = lax.axis_size(axis)
    return lax.ppermute(block, axis, [(i, (i + distance) % count) for i in range(count)])


def after(blocks, arrived):
    return [blocks[0]] + [
        lax.optimization_barrier(pair)[0] for pair in zip(blocks[1:], arrived[1:])
    ]


def column_offset(lon_shift):
    return lon_shift[lax.rem(lax.axis_index("win"), LAT_WINDOWS)]


def project(tokens, gain, weight, copies, qkv, slots, outs):
    groups = slots.shape[0]
    local = HEADS // groups
    count, features = tokens.shape
    span = slots.shape[2] // local
    factor = lax.rsqrt(jnp.mean(tokens * tokens, axis=-1, keepdims=True) + 1e-06)
    normed = (tokens * factor * gain[...].reshape(1, features)).astype(jnp.bfloat16)
    chunk = weight.shape[1] // CHUNKS
    for index in range(CHUNKS):
        copies[index].wait()
        columns = slice(index * chunk, (index + 1) * chunk)
        qkv[:, columns] = jnp.dot(normed, weight[:, columns], preferred_element_type=jnp.float32)
    tail = jnp.ones((count, span - 3 * HD), jnp.float32)
    place = lax.axis_index("tok")
    for group in range(groups):
        slot = lax.rem(group - place + groups, groups)
        columns = []
        for head in range(group * local, (group + 1) * local):
            columns += [
                qkv[:, (kind * HEADS + head) * HD : (kind * HEADS + head + 1) * HD]
                for kind in range(3)
            ] + [tail]
        slots[slot] = jnp.concatenate(columns, axis=1).astype(jnp.bfloat16)
    for index, out in enumerate(outs):
        first = index // groups * out.shape[1]
        out[...] = slots[index % groups, :, first : first + out.shape[1]]


def fetch(weight, held, sems):
    chunk = weight.shape[1] // CHUNKS
    copies = []
    for index in range(CHUNKS):
        columns = pl.ds(index * chunk, chunk)
        copies.append(
            pltpu.make_async_copy(weight.at[:, columns], held.at[:, columns], sems.at[index])
        )
        copies[-1].start()
    return copies


def kept_kernel(split, field, gain, weight, *refs):
    *outs, qkv, slots, held_weight, sems, held_field, held_gain = refs
    first = pltpu.make_async_copy(field, held_field, sems.at[CHUNKS])
    second = pltpu.make_async_copy(gain, held_gain, sems.at[CHUNKS + 1])
    first.start()
    second.start()
    copies = fetch(weight, held_weight, sems)
    first.wait()
    second.wait()
    rows, columns, features = field.shape
    tokens = held_field[...].astype(jnp.float32)[:, split:]
    tokens = tokens.reshape(rows * (columns - split), features)
    project(tokens, held_gain, held_weight, copies, qkv, slots, outs)


def mixed_kernel(split, field, gain, weight, lon_shift, eastern, *refs):
    *outs, qkv, slots, held_weight, sems = refs
    copies = fetch(weight, held_weight, sems)
    rows, _, features = field.shape
    own = field[...].astype(jnp.float32)[:, :split]
    column = lax.broadcasted_iota(jnp.int32, own.shape, 1)
    tokens = jnp.where(column < column_offset(lon_shift), eastern[...].astype(jnp.float32), own)
    project(tokens.reshape(rows * split, features), gain, held_weight, copies, qkv, slots, outs)


def gather(head, kept, mixed, held, keys):
    span = held.shape[1]
    start = 0
    for block in kept:
        held[start : start + block.shape[0]] = block[:, head * span : (head + 1) * span]
        start += block.shape[0]
    for block in mixed:
        held[start : start + block.shape[0]] = block[...]
        start += block.shape[0]
    keys[...] = held[...].T


def attend(held, keys, ranges, scores, weights):
    span = held.shape[1]
    factor = HD ** (-0.5) * 1.4426950408889634
    step = scores[0].shape[0]
    chunk = 16
    pieces = [
        (first + offset, out, offset)
        for first, count, out in ranges
        for offset in range(0, count, step)
    ]

    def score(index, out):
        first = pieces[index][0]
        queries = pltpu.roll(held[first : first + step].astype(jnp.float32), HD, axis=1)
        lane = lax.broadcasted_iota(jnp.int32, queries.shape, 1)
        queries = jnp.where((lane >= HD) & (lane < 2 * HD), queries, 0.0).astype(jnp.bfloat16)
        out[...] = jnp.dot(queries, keys[...], preferred_element_type=jnp.float32)

    score(0, scores[0])
    for index, (_, target, offset) in enumerate(pieces):
        if index + 1 < len(pieces):
            score(index + 1, scores[(index + 1) % 2])
        now, out = scores[index % 2], weights[index % 2]
        for first in range(0, step, chunk):
            part = now[first : first + chunk]
            top = jnp.max(part, axis=-1, keepdims=True)
            out[first : first + chunk] = jnp.exp2((part - top) * factor).astype(jnp.bfloat16)
        mixed_values = jnp.dot(out[...], held[...], preferred_element_type=jnp.float32)
        scaled = mixed_values / mixed_values[:, 3 * HD : 3 * HD + 1]
        values = pltpu.roll(scaled, span - 2 * HD, axis=1)[:, :LANES]
        target[offset : offset + step] = values.astype(jnp.bfloat16)


def first_head_kernel(groups, *refs):
    kept, mixed = refs[:groups], refs[groups : 2 * groups]
    kept_out, mixed_out, held, keys, *rest = refs[2 * groups :]
    gather(0, kept, mixed, held, keys)
    kept_count = kept_out.shape[0]
    ranges = [(0, kept_count, kept_out), (kept_count, mixed_out.shape[0], mixed_out)]
    attend(held, keys, ranges, rest[:2], rest[2:])


def second_mixed_kernel(groups, *refs):
    kept, mixed = refs[:groups], refs[groups : 2 * groups]
    mixed_out, held, keys, *rest = refs[2 * groups :]
    gather(1, kept, mixed, held, keys)
    count = mixed_out.shape[0]
    attend(held, keys, [(held.shape[0] - count, count, mixed_out)], rest[:2], rest[2:])


def second_kept_kernel(held, keys, kept_out, *rest):
    attend(held, keys, [(0, kept_out.shape[0], kept_out)], rest[:2], rest[2:])


def pack_kernel(split, lon_shift, kept, mixed, western, *outs):
    groups = len(outs)
    half = LANES // 2
    rest = HD - half
    fold = LANES // rest
    kept_count, mixed_count = kept.shape[0] // groups, mixed.shape[0] // groups
    count = kept_count + mixed_count
    part = round_up(-(-count // fold), SUBLANES)
    shape = (mixed_count // split, split, LANES)
    taken = lax.broadcasted_iota(jnp.int32, shape, 1) < column_offset(lon_shift)
    for group, out in enumerate(outs):
        rows = slice(group * mixed_count, (group + 1) * mixed_count)
        own, west = mixed[rows].astype(jnp.float32), western[rows].astype(jnp.float32)
        chosen = jnp.where(taken, west.reshape(shape), own.reshape(shape)).reshape(own.shape)
        rows = kept[group * kept_count : (group + 1) * kept_count].astype(jnp.float32)
        rows = jnp.concatenate([rows, chosen], axis=0)
        lane = lax.broadcasted_iota(jnp.int32, (count // 2, LANES), 1)
        main = jnp.where(lane < half, rows[: count // 2], pltpu.roll(rows[count // 2 :], half, axis=1))
        lane = lax.broadcasted_iota(jnp.int32, (part, LANES), 1)
        rests = jnp.zeros((part, LANES), jnp.float32)
        for index in range(fold):
            piece = rows[index * part : (index + 1) * part]
            if piece.shape[0] < part:
                empty = jnp.zeros((part - piece.shape[0], LANES), jnp.float32)
                piece = jnp.concatenate([piece, empty], axis=0)
            piece = pltpu.roll(piece, (index * rest + half) % LANES, axis=1)
            rests = jnp.where(lane // rest == index, piece, rests)
        out[...] = jnp.concatenate([main, rests], axis=0).astype(jnp.bfloat16)


def unpack(blocks, count):
    half = LANES // 2
    rest = HD - half
    fold = LANES // rest
    part = round_up(-(-count // fold), SUBLANES)
    columns = []
    for block in blocks:
        block = block[...].astype(jnp.float32)
        main, rests = block[: count // 2], block[count // 2 :]
        main = jnp.concatenate([main, pltpu.roll(main, half, axis=1)], axis=0)
        pieces = []
        for index in range(fold):
            turn = (half - index * rest) % LANES
            piece = pltpu.roll(rests, turn, axis=1) if turn else rests
            pieces.append(piece[: min(part, count - index * part)])
        lane = lax.broadcasted_iota(jnp.int32, main.shape, 1)
        columns.append(jnp.where(lane < half, main, jnp.concatenate(pieces, axis=0)))
    return jnp.concatenate(columns, axis=1).astype(jnp.bfloat16)


def by_column(projected, rows, columns, split):
    kept_count = rows * (columns - split)
    right = projected[:kept_count].reshape(rows, columns - split, -1)
    left = projected[kept_count:].reshape(rows, split, -1)
    return jnp.concatenate([left, right], axis=1)


def first_output_kernel(split, groups, field, weight, *refs):
    blocks, (out, second, first) = refs[:groups], refs[groups:]
    rows, columns, features = field.shape
    for slot in range(groups):
        group = lax.rem(lax.axis_index("tok") + slot, groups)
        for head, ordered in enumerate((first, second)):
            at = pl.multiple_of((group * HEADS // groups + head) * HD, 16)
            ordered[slot * LANES : slot * LANES + HD] = weight[pl.ds(at, HD)]
            ordered[slot * LANES + HD : (slot + 1) * LANES] = jnp.zeros(
                (LANES - HD, features), jnp.bfloat16
            )
    attended = unpack(blocks, rows * columns)
    projected = jnp.dot(attended, first[...], preferred_element_type=jnp.float32)
    out[...] = field[...].astype(jnp.float32) + by_column(projected, rows, columns, split)


def second_output_kernel(split, partial, weight, *refs):
    *blocks, out = refs
    rows, columns, _ = partial.shape
    attended = unpack(blocks, rows * columns)
    projected = jnp.dot(attended, weight[...], preferred_element_type=jnp.float32)
    out[...] = (partial[...] + by_column(projected, rows, columns, split)).astype(jnp.bfloat16)


def whole(count):
    return [pl.BlockSpec(memory_space=pltpu.VMEM)] * count


def shards(field_tokens, lon_shift, norm_gain, qkv_weight, out_weight):
    _, rows, columns, features = field_tokens.shape
    groups = lax.axis_size("tok")
    local = HEADS // groups
    width = local * HD
    span = round_up(3 * HD + 1, LANES)
    split = round_up(columns // 2, SUBLANES)
    field = field_tokens[0]
    smem = pl.BlockSpec(memory_space=pltpu.SMEM)
    kept_count, mixed_count = rows * (columns - split), rows * split

    def limit(size):
        return pltpu.CompilerParams(vmem_limit_bytes=size * MIB)

    def projection(kernel, count, parts, specs, held, params, *operands):
        block = jax.ShapeDtypeStruct((count, local * span // parts), jnp.bfloat16)
        return pl.pallas_call(
            functools.partial(kernel, split),
            out_shape=[block] * (parts * groups),
            in_specs=specs,
            out_specs=whole(parts * groups),
            scratch_shapes=[
                pltpu.VMEM((count, qkv_weight.shape[1]), jnp.float32),
                pltpu.VMEM((groups, count, local * span), jnp.bfloat16),
                *held,
            ],
            compiler_params=params,
            cost_estimate=pl.CostEstimate(
                flops=2 * count * features * 3 * HEADS * HD,
                bytes_accessed=2 * features * (3 * HEADS * HD + 2 * count),
                transcendentals=0,
            ),
        )(*operands)

    def spread(blocks, sign):
        return [blocks[0]] + [
            shifted(blocks[distance], "tok", sign * distance) for distance in range(1, groups)
        ]

    eastern = shifted(field[:, :split], "win", -LAT_WINDOWS)
    hbm = pl.BlockSpec(memory_space=pltpu.HBM)
    operands = (field, norm_gain, qkv_weight)
    held = [
        pltpu.VMEM(qkv_weight.shape, qkv_weight.dtype),
        pltpu.SemaphoreType.DMA((CHUNKS + 2,)),
        pltpu.VMEM(field.shape, field.dtype),
        pltpu.VMEM(norm_gain.shape, norm_gain.dtype),
    ]
    kept = spread(projection(kept_kernel, kept_count, 1, [hbm] * 3, held, limit(60), *operands), 1)
    specs = [*whole(2), hbm, smem, *whole(1)]
    operands += (lon_shift, eastern)
    mixed = projection(mixed_kernel, mixed_count, local, specs, held[:2], limit(52), *operands)
    first_mixed = spread(after(mixed[:groups], kept), 1)

    total = groups * rows * columns
    step = total // 5
    packed_rows = round_up(rows * columns // 2 + -(-rows * columns * (HD - LANES // 2) // LANES), 16)
    kept_values = jax.ShapeDtypeStruct((groups * kept_count, LANES), jnp.bfloat16)
    mixed_values = jax.ShapeDtypeStruct((groups * mixed_count, LANES), jnp.bfloat16)
    gathered = [
        jax.ShapeDtypeStruct((total, span), jnp.bfloat16),
        jax.ShapeDtypeStruct((span, total), jnp.bfloat16),
    ]

    def attention(kernel, count, out_shape, held, *operands):
        return pl.pallas_call(
            kernel,
            out_shape=out_shape,
            in_specs=whole(len(operands)),
            out_specs=whole(len(out_shape)),
            scratch_shapes=[pltpu.VMEM(leaf.shape, leaf.dtype) for leaf in held]
            + [pltpu.VMEM((step, total), jnp.float32)] * 2
            + [pltpu.VMEM((step, total), jnp.bfloat16)] * 2,
            compiler_params=limit(32),
            cost_estimate=pl.CostEstimate(
                flops=4 * count * total * span,
                bytes_accessed=2 * total * (span + LANES),
                transcendentals=count * total,
            ),
        )(*operands)

    def back(kept_values, mixed_values, western):
        packed = pl.pallas_call(
            functools.partial(pack_kernel, split),
            out_shape=[jax.ShapeDtypeStruct((packed_rows, LANES), jnp.bfloat16)] * groups,
            in_specs=[smem] + whole(3),
            out_specs=whole(groups),
            compiler_params=limit(16),
            cost_estimate=pl.CostEstimate(
                flops=total * LANES * 20, bytes_accessed=8 * total * LANES, transcendentals=0
            ),
        )(lon_shift, kept_values, mixed_values, western)
        return spread(packed, -1)

    first_kept_values, first_mixed_values = attention(
        functools.partial(first_head_kernel, groups),
        total,
        [kept_values, mixed_values],
        gathered,
        *kept,
        *first_mixed,
    )
    first_western = shifted(first_mixed_values, "win", LAT_WINDOWS)
    ready = first_mixed[:-1] + [first_mixed_values]
    second_mixed = spread(after(mixed[groups:], ready), 1)
    second_mixed_values, *second_gathered = attention(
        functools.partial(second_mixed_kernel, groups),
        groups * mixed_count,
        [mixed_values, *gathered],
        [],
        *kept,
        *second_mixed,
    )
    second_western = shifted(second_mixed_values, "win", LAT_WINDOWS)
    (second_kept_values,) = attention(
        second_kept_kernel, groups * kept_count, [kept_values], [], *second_gathered
    )
    first = back(first_kept_values, first_mixed_values, first_western)
    second = back(second_kept_values, second_mixed_values, second_western)

    cost = pl.CostEstimate(
        flops=2 * rows * columns * groups * LANES * features,
        bytes_accessed=features * (HEADS * HD + 6 * rows * columns),
        transcendentals=0,
    )
    ordered = (groups * LANES, features)
    partial, weight = pl.pallas_call(
        functools.partial(first_output_kernel, split, groups),
        out_shape=[
            jax.ShapeDtypeStruct(field.shape, jnp.float32),
            jax.ShapeDtypeStruct(ordered, jnp.bfloat16),
        ],
        in_specs=whole(2 + groups),
        out_specs=whole(2),
        scratch_shapes=[pltpu.VMEM(ordered, jnp.bfloat16)],
        compiler_params=limit(24),
        cost_estimate=cost,
    )(field, out_weight, *first)
    result = pl.pallas_call(
        functools.partial(second_output_kernel, split),
        out_shape=jax.ShapeDtypeStruct(field.shape, jnp.bfloat16),
        in_specs=whole(2 + groups),
        out_specs=pl.BlockSpec(memory_space=pltpu.VMEM),
        compiler_params=limit(24),
        cost_estimate=cost,
    )(partial, weight, *second)
    return result[None]


def solution(mesh):
    placed = (P("win", "tok", None, None), P(), P(), P(), P())
    return jax.shard_map(
        shards, mesh=mesh, in_specs=placed, out_specs=P("win", "tok", None, None), check_vma=False
    )
```

```python
import functools

import jax
import jax.numpy as jnp
from jax import lax
from jax.experimental import pallas as pl
from jax.experimental.pallas import tpu as pltpu
from jax.sharding import PartitionSpec as P

HEADS = 8
HD = 80
LAT_WINDOWS = 4
LANES = 128
SUBLANES = 8
MIB = 1024 * 1024
CHUNKS = 5


def round_up(value, unit):
    return -(-value // unit) * unit


def shifted(block, axis, distance):
    count = lax.axis_size(axis)
    return lax.ppermute(block, axis, [(i, (i + distance) % count) for i in range(count)])


def after(blocks, arrived):
    return [
        block if other is None else lax.optimization_barrier((block, other))[0]
        for block, other in zip(blocks, arrived)
    ]


def column_offset(lon_shift):
    return lon_shift[lax.rem(lax.axis_index("win"), LAT_WINDOWS)]


def project(tokens, gain, weight, copies, qkv, slots, outs):
    groups = slots.shape[0]
    local = HEADS // groups
    count, features = tokens.shape
    span = slots.shape[2] // local
    factor = lax.rsqrt(jnp.mean(tokens * tokens, axis=-1, keepdims=True) + 1e-06)
    normed = (tokens * factor * gain[...].reshape(1, features)).astype(jnp.bfloat16)
    chunk = features // CHUNKS
    for index in range(CHUNKS):
        copies[index].wait()
        inner = slice(index * chunk, (index + 1) * chunk)
        share = jnp.dot(normed[:, inner], weight[inner], preferred_element_type=jnp.float32)
        qkv[...] = qkv[...] + share if index else share
    tail = jnp.ones((count, span - 3 * HD), jnp.float32)
    place = lax.axis_index("tok")
    for group in range(groups):
        slot = lax.rem(group - place + groups, groups)
        columns = []
        for head in range(group * local, (group + 1) * local):
            columns += [
                qkv[:, (kind * HEADS + head) * HD : (kind * HEADS + head + 1) * HD]
                for kind in range(3)
            ] + [tail]
        slots[slot] = jnp.concatenate(columns, axis=1).astype(jnp.bfloat16)
    for index, out in enumerate(outs):
        first = index // groups * out.shape[1]
        out[...] = slots[index % groups, :, first : first + out.shape[1]]


def fetch(weight, held, sems):
    chunk = weight.shape[0] // CHUNKS
    copies = []
    for index in range(CHUNKS):
        inner = pl.ds(index * chunk, chunk)
        copies.append(pltpu.make_async_copy(weight.at[inner], held.at[inner], sems.at[index]))
        copies[-1].start()
    return copies


def kept_kernel(split, field, gain, weight, *refs):
    *outs, qkv, slots, held_weight, sems, held_field, held_gain = refs
    first = pltpu.make_async_copy(field, held_field, sems.at[CHUNKS])
    second = pltpu.make_async_copy(gain, held_gain, sems.at[CHUNKS + 1])
    first.start()
    second.start()
    copies = fetch(weight, held_weight, sems)
    first.wait()
    second.wait()
    rows, columns, features = field.shape
    tokens = held_field[...].astype(jnp.float32)[:, split:]
    tokens = tokens.reshape(rows * (columns - split), features)
    project(tokens, held_gain, held_weight, copies, qkv, slots, outs)


def leaving_kernel(field, out):
    rows, columns, _ = field.shape
    tokens = field[...].astype(jnp.float32)
    pieces = [tokens[row, : columns // 2] for row in range(rows)]
    out[...] = jnp.concatenate(pieces, axis=0).astype(jnp.bfloat16)


def mixed_kernel(split, field, gain, weight, lon_shift, eastern, *refs):
    *outs, qkv, slots, held_weight, sems = refs
    copies = fetch(weight, held_weight, sems)
    rows, columns, features = field.shape
    count = columns // 2
    own = field[...].astype(jnp.float32)[:, :split]
    arrived = eastern[...].astype(jnp.float32)
    filler = jnp.zeros((split - count, features), jnp.float32)
    pieces = []
    for row in range(rows):
        pieces += [arrived[row * count : (row + 1) * count], filler]
    arrived = jnp.concatenate(pieces, axis=0).reshape(own.shape)
    column = lax.broadcasted_iota(jnp.int32, own.shape, 1)
    tokens = jnp.where(column < column_offset(lon_shift), arrived, own)
    project(tokens.reshape(rows * split, features), gain, held_weight, copies, qkv, slots, outs)


def gather(head, kept, mixed, held, keys):
    span = held.shape[1]
    start = 0
    for block in kept:
        held[start : start + block.shape[0]] = block[:, head * span : (head + 1) * span]
        start += block.shape[0]
    for block in mixed:
        held[start : start + block.shape[0]] = block[...]
        start += block.shape[0]
    keys[...] = held[...].T


def attend(held, keys, ranges, scores, weights):
    span = held.shape[1]
    factor = HD ** (-0.5) * 1.4426950408889634
    step = scores[0].shape[0]
    chunk = 16
    pieces = [
        (first + offset, out, offset)
        for first, count, out in ranges
        for offset in range(0, count, step)
    ]

    def score(index, out):
        first = pieces[index][0]
        queries = pltpu.roll(held[first : first + step].astype(jnp.float32), HD, axis=1)
        lane = lax.broadcasted_iota(jnp.int32, queries.shape, 1)
        queries = jnp.where((lane >= HD) & (lane < 2 * HD), queries, 0.0).astype(jnp.bfloat16)
        out[...] = jnp.dot(queries, keys[...], preferred_element_type=jnp.float32)

    score(0, scores[0])
    for index, (_, target, offset) in enumerate(pieces):
        if index + 1 < len(pieces):
            score(index + 1, scores[(index + 1) % 2])
        now, out = scores[index % 2], weights[index % 2]
        for first in range(0, step, chunk):
            part = now[first : first + chunk]
            top = jnp.max(part, axis=-1, keepdims=True)
            out[first : first + chunk] = jnp.exp2((part - top) * factor).astype(jnp.bfloat16)
        mixed_values = jnp.dot(out[...], held[...], preferred_element_type=jnp.float32)
        scaled = mixed_values / mixed_values[:, 3 * HD : 3 * HD + 1]
        values = pltpu.roll(scaled, span - 2 * HD, axis=1)[:, :LANES]
        target[offset : offset + step] = values.astype(jnp.bfloat16)


def first_head_kernel(groups, *refs):
    kept, mixed = refs[:groups], refs[groups : 2 * groups]
    kept_out, mixed_out, held, keys, *rest = refs[2 * groups :]
    gather(0, kept, mixed, held, keys)
    kept_count = kept_out.shape[0]
    ranges = [(0, kept_count, kept_out), (kept_count, mixed_out.shape[0], mixed_out)]
    attend(held, keys, ranges, rest[:2], rest[2:])


def second_mixed_kernel(groups, *refs):
    kept, mixed = refs[:groups], refs[groups : 2 * groups]
    mixed_out, held, keys, *rest = refs[2 * groups :]
    gather(1, kept, mixed, held, keys)
    count = mixed_out.shape[0]
    attend(held, keys, [(held.shape[0] - count, count, mixed_out)], rest[:2], rest[2:])


def second_kept_kernel(held, keys, kept_out, *rest):
    attend(held, keys, [(0, kept_out.shape[0], kept_out)], rest[:2], rest[2:])


def pack_kernel(split, lon_shift, kept, mixed, western, *outs):
    groups = len(outs)
    half = LANES // 2
    rest = HD - half
    fold = LANES // rest
    kept_count, mixed_count = kept.shape[0] // groups, mixed.shape[0] // groups
    count = kept_count + mixed_count
    part = round_up(-(-count // fold), SUBLANES)
    shape = (mixed_count // split, split, LANES)
    taken = lax.broadcasted_iota(jnp.int32, shape, 1) < column_offset(lon_shift)
    for group, out in enumerate(outs):
        rows = slice(group * mixed_count, (group + 1) * mixed_count)
        own, west = mixed[rows].astype(jnp.float32), western[rows].astype(jnp.float32)
        chosen = jnp.where(taken, west.reshape(shape), own.reshape(shape)).reshape(own.shape)
        rows = kept[group * kept_count : (group + 1) * kept_count].astype(jnp.float32)
        rows = jnp.concatenate([rows, chosen], axis=0)
        lane = lax.broadcasted_iota(jnp.int32, (count // 2, LANES), 1)
        main = jnp.where(lane < half, rows[: count // 2], pltpu.roll(rows[count // 2 :], half, axis=1))
        lane = lax.broadcasted_iota(jnp.int32, (part, LANES), 1)
        rests = jnp.zeros((part, LANES), jnp.float32)
        for index in range(fold):
            piece = rows[index * part : (index + 1) * part]
            if piece.shape[0] < part:
                empty = jnp.zeros((part - piece.shape[0], LANES), jnp.float32)
                piece = jnp.concatenate([piece, empty], axis=0)
            piece = pltpu.roll(piece, (index * rest + half) % LANES, axis=1)
            rests = jnp.where(lane // rest == index, piece, rests)
        out[...] = jnp.concatenate([main, rests], axis=0).astype(jnp.bfloat16)


def unpack(blocks, count):
    half = LANES // 2
    rest = HD - half
    fold = LANES // rest
    part = round_up(-(-count // fold), SUBLANES)
    columns = []
    for block in blocks:
        block = block[...].astype(jnp.float32)
        main, rests = block[: count // 2], block[count // 2 :]
        main = jnp.concatenate([main, pltpu.roll(main, half, axis=1)], axis=0)
        pieces = []
        for index in range(fold):
            turn = (half - index * rest) % LANES
            piece = pltpu.roll(rests, turn, axis=1) if turn else rests
            pieces.append(piece[: min(part, count - index * part)])
        lane = lax.broadcasted_iota(jnp.int32, main.shape, 1)
        columns.append(jnp.where(lane < half, main, jnp.concatenate(pieces, axis=0)))
    return jnp.concatenate(columns, axis=1).astype(jnp.bfloat16)


def by_column(projected, rows, columns, split):
    kept_count = rows * (columns - split)
    right = projected[:kept_count].reshape(rows, columns - split, -1)
    left = projected[kept_count:].reshape(rows, split, -1)
    return jnp.concatenate([left, right], axis=1)


def first_output_kernel(split, groups, field, weight, *refs):
    blocks, (out, second, first) = refs[:groups], refs[groups:]
    rows, columns, features = field.shape
    for slot in range(groups):
        group = lax.rem(lax.axis_index("tok") + slot, groups)
        for head, ordered in enumerate((first, second)):
            at = pl.multiple_of((group * HEADS // groups + head) * HD, 16)
            ordered[slot * LANES : slot * LANES + HD] = weight[pl.ds(at, HD)]
            ordered[slot * LANES + HD : (slot + 1) * LANES] = jnp.zeros(
                (LANES - HD, features), jnp.bfloat16
            )
    attended = unpack(blocks, rows * columns)
    projected = jnp.dot(attended, first[...], preferred_element_type=jnp.float32)
    out[...] = field[...].astype(jnp.float32) + by_column(projected, rows, columns, split)


def second_output_kernel(split, partial, weight, *refs):
    *blocks, out = refs
    rows, columns, _ = partial.shape
    attended = unpack(blocks, rows * columns)
    projected = jnp.dot(attended, weight[...], preferred_element_type=jnp.float32)
    out[...] = (partial[...] + by_column(projected, rows, columns, split)).astype(jnp.bfloat16)


def whole(count):
    return [pl.BlockSpec(memory_space=pltpu.VMEM)] * count


def shards(field_tokens, lon_shift, norm_gain, qkv_weight, out_weight):
    _, rows, columns, features = field_tokens.shape
    groups = lax.axis_size("tok")
    local = HEADS // groups
    width = local * HD
    span = round_up(3 * HD + 1, LANES)
    split = round_up(columns // 2, SUBLANES)
    field = field_tokens[0]
    smem = pl.BlockSpec(memory_space=pltpu.SMEM)
    kept_count, mixed_count = rows * (columns - split), rows * split

    def limit(size):
        return pltpu.CompilerParams(vmem_limit_bytes=size * MIB)

    def projection(kernel, count, parts, specs, held, params, *operands):
        block = jax.ShapeDtypeStruct((count, local * span // parts), jnp.bfloat16)
        return pl.pallas_call(
            functools.partial(kernel, split),
            out_shape=[block] * (parts * groups),
            in_specs=specs,
            out_specs=whole(parts * groups),
            scratch_shapes=[
                pltpu.VMEM((count, qkv_weight.shape[1]), jnp.float32),
                pltpu.VMEM((groups, count, local * span), jnp.bfloat16),
                *held,
            ],
            compiler_params=params,
            cost_estimate=pl.CostEstimate(
                flops=2 * count * features * 3 * HEADS * HD,
                bytes_accessed=2 * features * (3 * HEADS * HD + 2 * count),
                transcendentals=0,
            ),
        )(*operands)

    def spread(blocks, sign):
        return [blocks[0]] + [
            shifted(blocks[distance], "tok", sign * distance) for distance in range(1, groups)
        ]

    leaving = pl.pallas_call(
        leaving_kernel,
        out_shape=jax.ShapeDtypeStruct((rows * (columns // 2), features), jnp.bfloat16),
        in_specs=whole(1),
        out_specs=pl.BlockSpec(memory_space=pltpu.VMEM),
        compiler_params=limit(62),
        cost_estimate=pl.CostEstimate(
            flops=0, bytes_accessed=3 * rows * columns * features, transcendentals=0
        ),
    )(field)
    eastern = shifted(leaving, "win", -LAT_WINDOWS)
    hbm = pl.BlockSpec(memory_space=pltpu.HBM)
    operands = (field, norm_gain, qkv_weight)
    held = [
        pltpu.VMEM(qkv_weight.shape, qkv_weight.dtype),
        pltpu.SemaphoreType.DMA((CHUNKS + 2,)),
        pltpu.VMEM(field.shape, field.dtype),
        pltpu.VMEM(norm_gain.shape, norm_gain.dtype),
    ]
    kept = spread(projection(kept_kernel, kept_count, 1, [hbm] * 3, held, limit(60), *operands), 1)
    specs = [*whole(2), hbm, smem, *whole(1)]
    operands += (lon_shift, eastern)
    mixed = projection(mixed_kernel, mixed_count, local, specs, held[:2], limit(52), *operands)
    ahead = [None] * (groups - 1)
    first_mixed = spread(after(mixed[:groups], [*ahead, kept[1]]), 1)

    total = groups * rows * columns
    step = total // 5
    packed_rows = round_up(rows * columns // 2 + -(-rows * columns * (HD - LANES // 2) // LANES), 16)
    kept_values = jax.ShapeDtypeStruct((groups * kept_count, LANES), jnp.bfloat16)
    mixed_values = jax.ShapeDtypeStruct((groups * mixed_count, LANES), jnp.bfloat16)
    gathered = [
        jax.ShapeDtypeStruct((total, span), jnp.bfloat16),
        jax.ShapeDtypeStruct((span, total), jnp.bfloat16),
    ]

    def attention(kernel, count, out_shape, held, *operands):
        return pl.pallas_call(
            kernel,
            out_shape=out_shape,
            in_specs=whole(len(operands)),
            out_specs=whole(len(out_shape)),
            scratch_shapes=[pltpu.VMEM(leaf.shape, leaf.dtype) for leaf in held]
            + [pltpu.VMEM((step, total), jnp.float32)] * 2
            + [pltpu.VMEM((step, total), jnp.bfloat16)] * 2,
            compiler_params=limit(32),
            cost_estimate=pl.CostEstimate(
                flops=4 * count * total * span,
                bytes_accessed=2 * total * (span + LANES),
                transcendentals=count * total,
            ),
        )(*operands)

    def back(kept_values, mixed_values, western):
        packed = pl.pallas_call(
            functools.partial(pack_kernel, split),
            out_shape=[jax.ShapeDtypeStruct((packed_rows, LANES), jnp.bfloat16)] * groups,
            in_specs=[smem] + whole(3),
            out_specs=whole(groups),
            compiler_params=limit(16),
            cost_estimate=pl.CostEstimate(
                flops=total * LANES * 20, bytes_accessed=8 * total * LANES, transcendentals=0
            ),
        )(lon_shift, kept_values, mixed_values, western)
        return spread(packed, -1)

    first_kept_values, first_mixed_values = attention(
        functools.partial(first_head_kernel, groups),
        total,
        [kept_values, mixed_values],
        gathered,
        *kept,
        *first_mixed,
    )
    first_western = shifted(first_mixed_values, "win", LAT_WINDOWS)
    second_mixed = spread(after(mixed[groups:], [None, *kept[2:], first_mixed[1]]), 1)
    second_mixed_values, *second_gathered = attention(
        functools.partial(second_mixed_kernel, groups),
        groups * mixed_count,
        [mixed_values, *gathered],
        [],
        *kept,
        *second_mixed,
    )
    second_western = shifted(second_mixed_values, "win", LAT_WINDOWS)
    (second_kept_values,) = attention(
        second_kept_kernel, groups * kept_count, [kept_values], [], *second_gathered
    )
    first = back(first_kept_values, first_mixed_values, first_western)
    second = back(second_kept_values, second_mixed_values, second_western)

    cost = pl.CostEstimate(
        flops=2 * rows * columns * groups * LANES * features,
        bytes_accessed=features * (HEADS * HD + 6 * rows * columns),
        transcendentals=0,
    )
    ordered = (groups * LANES, features)
    partial, weight = pl.pallas_call(
        functools.partial(first_output_kernel, split, groups),
        out_shape=[
            jax.ShapeDtypeStruct(field.shape, jnp.float32),
            jax.ShapeDtypeStruct(ordered, jnp.bfloat16),
        ],
        in_specs=whole(2 + groups),
        out_specs=whole(2),
        scratch_shapes=[pltpu.VMEM(ordered, jnp.bfloat16)],
        compiler_params=limit(24),
        cost_estimate=cost,
    )(field, out_weight, *first)
    result = pl.pallas_call(
        functools.partial(second_output_kernel, split),
        out_shape=jax.ShapeDtypeStruct(field.shape, jnp.bfloat16),
        in_specs=whole(2 + groups),
        out_specs=pl.BlockSpec(memory_space=pltpu.VMEM),
        compiler_params=limit(24),
        cost_estimate=cost,
    )(partial, weight, *second)
    return result[None]


def solution(mesh):
    placed = (P("win", "tok", None, None), P(), P(), P(), P())
    return jax.shard_map(
        shards, mesh=mesh, in_specs=placed, out_specs=P("win", "tok", None, None), check_vma=False
    )
```

```python
import functools

import jax
import jax.numpy as jnp
from jax import lax
from jax.experimental import pallas as pl
from jax.experimental.pallas import tpu as pltpu
from jax.sharding import PartitionSpec as P

HEADS = 8
HD = 80
LAT_WINDOWS = 4
LANES = 128
SUBLANES = 8
MIB = 1024 * 1024


def round_up(value, unit):
    return -(-value // unit) * unit


def shifted(block, axis, distance):
    count = lax.axis_size(axis)
    return lax.ppermute(block, axis, [(i, (i + distance) % count) for i in range(count)])


def after(blocks, arrived):
    return [
        block if other is None else lax.optimization_barrier((block, other))[0]
        for block, other in zip(blocks, arrived)
    ]


def column_offset(lon_shift):
    return lon_shift[lax.rem(lax.axis_index("win"), LAT_WINDOWS)]


def project(tokens, gain, weight, copy, slots, outs):
    groups = slots.shape[0]
    local = HEADS // groups
    count, features = tokens.shape
    span = slots.shape[2] // local
    factor = lax.rsqrt(jnp.mean(tokens * tokens, axis=-1, keepdims=True) + 1e-06)
    normed = (tokens * factor * gain[...].reshape(1, features)).astype(jnp.bfloat16)
    copy.wait()
    qkv = jnp.dot(normed, weight[...], preferred_element_type=jnp.float32).astype(jnp.bfloat16)
    tail = jnp.ones((count, span - 3 * HD), jnp.bfloat16)
    place = lax.axis_index("tok")
    for group in range(groups):
        slot = lax.rem(group - place + groups, groups)
        columns = []
        for head in range(group * local, (group + 1) * local):
            columns += [
                qkv[:, (kind * HEADS + head) * HD : (kind * HEADS + head + 1) * HD]
                for kind in range(3)
            ] + [tail]
        slots[slot] = jnp.concatenate(columns, axis=1)
    for index, out in enumerate(outs):
        first = index // groups * out.shape[1]
        out[...] = slots[index % groups, :, first : first + out.shape[1]]


def kept_kernel(split, field, gain, weight, *refs):
    *outs, slots, held_weight, sems, held_field, held_gain = refs
    copy = pltpu.make_async_copy(weight, held_weight, sems.at[0])
    first = pltpu.make_async_copy(field, held_field, sems.at[1])
    second = pltpu.make_async_copy(gain, held_gain, sems.at[2])
    first.start()
    second.start()
    copy.start()
    first.wait()
    second.wait()
    rows, columns, features = field.shape
    tokens = held_field[...].astype(jnp.float32)[:, split:]
    tokens = tokens.reshape(rows * (columns - split), features)
    project(tokens, held_gain, held_weight, copy, slots, outs)


def mixed_kernel(split, field, gain, weight, lon_shift, eastern, *refs):
    *outs, slots, held_weight, sems = refs
    copy = pltpu.make_async_copy(weight, held_weight, sems.at[0])
    copy.start()
    rows, _, features = field.shape
    own = field[...].astype(jnp.float32)[:, :split]
    column = lax.broadcasted_iota(jnp.int32, own.shape, 1)
    tokens = jnp.where(column < column_offset(lon_shift), eastern[...].astype(jnp.float32), own)
    project(tokens.reshape(rows * split, features), gain, held_weight, copy, slots, outs)


def gather(head, kept, mixed, held, keys):
    span = held.shape[1]
    start = 0
    for block in kept:
        held[start : start + block.shape[0]] = block[:, head * span : (head + 1) * span]
        start += block.shape[0]
    for block in mixed:
        held[start : start + block.shape[0]] = block[...]
        start += block.shape[0]
    keys[...] = held[...].T


def attend(held, keys, attended, scores, weights):
    span = held.shape[1]
    factor = HD ** (-0.5) * 1.4426950408889634
    step = scores[0].shape[0]
    chunk = 16
    steps = held.shape[0] // step

    def score(index, out):
        first = index * step
        queries = pltpu.roll(held[first : first + step].astype(jnp.float32), HD, axis=1)
        lane = lax.broadcasted_iota(jnp.int32, queries.shape, 1)
        queries = jnp.where((lane >= HD) & (lane < 2 * HD), queries, 0.0).astype(jnp.bfloat16)
        out[...] = jnp.dot(queries, keys[...], preferred_element_type=jnp.float32)

    score(0, scores[0])
    for index in range(steps):
        if index + 1 < steps:
            score(index + 1, scores[(index + 1) % 2])
        now, out = scores[index % 2], weights[index % 2]
        for first in range(0, step, chunk):
            part = now[first : first + chunk]
            top = jnp.max(part, axis=-1, keepdims=True)
            out[first : first + chunk] = jnp.exp2((part - top) * factor).astype(jnp.bfloat16)
        mixed_values = jnp.dot(out[...], held[...], preferred_element_type=jnp.float32)
        scaled = mixed_values / mixed_values[:, 3 * HD : 3 * HD + 1]
        values = pltpu.roll(scaled, span - 2 * HD, axis=1)[:, :LANES]
        attended[index * step : (index + 1) * step] = values


def packed_rows(count):
    part = round_up(-(-count * (HD - LANES // 2) // LANES), SUBLANES)
    return count // 2 + part, part


def pack(rows):
    count = rows.shape[0]
    half = LANES // 2
    rest = HD - half
    part = packed_rows(count)[1]
    lane = lax.broadcasted_iota(jnp.int32, (count // 2, LANES), 1)
    main = jnp.where(lane < half, rows[: count // 2], pltpu.roll(rows[count // 2 :], half, axis=1))
    lane = lax.broadcasted_iota(jnp.int32, (part, LANES), 1)
    rests = jnp.zeros((part, LANES), jnp.float32)
    for index in range(-(-count // part)):
        piece = rows[index * part : (index + 1) * part]
        if piece.shape[0] < part:
            empty = jnp.zeros((part - piece.shape[0], LANES), jnp.float32)
            piece = jnp.concatenate([piece, empty], axis=0)
        turn = (index * rest + half) % LANES
        piece = pltpu.roll(piece, turn, axis=1) if turn else piece
        rests = jnp.where(lane // rest == index, piece, rests)
    return jnp.concatenate([main, rests], axis=0)


def unpack(block, count):
    half = LANES // 2
    rest = HD - half
    part = packed_rows(count)[1]
    main, rests = block[: count // 2], block[count // 2 : count // 2 + part]
    main = jnp.concatenate([main, pltpu.roll(main, half, axis=1)], axis=0)
    pieces = []
    for index in range(-(-count // part)):
        turn = (half - index * rest) % LANES
        piece = pltpu.roll(rests, turn, axis=1) if turn else rests
        pieces.append(piece[: min(part, count - index * part)])
    lane = lax.broadcasted_iota(jnp.int32, main.shape, 1)
    return jnp.where(lane < half, main, jnp.concatenate(pieces, axis=0))


def packed_tokens(count):
    half = LANES // 2
    total, part = packed_rows(count)
    row = lax.broadcasted_iota(jnp.int32, (total, LANES), 0)
    lane = lax.broadcasted_iota(jnp.int32, (total, LANES), 1)
    main = row + jnp.where(lane < half, 0, count // 2)
    rests = row - count // 2 + lane // (HD - half) * part
    return jnp.where(row < count // 2, main, rests)


def attention_kernel(head, groups, *refs):
    kept, mixed = refs[:groups], refs[groups : 2 * groups]
    outs, (held, keys, attended, *rest) = refs[2 * groups : -7], refs[-7:]
    gather(head, kept, mixed, held, keys)
    attend(held, keys, attended, rest[:2], rest[2:])
    kept_count, mixed_count = kept[0].shape[0], mixed[0].shape[0]
    for group in range(groups):
        first = groups * kept_count + group * mixed_count
        left = pack(attended[first : first + mixed_count])
        right = pack(attended[group * kept_count : (group + 1) * kept_count])
        outs[group][...] = jnp.concatenate([left, right], axis=0).astype(jnp.bfloat16)
        if len(outs) > groups:
            outs[groups + group][...] = left.astype(jnp.bfloat16)


def mixed_rows_kernel(*refs):
    *blocks, out = refs
    rows = out.shape[0] // len(blocks)
    pieces = [block[...].astype(jnp.float32)[:rows] for block in blocks]
    out[...] = jnp.concatenate(pieces, axis=0).astype(jnp.bfloat16)


def projected_rows(split, lon_shift, shape, blocks, western, weight):
    rows, columns, _ = shape
    kept_count, mixed_count = rows * (columns - split), rows * split
    total = packed_rows(mixed_count)[0]
    taken = lax.rem(packed_tokens(mixed_count), split) < column_offset(lon_shift)
    attended = []
    for block, west in zip(blocks, western):
        block = block[...].astype(jnp.float32)
        left = unpack(jnp.where(taken, west, block[:total]), mixed_count)
        right = unpack(block[total:], kept_count)
        attended.append(jnp.concatenate([right, left], axis=0))
    attended = jnp.concatenate(attended, axis=1).astype(jnp.bfloat16)
    projected = jnp.dot(attended, weight[...], preferred_element_type=jnp.float32)
    return by_column(projected, rows, columns, split)


def by_column(projected, rows, columns, split):
    kept_count = rows * (columns - split)
    right = projected[:kept_count].reshape(rows, columns - split, -1)
    left = projected[kept_count:].reshape(rows, split, -1)
    return jnp.concatenate([left, right], axis=1)


def first_output_kernel(split, groups, lon_shift, field, weight, *refs):
    *blocks, western, out, second, first = refs
    features = field.shape[2]
    for slot in range(groups):
        group = lax.rem(lax.axis_index("tok") + slot, groups)
        for head, ordered in enumerate((first, second)):
            at = pl.multiple_of((group * HEADS // groups + head) * HD, 16)
            ordered[slot * LANES : slot * LANES + HD] = weight[pl.ds(at, HD)]
            ordered[slot * LANES + HD : (slot + 1) * LANES] = jnp.zeros(
                (LANES - HD, features), jnp.bfloat16
            )
    west = western[...].astype(jnp.float32)
    total = west.shape[0] // groups
    west = [west[slot * total : (slot + 1) * total] for slot in range(groups)]
    projected = projected_rows(split, lon_shift, field.shape, blocks, west, first)
    out[...] = field[...].astype(jnp.float32) + projected


def second_output_kernel(split, groups, lon_shift, partial, weight, *refs):
    *blocks, out = refs
    west = [block[...].astype(jnp.float32) for block in blocks[groups:]]
    projected = projected_rows(split, lon_shift, partial.shape, blocks[:groups], west, weight)
    out[...] = (partial[...] + projected).astype(jnp.bfloat16)


def whole(count):
    return [pl.BlockSpec(memory_space=pltpu.VMEM)] * count


def shards(field_tokens, lon_shift, norm_gain, qkv_weight, out_weight):
    _, rows, columns, features = field_tokens.shape
    groups = lax.axis_size("tok")
    local = HEADS // groups
    width = local * HD
    span = round_up(3 * HD + 1, LANES)
    split = round_up(columns // 2, SUBLANES)
    field = field_tokens[0]
    smem = pl.BlockSpec(memory_space=pltpu.SMEM)
    kept_count, mixed_count = rows * (columns - split), rows * split

    def limit(size):
        return pltpu.CompilerParams(vmem_limit_bytes=size * MIB)

    def projection(kernel, count, parts, specs, held, params, *operands):
        block = jax.ShapeDtypeStruct((count, local * span // parts), jnp.bfloat16)
        return pl.pallas_call(
            functools.partial(kernel, split),
            out_shape=[block] * (parts * groups),
            in_specs=specs,
            out_specs=whole(parts * groups),
            scratch_shapes=[
                pltpu.VMEM((groups, count, local * span), jnp.bfloat16),
                *held,
            ],
            compiler_params=params,
            cost_estimate=pl.CostEstimate(
                flops=2 * count * features * 3 * HEADS * HD,
                bytes_accessed=2 * features * (3 * HEADS * HD + 2 * count),
                transcendentals=0,
            ),
        )(*operands)

    def spread(blocks, sign):
        return [blocks[0]] + [
            shifted(blocks[distance], "tok", sign * distance) for distance in range(1, groups)
        ]

    eastern = shifted(field[:, :split], "win", -LAT_WINDOWS)
    hbm = pl.BlockSpec(memory_space=pltpu.HBM)
    operands = (field, norm_gain, qkv_weight)
    held = [
        pltpu.VMEM(qkv_weight.shape, qkv_weight.dtype),
        pltpu.SemaphoreType.DMA((3,)),
        pltpu.VMEM(field.shape, field.dtype),
        pltpu.VMEM(norm_gain.shape, norm_gain.dtype),
    ]
    kept = spread(projection(kept_kernel, kept_count, 1, [hbm] * 3, held, limit(60), *operands), 1)
    specs = [*whole(2), hbm, smem, *whole(1)]
    operands += (lon_shift, eastern)
    mixed = projection(mixed_kernel, mixed_count, local, specs, held[:2], limit(52), *operands)
    ahead = [None] * (groups - 1)
    first_mixed = spread(after(mixed[:groups], [*ahead, kept[1]]), 1)

    second_mixed = spread(after(mixed[groups:], [None, *kept[2:], first_mixed[1]]), 1)

    total = groups * rows * columns
    step = total // 5
    mixed_packed = packed_rows(mixed_count)[0]
    all_packed = mixed_packed + packed_rows(kept_count)[0]

    def block(count):
        return jax.ShapeDtypeStruct((count, LANES), jnp.bfloat16)

    def attention(head, out_shape, blocks):
        return pl.pallas_call(
            functools.partial(attention_kernel, head, groups),
            out_shape=out_shape,
            in_specs=whole(len(blocks)),
            out_specs=whole(len(out_shape)),
            scratch_shapes=[
                pltpu.VMEM((total, span), jnp.bfloat16),
                pltpu.VMEM((span, total), jnp.bfloat16),
                pltpu.VMEM((total, LANES), jnp.float32),
                pltpu.VMEM((step, total), jnp.float32),
                pltpu.VMEM((step, total), jnp.float32),
                pltpu.VMEM((step, total), jnp.bfloat16),
                pltpu.VMEM((step, total), jnp.bfloat16),
            ],
            compiler_params=limit(32),
            cost_estimate=pl.CostEstimate(
                flops=4 * total * total * span,
                bytes_accessed=2 * total * (span + LANES),
                transcendentals=total * total,
            ),
        )(*blocks)

    first = attention(0, [block(all_packed)] * groups, [*kept, *first_mixed])
    first = spread(first, -1)
    second = attention(
        1,
        [block(all_packed)] * groups + [block(mixed_packed)] * groups,
        [*kept, *second_mixed],
    )
    windows = lax.axis_size("win")
    western = []
    for distance in range(groups):
        route = [
            (
                win * groups + tok,
                (win + LAT_WINDOWS) % windows * groups + (tok - distance) % groups,
            )
            for win in range(windows)
            for tok in range(groups)
        ]
        western.append(lax.ppermute(second[groups + distance], ("win", "tok"), route))
    returned = [lax.optimization_barrier((block, second[0]))[0] for block in first]
    second = spread(after(second[:groups], [None, *first[1:]]), -1)
    first_western = pl.pallas_call(
        mixed_rows_kernel,
        out_shape=block(groups * mixed_packed),
        in_specs=whole(groups),
        out_specs=pl.BlockSpec(memory_space=pltpu.VMEM),
        compiler_params=limit(16),
        cost_estimate=pl.CostEstimate(
            flops=0, bytes_accessed=4 * groups * all_packed * LANES, transcendentals=0
        ),
    )(*returned)
    first_western = shifted(first_western, "win", LAT_WINDOWS)

    cost = pl.CostEstimate(
        flops=2 * rows * columns * groups * LANES * features,
        bytes_accessed=features * (HEADS * HD + 6 * rows * columns),
        transcendentals=0,
    )
    ordered = (groups * LANES, features)
    partial, weight = pl.pallas_call(
        functools.partial(first_output_kernel, split, groups),
        out_shape=[
            jax.ShapeDtypeStruct(field.shape, jnp.float32),
            jax.ShapeDtypeStruct(ordered, jnp.bfloat16),
        ],
        in_specs=[smem] + whole(3 + groups),
        out_specs=whole(2),
        scratch_shapes=[pltpu.VMEM(ordered, jnp.bfloat16)],
        compiler_params=limit(24),
        cost_estimate=cost,
    )(lon_shift, field, out_weight, *first, first_western)
    result = pl.pallas_call(
        functools.partial(second_output_kernel, split, groups),
        out_shape=jax.ShapeDtypeStruct(field.shape, jnp.bfloat16),
        in_specs=[smem] + whole(2 + 2 * groups),
        out_specs=pl.BlockSpec(memory_space=pltpu.VMEM),
        compiler_params=limit(24),
        cost_estimate=cost,
    )(lon_shift, partial, weight, *second, *western)
    return result[None]


def solution(mesh):
    placed = (P("win", "tok", None, None), P(), P(), P(), P())
    return jax.shard_map(
        shards, mesh=mesh, in_specs=placed, out_specs=P("win", "tok", None, None), check_vma=False
    )
```

```python
import functools

import jax
import jax.numpy as jnp
from jax import lax
from jax.experimental import pallas as pl
from jax.experimental.pallas import tpu as pltpu
from jax.sharding import PartitionSpec as P

HEADS = 8
HD = 80
LAT_WINDOWS = 4
LANES = 128
SUBLANES = 8
MIB = 1024 * 1024


def round_up(value, unit):
    return -(-value // unit) * unit


def shifted(block, axis, distance):
    count = lax.axis_size(axis)
    return lax.ppermute(block, axis, [(i, (i + distance) % count) for i in range(count)])


def after(blocks, arrived):
    return [
        block if other is None else lax.optimization_barrier((block, other))[0]
        for block, other in zip(blocks, arrived)
    ]


def column_offset(lon_shift):
    return lon_shift[lax.rem(lax.axis_index("win"), LAT_WINDOWS)]


def project(tokens, gain, weight, copy, slots, outs):
    groups = slots.shape[0]
    local = HEADS // groups
    count, features = tokens.shape
    span = slots.shape[2] // local
    factor = lax.rsqrt(jnp.mean(tokens * tokens, axis=-1, keepdims=True) + 1e-06)
    normed = (tokens * factor * gain[...].reshape(1, features)).astype(jnp.bfloat16)
    if copy is not None:
        copy.wait()
    qkv = jnp.dot(normed, weight[...], preferred_element_type=jnp.float32).astype(jnp.bfloat16)
    tail = jnp.ones((count, span - 3 * HD), jnp.bfloat16)
    place = lax.axis_index("tok")
    for group in range(groups):
        slot = lax.rem(group - place + groups, groups)
        columns = []
        for head in range(group * local, (group + 1) * local):
            columns += [
                qkv[:, (kind * HEADS + head) * HD : (kind * HEADS + head + 1) * HD]
                for kind in (1, 0, 2)
            ] + [tail]
        slots[slot] = jnp.concatenate(columns, axis=1)
    for index, out in enumerate(outs):
        first = index // groups * out.shape[1]
        out[...] = slots[index % groups, :, first : first + out.shape[1]]


def kept_kernel(split, field, gain, weight, *refs):
    *outs, slots, held_weight, sems, held_field, held_gain = refs
    copy = pltpu.make_async_copy(weight, held_weight, sems.at[0])
    first = pltpu.make_async_copy(field, held_field, sems.at[1])
    second = pltpu.make_async_copy(gain, held_gain, sems.at[2])
    first.start()
    second.start()
    copy.start()
    first.wait()
    second.wait()
    rows, columns, features = field.shape
    tokens = held_field[...].astype(jnp.float32)[:, split:]
    tokens = tokens.reshape(rows * (columns - split), features)
    project(tokens, held_gain, held_weight, copy, slots, outs)


def mixed_kernel(split, field, gain, weight, lon_shift, eastern, *refs):
    *outs, slots = refs
    rows, _, features = field.shape
    own = field[...].astype(jnp.float32)[:, :split]
    column = lax.broadcasted_iota(jnp.int32, own.shape, 1)
    tokens = jnp.where(column < column_offset(lon_shift), eastern[...].astype(jnp.float32), own)
    project(tokens.reshape(rows * split, features), gain, weight, None, slots, outs)


def gather(head, kept, mixed, held, keys):
    span = held.shape[1]
    start = 0
    for block in kept:
        held[start : start + block.shape[0]] = block[:, head * span : (head + 1) * span]
        start += block.shape[0]
    for block in mixed:
        held[start : start + block.shape[0]] = block[...]
        start += block.shape[0]
    keys[...] = held[:, :LANES].T


def attend(held, keys, attended, scores, weights):
    span = held.shape[1]
    factor = HD ** (-0.5) * 1.4426950408889634
    step = scores[0].shape[0]
    chunk = 16
    steps = held.shape[0] // step

    def score(index, out):
        first = index * step
        queries = pltpu.roll(held[first : first + step].astype(jnp.float32), span - HD, axis=1)
        queries = queries[:, :LANES]
        lane = lax.broadcasted_iota(jnp.int32, queries.shape, 1)
        queries = jnp.where(lane < HD, queries, 0.0).astype(jnp.bfloat16)
        out[...] = jnp.dot(queries, keys[...], preferred_element_type=jnp.float32)

    score(0, scores[0])
    for index in range(steps):
        if index + 1 < steps:
            score(index + 1, scores[(index + 1) % 2])
        now, out = scores[index % 2], weights[index % 2]
        for first in range(0, step, chunk):
            part = now[first : first + chunk]
            top = jnp.max(part, axis=-1, keepdims=True)
            out[first : first + chunk] = jnp.exp2((part - top) * factor).astype(jnp.bfloat16)
        values = jnp.dot(out[...], held[:, span - LANES :], preferred_element_type=jnp.float32)
        first = 2 * HD - (span - LANES)
        values = values / values[:, first + HD : first + HD + 1]
        attended[index * step : (index + 1) * step] = pltpu.roll(values, LANES - first, axis=1)


def packed_rows(count):
    part = round_up(-(-count * (HD - LANES // 2) // LANES), SUBLANES)
    return count // 2 + part, part


def pack(rows):
    count = rows.shape[0]
    half = LANES // 2
    rest = HD - half
    part = packed_rows(count)[1]
    lane = lax.broadcasted_iota(jnp.int32, (count // 2, LANES), 1)
    main = jnp.where(lane < half, rows[: count // 2], pltpu.roll(rows[count // 2 :], half, axis=1))
    lane = lax.broadcasted_iota(jnp.int32, (part, LANES), 1)
    rests = jnp.zeros((part, LANES), jnp.float32)
    for index in range(-(-count // part)):
        piece = rows[index * part : (index + 1) * part]
        if piece.shape[0] < part:
            empty = jnp.zeros((part - piece.shape[0], LANES), jnp.float32)
            piece = jnp.concatenate([piece, empty], axis=0)
        turn = (index * rest + half) % LANES
        piece = pltpu.roll(piece, turn, axis=1) if turn else piece
        rests = jnp.where(lane // rest == index, piece, rests)
    return jnp.concatenate([main, rests], axis=0)


def unpack(block, count):
    half = LANES // 2
    rest = HD - half
    part = packed_rows(count)[1]
    main, rests = block[: count // 2], block[count // 2 : count // 2 + part]
    main = jnp.concatenate([main, pltpu.roll(main, half, axis=1)], axis=0)
    pieces = []
    for index in range(-(-count // part)):
        turn = (half - index * rest) % LANES
        piece = pltpu.roll(rests, turn, axis=1) if turn else rests
        pieces.append(piece[: min(part, count - index * part)])
    lane = lax.broadcasted_iota(jnp.int32, main.shape, 1)
    return jnp.where(lane < half, main, jnp.concatenate(pieces, axis=0))


def packed_tokens(count):
    half = LANES // 2
    total, part = packed_rows(count)
    row = lax.broadcasted_iota(jnp.int32, (total, LANES), 0)
    lane = lax.broadcasted_iota(jnp.int32, (total, LANES), 1)
    main = row + jnp.where(lane < half, 0, count // 2)
    rests = row - count // 2 + lane // (HD - half) * part
    return jnp.where(row < count // 2, main, rests)


def attention_kernel(head, groups, *refs):
    kept, mixed = refs[:groups], refs[groups : 2 * groups]
    kept_out, mixed_out, held, keys, attended, *rest = refs[2 * groups :]
    gather(head, kept, mixed, held, keys)
    attend(held, keys, attended, rest[:2], rest[2:])
    start = 0
    for blocks, out in ((kept, kept_out), (mixed, mixed_out)):
        packed = []
        for block in blocks:
            packed.append(pack(attended[start : start + block.shape[0]]))
            start += block.shape[0]
        out[...] = jnp.concatenate(packed, axis=0).astype(jnp.bfloat16)


def select_kernel(split, count, lon_shift, kept, mixed, western, *outs):
    taken = lax.rem(packed_tokens(count), split) < column_offset(lon_shift)
    own, west = mixed[...].astype(jnp.float32), western[...].astype(jnp.float32)
    rest = kept[...].astype(jnp.float32)
    left, right = own.shape[0] // len(outs), rest.shape[0] // len(outs)
    for group, out in enumerate(outs):
        rows = slice(group * left, (group + 1) * left)
        chosen = jnp.where(taken, west[rows], own[rows])
        out[...] = jnp.concatenate(
            [chosen, rest[group * right : (group + 1) * right]], axis=0
        ).astype(jnp.bfloat16)


def projected_rows(split, shape, blocks, weight):
    rows, columns, _ = shape
    kept_count, mixed_count = rows * (columns - split), rows * split
    total = packed_rows(mixed_count)[0]
    attended = []
    for block in blocks:
        block = block[...].astype(jnp.float32)
        left, right = unpack(block[:total], mixed_count), unpack(block[total:], kept_count)
        attended.append(jnp.concatenate([right, left], axis=0))
    attended = jnp.concatenate(attended, axis=1).astype(jnp.bfloat16)
    projected = jnp.dot(attended, weight[...], preferred_element_type=jnp.float32)
    return by_column(projected, rows, columns, split)


def by_column(projected, rows, columns, split):
    kept_count = rows * (columns - split)
    right = projected[:kept_count].reshape(rows, columns - split, -1)
    left = projected[kept_count:].reshape(rows, split, -1)
    return jnp.concatenate([left, right], axis=1)


def first_output_kernel(split, groups, field, weight, *refs):
    *blocks, out, second, first = refs
    features = field.shape[2]
    for slot in range(groups):
        group = lax.rem(lax.axis_index("tok") + slot, groups)
        for head, ordered in enumerate((first, second)):
            at = pl.multiple_of((group * HEADS // groups + head) * HD, 16)
            ordered[slot * LANES : slot * LANES + HD] = weight[pl.ds(at, HD)]
            ordered[slot * LANES + HD : (slot + 1) * LANES] = jnp.zeros(
                (LANES - HD, features), jnp.bfloat16
            )
    projected = projected_rows(split, field.shape, blocks, first)
    out[...] = field[...].astype(jnp.float32) + projected


def second_output_kernel(split, partial, weight, *refs):
    *blocks, out = refs
    projected = projected_rows(split, partial.shape, blocks, weight)
    out[...] = (partial[...] + projected).astype(jnp.bfloat16)


def whole(count):
    return [pl.BlockSpec(memory_space=pltpu.VMEM)] * count


def shards(field_tokens, lon_shift, norm_gain, qkv_weight, out_weight):
    _, rows, columns, features = field_tokens.shape
    groups = lax.axis_size("tok")
    local = HEADS // groups
    width = local * HD
    span = round_up(3 * HD + 1, LANES)
    split = round_up(columns // 2, SUBLANES)
    field = field_tokens[0]
    smem = pl.BlockSpec(memory_space=pltpu.SMEM)
    kept_count, mixed_count = rows * (columns - split), rows * split

    def limit(size):
        return pltpu.CompilerParams(vmem_limit_bytes=size * MIB)

    def projection(kernel, count, parts, specs, held, params, *operands):
        block = jax.ShapeDtypeStruct((count, local * span // parts), jnp.bfloat16)
        return pl.pallas_call(
            functools.partial(kernel, split),
            out_shape=[block] * (parts * groups),
            in_specs=specs,
            out_specs=whole(parts * groups),
            scratch_shapes=[
                pltpu.VMEM((groups, count, local * span), jnp.bfloat16),
                *held,
            ],
            compiler_params=params,
            cost_estimate=pl.CostEstimate(
                flops=2 * count * features * 3 * HEADS * HD,
                bytes_accessed=2 * features * (3 * HEADS * HD + 2 * count),
                transcendentals=0,
            ),
        )(*operands)

    def spread(blocks, sign):
        arrived = list(blocks)
        for distance in sorted(range(1, groups), key=lambda step: step * (step - groups)):
            arrived[distance] = shifted(blocks[distance], "tok", sign * distance)
        return arrived

    eastern = shifted(field[:, :split], "win", -LAT_WINDOWS)
    hbm = pl.BlockSpec(memory_space=pltpu.HBM)
    operands = (field, norm_gain, qkv_weight)
    held = [
        pltpu.VMEM(qkv_weight.shape, qkv_weight.dtype),
        pltpu.SemaphoreType.DMA((3,)),
        pltpu.VMEM(field.shape, field.dtype),
        pltpu.VMEM(norm_gain.shape, norm_gain.dtype),
    ]
    kept = spread(projection(kept_kernel, kept_count, 1, [hbm] * 3, held, limit(60), *operands), 1)
    specs = [*whole(3), smem, *whole(1)]
    operands += (lon_shift, eastern)
    mixed = projection(mixed_kernel, mixed_count, local, specs, [], limit(48), *operands)
    first_mixed = spread(after(mixed[:groups], [None, *kept[1:]]), 1)
    second_mixed = spread(after(mixed[groups:], [None, *first_mixed[1:]]), 1)

    total = groups * rows * columns
    step = total // 5
    mixed_packed, kept_packed = packed_rows(mixed_count)[0], packed_rows(kept_count)[0]

    def block(count):
        return jax.ShapeDtypeStruct((count, LANES), jnp.bfloat16)

    def attention(head, *blocks):
        return pl.pallas_call(
            functools.partial(attention_kernel, head, groups),
            out_shape=[block(groups * kept_packed), block(groups * mixed_packed)],
            in_specs=whole(len(blocks)),
            out_specs=whole(2),
            scratch_shapes=[
                pltpu.VMEM((total, span), jnp.bfloat16),
                pltpu.VMEM((LANES, total), jnp.bfloat16),
                pltpu.VMEM((total, LANES), jnp.float32),
                pltpu.VMEM((step, total), jnp.float32),
                pltpu.VMEM((step, total), jnp.float32),
                pltpu.VMEM((step, total), jnp.bfloat16),
                pltpu.VMEM((step, total), jnp.bfloat16),
            ],
            compiler_params=limit(32),
            cost_estimate=pl.CostEstimate(
                flops=4 * total * total * span,
                bytes_accessed=2 * total * (span + LANES),
                transcendentals=total * total,
            ),
        )(*blocks)

    def back(kept_values, mixed_values):
        western = shifted(mixed_values, "win", LAT_WINDOWS)
        selected = pl.pallas_call(
            functools.partial(select_kernel, split, mixed_count),
            out_shape=[block(mixed_packed + kept_packed)] * groups,
            in_specs=[smem] + whole(3),
            out_specs=whole(groups),
            compiler_params=limit(16),
            cost_estimate=pl.CostEstimate(
                flops=total * LANES * 20, bytes_accessed=8 * total * LANES, transcendentals=0
            ),
        )(lon_shift, kept_values, mixed_values, western)
        return spread(selected, -1)

    first = back(*attention(0, *kept, *first_mixed))
    second = back(*attention(1, *kept, *second_mixed))

    cost = pl.CostEstimate(
        flops=2 * rows * columns * groups * LANES * features,
        bytes_accessed=features * (HEADS * HD + 6 * rows * columns),
        transcendentals=0,
    )
    ordered = (groups * LANES, features)
    partial, weight = pl.pallas_call(
        functools.partial(first_output_kernel, split, groups),
        out_shape=[
            jax.ShapeDtypeStruct(field.shape, jnp.float32),
            jax.ShapeDtypeStruct(ordered, jnp.bfloat16),
        ],
        in_specs=whole(2 + groups),
        out_specs=whole(2),
        scratch_shapes=[pltpu.VMEM(ordered, jnp.bfloat16)],
        compiler_params=limit(24),
        cost_estimate=cost,
    )(field, out_weight, *first)
    result = pl.pallas_call(
        functools.partial(second_output_kernel, split),
        out_shape=jax.ShapeDtypeStruct(field.shape, jnp.bfloat16),
        in_specs=whole(2 + groups),
        out_specs=pl.BlockSpec(memory_space=pltpu.VMEM),
        compiler_params=limit(24),
        cost_estimate=cost,
    )(partial, weight, *second)
    return result[None]


def solution(mesh):
    placed = (P("win", "tok", None, None), P(), P(), P(), P())
    return jax.shard_map(
        shards, mesh=mesh, in_specs=placed, out_specs=P("win", "tok", None, None), check_vma=False
    )
```

```python
import functools

import jax
import jax.numpy as jnp
from jax import lax
from jax.experimental import pallas as pl
from jax.experimental.pallas import tpu as pltpu
from jax.sharding import PartitionSpec as P

HEADS = 8
HD = 80
LAT_WINDOWS = 4
LANES = 128
SUBLANES = 8
MIB = 1024 * 1024


def round_up(value, unit):
    return -(-value // unit) * unit


def shifted(block, axis, distance):
    count = lax.axis_size(axis)
    return lax.ppermute(block, axis, [(i, (i + distance) % count) for i in range(count)])


def travel_order(groups):
    return sorted(range(groups), key=lambda distance: (distance > 0, distance * (distance - groups)))


def after(blocks, arrived):
    return [
        block if other is None else lax.optimization_barrier((block, other))[0]
        for block, other in zip(blocks, arrived)
    ]


def column_offset(lon_shift):
    return lon_shift[lax.rem(lax.axis_index("win"), LAT_WINDOWS)]


def project(tokens, gain, weight, copies, slots, outs):
    groups = slots.shape[0]
    local = HEADS // groups
    count, features = tokens.shape
    span = slots.shape[2] // local
    factor = lax.rsqrt(jnp.mean(tokens * tokens, axis=-1, keepdims=True) + 1e-06)
    normed = (tokens * factor * gain[...].reshape(1, features)).astype(jnp.bfloat16)
    qkv = None
    for copy, first, size in copies:
        if copy is not None:
            copy.wait()
        inner = slice(first, first + size)
        share = jnp.dot(normed[:, inner], weight[inner], preferred_element_type=jnp.float32)
        qkv = share if qkv is None else qkv + share
    qkv = qkv.astype(jnp.bfloat16)
    tail = jnp.ones((count, span - 3 * HD), jnp.bfloat16)
    place = lax.axis_index("tok")
    for group in range(groups):
        slot = lax.rem(group - place + groups, groups)
        columns = []
        for head in range(group * local, (group + 1) * local):
            columns += [
                qkv[:, (kind * HEADS + head) * HD : (kind * HEADS + head + 1) * HD]
                for kind in (1, 0, 2)
            ] + [tail]
        slots[slot] = jnp.concatenate(columns, axis=1)
    for index, out in enumerate(outs):
        first = index // groups * out.shape[1]
        slot = travel_order(groups)[index % groups]
        out[...] = slots[slot, :, first : first + out.shape[1]]


def kept_kernel(split, field, gain, weight, *refs):
    *outs, slots, held_weight, sems, held_field, held_gain = refs
    half = weight.shape[0] // (2 * LANES) // 2 * 2 * LANES
    copies = []
    for start, size in ((0, half), (half, weight.shape[0] - half)):
        inner = pl.ds(start, size)
        copy = pltpu.make_async_copy(weight.at[inner], held_weight.at[inner], sems.at[len(copies)])
        copies.append((copy, start, size))
    first = pltpu.make_async_copy(field, held_field, sems.at[2])
    second = pltpu.make_async_copy(gain, held_gain, sems.at[3])
    first.start()
    second.start()
    for copy, _, _ in copies:
        copy.start()
    first.wait()
    second.wait()
    rows, columns, features = field.shape
    tokens = held_field[...].astype(jnp.float32)[:, split:]
    tokens = tokens.reshape(rows * (columns - split), features)
    project(tokens, held_gain, held_weight, copies, slots, outs)


def mixed_kernel(split, field, gain, weight, lon_shift, eastern, *refs):
    *outs, slots = refs
    rows, _, features = field.shape
    own = field[...].astype(jnp.float32)[:, :split]
    column = lax.broadcasted_iota(jnp.int32, own.shape, 1)
    tokens = jnp.where(column < column_offset(lon_shift), eastern[...].astype(jnp.float32), own)
    copies = [(None, 0, features)]
    project(tokens.reshape(rows * split, features), gain, weight, copies, slots, outs)


def gather(head, kept, mixed, held, keys):
    span = held.shape[1]
    start = 0
    for block in kept:
        held[start : start + block.shape[0]] = block[:, head * span : (head + 1) * span]
        start += block.shape[0]
    for block in mixed:
        held[start : start + block.shape[0]] = block[...]
        start += block.shape[0]
    keys[...] = held[:, :LANES].T


def attend(held, keys, attended, scores, weights):
    span = held.shape[1]
    factor = HD ** (-0.5) * 1.4426950408889634
    step = scores[0].shape[0]
    chunk = 16
    steps = held.shape[0] // step

    def score(index, out):
        first = index * step
        queries = pltpu.roll(held[first : first + step].astype(jnp.float32), span - HD, axis=1)
        queries = queries[:, :LANES]
        lane = lax.broadcasted_iota(jnp.int32, queries.shape, 1)
        queries = jnp.where(lane < HD, queries, 0.0).astype(jnp.bfloat16)
        out[...] = jnp.dot(queries, keys[...], preferred_element_type=jnp.float32)

    score(0, scores[0])
    for index in range(steps):
        if index + 1 < steps:
            score(index + 1, scores[(index + 1) % 2])
        now, out = scores[index % 2], weights[index % 2]
        for first in range(0, step, chunk):
            part = now[first : first + chunk]
            top = jnp.max(part, axis=-1, keepdims=True)
            out[first : first + chunk] = jnp.exp2((part - top) * factor).astype(jnp.bfloat16)
        values = jnp.dot(out[...], held[:, span - LANES :], preferred_element_type=jnp.float32)
        first = 2 * HD - (span - LANES)
        values = values / values[:, first + HD : first + HD + 1]
        attended[index * step : (index + 1) * step] = pltpu.roll(values, LANES - first, axis=1)


def packed_rows(count):
    part = round_up(-(-count * (HD - LANES // 2) // LANES), SUBLANES)
    return count // 2 + part, part


def pack(rows):
    count = rows.shape[0]
    half = LANES // 2
    rest = HD - half
    part = packed_rows(count)[1]
    lane = lax.broadcasted_iota(jnp.int32, (count // 2, LANES), 1)
    main = jnp.where(lane < half, rows[: count // 2], pltpu.roll(rows[count // 2 :], half, axis=1))
    lane = lax.broadcasted_iota(jnp.int32, (part, LANES), 1)
    rests = jnp.zeros((part, LANES), jnp.float32)
    for index in range(-(-count // part)):
        piece = rows[index * part : (index + 1) * part]
        if piece.shape[0] < part:
            empty = jnp.zeros((part - piece.shape[0], LANES), jnp.float32)
            piece = jnp.concatenate([piece, empty], axis=0)
        turn = (index * rest + half) % LANES
        piece = pltpu.roll(piece, turn, axis=1) if turn else piece
        rests = jnp.where(lane // rest == index, piece, rests)
    return jnp.concatenate([main, rests], axis=0)


def unpack(block, count):
    half = LANES // 2
    rest = HD - half
    part = packed_rows(count)[1]
    main, rests = block[: count // 2], block[count // 2 : count // 2 + part]
    main = jnp.concatenate([main, pltpu.roll(main, half, axis=1)], axis=0)
    pieces = []
    for index in range(-(-count // part)):
        turn = (half - index * rest) % LANES
        piece = pltpu.roll(rests, turn, axis=1) if turn else rests
        pieces.append(piece[: min(part, count - index * part)])
    lane = lax.broadcasted_iota(jnp.int32, main.shape, 1)
    return jnp.where(lane < half, main, jnp.concatenate(pieces, axis=0))


def packed_tokens(count):
    half = LANES // 2
    total, part = packed_rows(count)
    row = lax.broadcasted_iota(jnp.int32, (total, LANES), 0)
    lane = lax.broadcasted_iota(jnp.int32, (total, LANES), 1)
    main = row + jnp.where(lane < half, 0, count // 2)
    rests = row - count // 2 + lane // (HD - half) * part
    return jnp.where(row < count // 2, main, rests)


def attention_kernel(head, groups, *refs):
    kept, mixed = refs[:groups], refs[groups : 2 * groups]
    kept_out, mixed_out, held, keys, attended, *rest = refs[2 * groups :]
    gather(head, kept, mixed, held, keys)
    attend(held, keys, attended, rest[:2], rest[2:])
    start = 0
    for blocks, out in ((kept, kept_out), (mixed, mixed_out)):
        packed = []
        for block in blocks:
            packed.append(pack(attended[start : start + block.shape[0]]))
            start += block.shape[0]
        out[...] = jnp.concatenate(packed, axis=0).astype(jnp.bfloat16)


def select_kernel(split, count, lon_shift, kept, mixed, western, *outs):
    taken = lax.rem(packed_tokens(count), split) < column_offset(lon_shift)
    own, west = mixed[...].astype(jnp.float32), western[...].astype(jnp.float32)
    rest = kept[...].astype(jnp.float32)
    left, right = own.shape[0] // len(outs), rest.shape[0] // len(outs)
    for group, out in enumerate(outs):
        rows = slice(group * left, (group + 1) * left)
        chosen = jnp.where(taken, west[rows], own[rows])
        out[...] = jnp.concatenate(
            [chosen, rest[group * right : (group + 1) * right]], axis=0
        ).astype(jnp.bfloat16)


def projected_rows(split, shape, blocks, weight):
    rows, columns, _ = shape
    kept_count, mixed_count = rows * (columns - split), rows * split
    total = packed_rows(mixed_count)[0]
    attended = []
    for block in blocks:
        block = block[...].astype(jnp.float32)
        left, right = unpack(block[:total], mixed_count), unpack(block[total:], kept_count)
        attended.append(jnp.concatenate([right, left], axis=0))
    attended = jnp.concatenate(attended, axis=1).astype(jnp.bfloat16)
    projected = jnp.dot(attended, weight[...], preferred_element_type=jnp.float32)
    return by_column(projected, rows, columns, split)


def by_column(projected, rows, columns, split):
    kept_count = rows * (columns - split)
    right = projected[:kept_count].reshape(rows, columns - split, -1)
    left = projected[kept_count:].reshape(rows, split, -1)
    return jnp.concatenate([left, right], axis=1)


def first_output_kernel(split, groups, field, weight, *refs):
    *blocks, out, second, first = refs
    features = field.shape[2]
    for slot, distance in enumerate(travel_order(groups)):
        group = lax.rem(lax.axis_index("tok") + distance, groups)
        for head, ordered in enumerate((first, second)):
            at = pl.multiple_of((group * HEADS // groups + head) * HD, 16)
            ordered[slot * LANES : slot * LANES + HD] = weight[pl.ds(at, HD)]
            ordered[slot * LANES + HD : (slot + 1) * LANES] = jnp.zeros(
                (LANES - HD, features), jnp.bfloat16
            )
    projected = projected_rows(split, field.shape, blocks, first)
    out[...] = field[...].astype(jnp.float32) + projected


def second_output_kernel(split, partial, weight, *refs):
    *blocks, out = refs
    projected = projected_rows(split, partial.shape, blocks, weight)
    out[...] = (partial[...] + projected).astype(jnp.bfloat16)


def whole(count):
    return [pl.BlockSpec(memory_space=pltpu.VMEM)] * count


def shards(field_tokens, lon_shift, norm_gain, qkv_weight, out_weight):
    _, rows, columns, features = field_tokens.shape
    groups = lax.axis_size("tok")
    local = HEADS // groups
    width = local * HD
    span = round_up(3 * HD + 1, LANES)
    split = round_up(columns // 2, SUBLANES)
    field = field_tokens[0]
    smem = pl.BlockSpec(memory_space=pltpu.SMEM)
    kept_count, mixed_count = rows * (columns - split), rows * split

    def limit(size):
        return pltpu.CompilerParams(vmem_limit_bytes=size * MIB)

    def projection(kernel, count, parts, specs, held, params, *operands):
        block = jax.ShapeDtypeStruct((count, local * span // parts), jnp.bfloat16)
        return pl.pallas_call(
            functools.partial(kernel, split),
            out_shape=[block] * (parts * groups),
            in_specs=specs,
            out_specs=whole(parts * groups),
            scratch_shapes=[
                pltpu.VMEM((groups, count, local * span), jnp.bfloat16),
                *held,
            ],
            compiler_params=params,
            cost_estimate=pl.CostEstimate(
                flops=2 * count * features * 3 * HEADS * HD,
                bytes_accessed=2 * features * (3 * HEADS * HD + 2 * count),
                transcendentals=0,
            ),
        )(*operands)

    def spread(blocks, sign):
        return [blocks[0]] + [
            shifted(block, "tok", sign * distance)
            for block, distance in zip(blocks[1:], travel_order(groups)[1:])
        ]

    eastern = shifted(field[:, :split], "win", -LAT_WINDOWS)
    hbm = pl.BlockSpec(memory_space=pltpu.HBM)
    operands = (field, norm_gain, qkv_weight)
    held = [
        pltpu.VMEM(qkv_weight.shape, qkv_weight.dtype),
        pltpu.SemaphoreType.DMA((4,)),
        pltpu.VMEM(field.shape, field.dtype),
        pltpu.VMEM(norm_gain.shape, norm_gain.dtype),
    ]
    kept = spread(projection(kept_kernel, kept_count, 1, [hbm] * 3, held, limit(60), *operands), 1)
    specs = [*whole(3), smem, *whole(1)]
    operands += (lon_shift, eastern)
    mixed = projection(mixed_kernel, mixed_count, local, specs, [], limit(48), *operands)
    first_mixed = spread(after(mixed[:groups], [None, *kept[1:]]), 1)
    second_mixed = spread(after(mixed[groups:], [None, *first_mixed[1:]]), 1)

    total = groups * rows * columns
    step = total // 5
    mixed_packed, kept_packed = packed_rows(mixed_count)[0], packed_rows(kept_count)[0]

    def block(count):
        return jax.ShapeDtypeStruct((count, LANES), jnp.bfloat16)

    def attention(head, *blocks):
        return pl.pallas_call(
            functools.partial(attention_kernel, head, groups),
            out_shape=[block(groups * kept_packed), block(groups * mixed_packed)],
            in_specs=whole(len(blocks)),
            out_specs=whole(2),
            scratch_shapes=[
                pltpu.VMEM((total, span), jnp.bfloat16),
                pltpu.VMEM((LANES, total), jnp.bfloat16),
                pltpu.VMEM((total, LANES), jnp.float32),
                pltpu.VMEM((step, total), jnp.float32),
                pltpu.VMEM((step, total), jnp.float32),
                pltpu.VMEM((step, total), jnp.bfloat16),
                pltpu.VMEM((step, total), jnp.bfloat16),
            ],
            compiler_params=limit(32),
            cost_estimate=pl.CostEstimate(
                flops=4 * total * total * span,
                bytes_accessed=2 * total * (span + LANES),
                transcendentals=total * total,
            ),
        )(*blocks)

    def back(kept_values, mixed_values):
        western = shifted(mixed_values, "win", LAT_WINDOWS)
        selected = pl.pallas_call(
            functools.partial(select_kernel, split, mixed_count),
            out_shape=[block(mixed_packed + kept_packed)] * groups,
            in_specs=[smem] + whole(3),
            out_specs=whole(groups),
            compiler_params=limit(16),
            cost_estimate=pl.CostEstimate(
                flops=total * LANES * 20, bytes_accessed=8 * total * LANES, transcendentals=0
            ),
        )(lon_shift, kept_values, mixed_values, western)
        return spread(selected, -1)

    first = back(*attention(0, *kept, *first_mixed))
    second = back(*attention(1, *kept, *second_mixed))

    cost = pl.CostEstimate(
        flops=2 * rows * columns * groups * LANES * features,
        bytes_accessed=features * (HEADS * HD + 6 * rows * columns),
        transcendentals=0,
    )
    ordered = (groups * LANES, features)
    partial, weight = pl.pallas_call(
        functools.partial(first_output_kernel, split, groups),
        out_shape=[
            jax.ShapeDtypeStruct(field.shape, jnp.float32),
            jax.ShapeDtypeStruct(ordered, jnp.bfloat16),
        ],
        in_specs=whole(2 + groups),
        out_specs=whole(2),
        scratch_shapes=[pltpu.VMEM(ordered, jnp.bfloat16)],
        compiler_params=limit(24),
        cost_estimate=cost,
    )(field, out_weight, *first)
    result = pl.pallas_call(
        functools.partial(second_output_kernel, split),
        out_shape=jax.ShapeDtypeStruct(field.shape, jnp.bfloat16),
        in_specs=whole(2 + groups),
        out_specs=pl.BlockSpec(memory_space=pltpu.VMEM),
        compiler_params=limit(24),
        cost_estimate=cost,
    )(partial, weight, *second)
    return result[None]


def solution(mesh):
    placed = (P("win", "tok", None, None), P(), P(), P(), P())
    return jax.shard_map(
        shards, mesh=mesh, in_specs=placed, out_specs=P("win", "tok", None, None), check_vma=False
    )
```

```python
import functools

import jax
import jax.numpy as jnp
from jax import lax
from jax.experimental import pallas as pl
from jax.experimental.pallas import tpu as pltpu
from jax.sharding import PartitionSpec as P

HEADS = 8
HD = 80
LAT_WINDOWS = 4
LANES = 128
SUBLANES = 8
MIB = 1024 * 1024


def round_up(value, unit):
    return -(-value // unit) * unit


def shifted(block, axis, distance):
    count = lax.axis_size(axis)
    return lax.ppermute(block, axis, [(i, (i + distance) % count) for i in range(count)])


def after(blocks, arrived):
    return [
        block if other is None else lax.optimization_barrier((block, other))[0]
        for block, other in zip(blocks, arrived)
    ]


def column_offset(lon_shift):
    return lon_shift[lax.rem(lax.axis_index("win"), LAT_WINDOWS)]


def project(tokens, gain, weight, copy, slots, outs):
    groups = slots.shape[0]
    local = HEADS // groups
    count, features = tokens.shape
    span = slots.shape[2] // local
    factor = lax.rsqrt(jnp.mean(tokens * tokens, axis=-1, keepdims=True) + 1e-06)
    normed = (tokens * factor * gain[...].reshape(1, features)).astype(jnp.bfloat16)
    if copy is not None:
        copy.wait()
    qkv = jnp.dot(normed, weight[...], preferred_element_type=jnp.float32).astype(jnp.bfloat16)
    tail = jnp.ones((count, span - 3 * HD), jnp.bfloat16)
    place = lax.axis_index("tok")
    for group in range(groups):
        slot = lax.rem(group - place + groups, groups)
        columns = []
        for head in range(group * local, (group + 1) * local):
            columns += [
                qkv[:, (kind * HEADS + head) * HD : (kind * HEADS + head + 1) * HD]
                for kind in (1, 0, 2)
            ] + [tail]
        slots[slot] = jnp.concatenate(columns, axis=1)
    for index, out in enumerate(outs):
        first = index // groups * out.shape[1]
        out[...] = slots[index % groups, :, first : first + out.shape[1]]


def kept_kernel(split, field, gain, weight, *refs):
    *outs, slots, held_weight, sems, held_field, held_gain = refs
    copy = pltpu.make_async_copy(weight, held_weight, sems.at[0])
    first = pltpu.make_async_copy(field, held_field, sems.at[1])
    second = pltpu.make_async_copy(gain, held_gain, sems.at[2])
    first.start()
    second.start()
    copy.start()
    first.wait()
    second.wait()
    rows, columns, features = field.shape
    tokens = held_field[...].astype(jnp.float32)[:, split:]
    tokens = tokens.reshape(rows * (columns - split), features)
    project(tokens, held_gain, held_weight, copy, slots, outs)


def mixed_kernel(split, field, gain, weight, lon_shift, eastern, *refs):
    *outs, slots = refs
    rows, _, features = field.shape
    own = field[...].astype(jnp.float32)[:, :split]
    column = lax.broadcasted_iota(jnp.int32, own.shape, 1)
    tokens = jnp.where(column < column_offset(lon_shift), eastern[...].astype(jnp.float32), own)
    project(tokens.reshape(rows * split, features), gain, weight, None, slots, outs)


def gather(head, kept, mixed, held, keys):
    span = held.shape[1]
    start = 0
    for block in kept:
        held[start : start + block.shape[0]] = block[:, head * span : (head + 1) * span]
        start += block.shape[0]
    for block in mixed:
        held[start : start + block.shape[0]] = block[...]
        start += block.shape[0]
    keys[...] = held[:, :LANES].T


def attend(held, keys, attended, scores, weights):
    span = held.shape[1]
    factor = HD ** (-0.5) * 1.4426950408889634
    step = scores[0].shape[0]
    chunk = 16
    steps = held.shape[0] // step

    def score(index, out):
        first = index * step
        queries = pltpu.roll(held[first : first + step].astype(jnp.float32), span - HD, axis=1)
        queries = queries[:, :LANES]
        lane = lax.broadcasted_iota(jnp.int32, queries.shape, 1)
        queries = jnp.where(lane < HD, queries, 0.0).astype(jnp.bfloat16)
        out[...] = jnp.dot(queries, keys[...], preferred_element_type=jnp.float32)

    score(0, scores[0])
    for index in range(steps):
        if index + 1 < steps:
            score(index + 1, scores[(index + 1) % 2])
        now, out = scores[index % 2], weights[index % 2]
        for first in range(0, step, chunk):
            part = now[first : first + chunk]
            top = jnp.max(part, axis=-1, keepdims=True)
            out[first : first + chunk] = jnp.exp2((part - top) * factor).astype(jnp.bfloat16)
        values = jnp.dot(out[...], held[:, span - LANES :], preferred_element_type=jnp.float32)
        first = 2 * HD - (span - LANES)
        values = values / values[:, first + HD : first + HD + 1]
        attended[index * step : (index + 1) * step] = pltpu.roll(values, LANES - first, axis=1)


def packed_rows(count):
    part = round_up(-(-count * (HD - LANES // 2) // LANES), SUBLANES)
    return count // 2 + part, part


def pack(rows):
    count = rows.shape[0]
    half = LANES // 2
    rest = HD - half
    part = packed_rows(count)[1]
    lane = lax.broadcasted_iota(jnp.int32, (count // 2, LANES), 1)
    main = jnp.where(lane < half, rows[: count // 2], pltpu.roll(rows[count // 2 :], half, axis=1))
    lane = lax.broadcasted_iota(jnp.int32, (part, LANES), 1)
    rests = jnp.zeros((part, LANES), jnp.float32)
    for index in range(-(-count // part)):
        piece = rows[index * part : (index + 1) * part]
        if piece.shape[0] < part:
            empty = jnp.zeros((part - piece.shape[0], LANES), jnp.float32)
            piece = jnp.concatenate([piece, empty], axis=0)
        turn = (index * rest + half) % LANES
        piece = pltpu.roll(piece, turn, axis=1) if turn else piece
        rests = jnp.where(lane // rest == index, piece, rests)
    return jnp.concatenate([main, rests], axis=0)


def unpack(block, count):
    half = LANES // 2
    rest = HD - half
    part = packed_rows(count)[1]
    main, rests = block[: count // 2], block[count // 2 : count // 2 + part]
    main = jnp.concatenate([main, pltpu.roll(main, half, axis=1)], axis=0)
    pieces = []
    for index in range(-(-count // part)):
        turn = (half - index * rest) % LANES
        piece = pltpu.roll(rests, turn, axis=1) if turn else rests
        pieces.append(piece[: min(part, count - index * part)])
    lane = lax.broadcasted_iota(jnp.int32, main.shape, 1)
    return jnp.where(lane < half, main, jnp.concatenate(pieces, axis=0))


def packed_tokens(count):
    half = LANES // 2
    total, part = packed_rows(count)
    row = lax.broadcasted_iota(jnp.int32, (total, LANES), 0)
    lane = lax.broadcasted_iota(jnp.int32, (total, LANES), 1)
    main = row + jnp.where(lane < half, 0, count // 2)
    rests = row - count // 2 + lane // (HD - half) * part
    return jnp.where(row < count // 2, main, rests)


def attention_kernel(head, groups, *refs):
    kept, mixed = refs[:groups], refs[groups : 2 * groups]
    kept_out, mixed_out, held, keys, attended, *rest = refs[2 * groups :]
    gather(head, kept, mixed, held, keys)
    attend(held, keys, attended, rest[:2], rest[2:])
    start = 0
    for blocks, out in ((kept, kept_out), (mixed, mixed_out)):
        packed = []
        for block in blocks:
            packed.append(pack(attended[start : start + block.shape[0]]))
            start += block.shape[0]
        out[...] = jnp.concatenate(packed, axis=0).astype(jnp.bfloat16)


def select_kernel(split, count, groups, lon_shift, mixed, western, *refs):
    kept, outs = refs[:-groups], refs[-groups:]
    taken = lax.rem(packed_tokens(count), split) < column_offset(lon_shift)
    own, west = mixed[...].astype(jnp.float32), western[...].astype(jnp.float32)
    rests = [rest[...].astype(jnp.float32) for rest in kept]
    size = own.shape[0] // groups
    for group, out in enumerate(outs):
        rows = slice(group * size, (group + 1) * size)
        pieces = [jnp.where(taken, west[rows], own[rows])]
        for rest in rests:
            part = rest.shape[0] // groups
            pieces.append(rest[group * part : (group + 1) * part])
        out[...] = jnp.concatenate(pieces, axis=0).astype(jnp.bfloat16)


def projected(blocks, first, count, weight, shape):
    total = packed_rows(count)[0]
    columns = [unpack(block[first : first + total], count) for block in blocks]
    attended = jnp.concatenate(columns, axis=1).astype(jnp.bfloat16)
    return jnp.dot(attended, weight[...], preferred_element_type=jnp.float32).reshape(shape)


def first_output_kernel(split, groups, field, weight, *refs):
    *blocks, out, second, first = refs
    features = field.shape[2]
    for slot in range(groups):
        group = lax.rem(lax.axis_index("tok") + slot, groups)
        for head, ordered in enumerate((first, second)):
            at = pl.multiple_of((group * HEADS // groups + head) * HD, 16)
            ordered[slot * LANES : slot * LANES + HD] = weight[pl.ds(at, HD)]
            ordered[slot * LANES + HD : (slot + 1) * LANES] = jnp.zeros(
                (LANES - HD, features), jnp.bfloat16
            )
    rows, columns, _ = field.shape
    kept_count, mixed_count = rows * (columns - split), rows * split
    blocks = [block[...].astype(jnp.float32) for block in blocks]
    tokens = field[...].astype(jnp.float32)
    at = packed_rows(mixed_count)[0]
    shape = (rows, split, features)
    left = tokens[:, :split] + projected(blocks, 0, mixed_count, first, shape)
    shape = (rows, columns - split, features)
    right = tokens[:, split:] + projected(blocks, at, kept_count, first, shape)
    at += packed_rows(kept_count)[0]
    right += projected(blocks, at, kept_count, second, shape)
    out[...] = jnp.concatenate([left, right], axis=1)


def second_output_kernel(split, partial, weight, *refs):
    *blocks, out = refs
    rows, _, features = partial.shape
    blocks = [block[...].astype(jnp.float32) for block in blocks]
    tokens = partial[...]
    left = projected(blocks, 0, rows * split, weight, (rows, split, features))
    out[...] = jnp.concatenate(
        [tokens[:, :split] + left, tokens[:, split:]], axis=1
    ).astype(jnp.bfloat16)


def whole(count):
    return [pl.BlockSpec(memory_space=pltpu.VMEM)] * count


def shards(field_tokens, lon_shift, norm_gain, qkv_weight, out_weight):
    _, rows, columns, features = field_tokens.shape
    groups = lax.axis_size("tok")
    local = HEADS // groups
    width = local * HD
    span = round_up(3 * HD + 1, LANES)
    split = round_up(columns // 2, SUBLANES)
    field = field_tokens[0]
    smem = pl.BlockSpec(memory_space=pltpu.SMEM)
    kept_count, mixed_count = rows * (columns - split), rows * split

    def limit(size):
        return pltpu.CompilerParams(vmem_limit_bytes=size * MIB)

    def projection(kernel, count, parts, specs, held, params, *operands):
        block = jax.ShapeDtypeStruct((count, local * span // parts), jnp.bfloat16)
        return pl.pallas_call(
            functools.partial(kernel, split),
            out_shape=[block] * (parts * groups),
            in_specs=specs,
            out_specs=whole(parts * groups),
            scratch_shapes=[
                pltpu.VMEM((groups, count, local * span), jnp.bfloat16),
                *held,
            ],
            compiler_params=params,
            cost_estimate=pl.CostEstimate(
                flops=2 * count * features * 3 * HEADS * HD,
                bytes_accessed=2 * features * (3 * HEADS * HD + 2 * count),
                transcendentals=0,
            ),
        )(*operands)

    def spread(blocks, sign):
        arrived = list(blocks)
        for distance in sorted(range(1, groups), key=lambda step: step * (step - groups)):
            arrived[distance] = shifted(blocks[distance], "tok", sign * distance)
        return arrived

    eastern = shifted(field[:, :split], "win", -LAT_WINDOWS)
    hbm = pl.BlockSpec(memory_space=pltpu.HBM)
    operands = (field, norm_gain, qkv_weight)
    held = [
        pltpu.VMEM(qkv_weight.shape, qkv_weight.dtype),
        pltpu.SemaphoreType.DMA((3,)),
        pltpu.VMEM(field.shape, field.dtype),
        pltpu.VMEM(norm_gain.shape, norm_gain.dtype),
    ]
    kept = spread(projection(kept_kernel, kept_count, 1, [hbm] * 3, held, limit(60), *operands), 1)
    specs = [*whole(3), smem, *whole(1)]
    operands += (lon_shift, eastern)
    mixed = projection(mixed_kernel, mixed_count, local, specs, [], limit(48), *operands)
    first_mixed = spread(after(mixed[:groups], [None, *kept[1:]]), 1)
    second_mixed = spread(after(mixed[groups:], [None, *first_mixed[1:]]), 1)

    total = groups * rows * columns
    step = total // 5
    mixed_packed, kept_packed = packed_rows(mixed_count)[0], packed_rows(kept_count)[0]

    def block(count):
        return jax.ShapeDtypeStruct((count, LANES), jnp.bfloat16)

    def attention(head, *blocks):
        return pl.pallas_call(
            functools.partial(attention_kernel, head, groups),
            out_shape=[block(groups * kept_packed), block(groups * mixed_packed)],
            in_specs=whole(len(blocks)),
            out_specs=whole(2),
            scratch_shapes=[
                pltpu.VMEM((total, span), jnp.bfloat16),
                pltpu.VMEM((LANES, total), jnp.bfloat16),
                pltpu.VMEM((total, LANES), jnp.float32),
                pltpu.VMEM((step, total), jnp.float32),
                pltpu.VMEM((step, total), jnp.float32),
                pltpu.VMEM((step, total), jnp.bfloat16),
                pltpu.VMEM((step, total), jnp.bfloat16),
            ],
            compiler_params=limit(32),
            cost_estimate=pl.CostEstimate(
                flops=4 * total * total * span,
                bytes_accessed=2 * total * (span + LANES),
                transcendentals=total * total,
            ),
        )(*blocks)

    def back(mixed_values, *kept_values):
        western = shifted(mixed_values, "win", LAT_WINDOWS)
        selected = pl.pallas_call(
            functools.partial(select_kernel, split, mixed_count, groups),
            out_shape=[block(mixed_packed + len(kept_values) * kept_packed)] * groups,
            in_specs=[smem] + whole(2 + len(kept_values)),
            out_specs=whole(groups),
            compiler_params=limit(16),
            cost_estimate=pl.CostEstimate(
                flops=total * LANES * 20, bytes_accessed=8 * total * LANES, transcendentals=0
            ),
        )(lon_shift, mixed_values, western, *kept_values)
        return spread(selected, -1)

    first_kept_values, first_mixed_values = attention(0, *kept, *first_mixed)
    second_kept_values, second_mixed_values = attention(1, *kept, *second_mixed)
    first = back(first_mixed_values, first_kept_values, second_kept_values)
    second = back(second_mixed_values)

    cost = pl.CostEstimate(
        flops=2 * rows * columns * groups * LANES * features,
        bytes_accessed=features * (HEADS * HD + 6 * rows * columns),
        transcendentals=0,
    )
    ordered = (groups * LANES, features)
    partial, weight = pl.pallas_call(
        functools.partial(first_output_kernel, split, groups),
        out_shape=[
            jax.ShapeDtypeStruct(field.shape, jnp.float32),
            jax.ShapeDtypeStruct(ordered, jnp.bfloat16),
        ],
        in_specs=whole(2 + groups),
        out_specs=whole(2),
        scratch_shapes=[pltpu.VMEM(ordered, jnp.bfloat16)],
        compiler_params=limit(24),
        cost_estimate=cost,
    )(field, out_weight, *first)
    result = pl.pallas_call(
        functools.partial(second_output_kernel, split),
        out_shape=jax.ShapeDtypeStruct(field.shape, jnp.bfloat16),
        in_specs=whole(2 + groups),
        out_specs=pl.BlockSpec(memory_space=pltpu.VMEM),
        compiler_params=limit(24),
        cost_estimate=cost,
    )(partial, weight, *second)
    return result[None]


def solution(mesh):
    placed = (P("win", "tok", None, None), P(), P(), P(), P())
    return jax.shard_map(
        shards, mesh=mesh, in_specs=placed, out_specs=P("win", "tok", None, None), check_vma=False
    )
```

```python
import functools

import jax
import jax.numpy as jnp
from jax import lax
from jax.experimental import pallas as pl
from jax.experimental.pallas import tpu as pltpu
from jax.sharding import PartitionSpec as P

HEADS = 8
HD = 80
LAT_WINDOWS = 4
LANES = 128
SUBLANES = 8
MIB = 1024 * 1024
CHUNKS = 5


def round_up(value, unit):
    return -(-value // unit) * unit


def shifted(block, axis, distance):
    count = lax.axis_size(axis)
    return lax.ppermute(block, axis, [(i, (i + distance) % count) for i in range(count)])


def after(blocks, arrived):
    return [
        block if other is None else lax.optimization_barrier((block, other))[0]
        for block, other in zip(blocks, arrived)
    ]


def column_offset(lon_shift):
    return lon_shift[lax.rem(lax.axis_index("win"), LAT_WINDOWS)]


def project(tokens, gain, weight, copies, slots):
    groups = slots.shape[0]
    local = HEADS // groups
    count, features = tokens.shape
    span = slots.shape[2] // local
    factor = lax.rsqrt(jnp.mean(tokens * tokens, axis=-1, keepdims=True) + 1e-06)
    normed = (tokens * factor * gain[...].reshape(1, features)).astype(jnp.bfloat16)
    chunk = features // len(copies)
    qkv = None
    for index, copy in enumerate(copies):
        if copy is not None:
            copy.wait()
        inner = slice(index * chunk, (index + 1) * chunk)
        share = jnp.dot(normed[:, inner], weight[inner], preferred_element_type=jnp.float32)
        qkv = share if qkv is None else qkv + share
    qkv = qkv.astype(jnp.bfloat16)
    tail = jnp.ones((count, span - 3 * HD), jnp.bfloat16)
    place = lax.axis_index("tok")
    for group in range(groups):
        slot = lax.rem(group - place + groups, groups)
        columns = []
        for head in range(group * local, (group + 1) * local):
            columns += [
                qkv[:, (kind * HEADS + head) * HD : (kind * HEADS + head + 1) * HD]
                for kind in (1, 0, 2)
            ] + [tail]
        slots[slot] = jnp.concatenate(columns, axis=1)


def kept_kernel(split, field, gain, weight, *refs):
    *outs, slots, held_weight, sems, held_field, held_gain = refs
    first = pltpu.make_async_copy(field, held_field, sems.at[CHUNKS])
    second = pltpu.make_async_copy(gain, held_gain, sems.at[CHUNKS + 1])
    chunk = weight.shape[0] // CHUNKS
    copies = []
    for index in range(CHUNKS):
        inner = pl.ds(index * chunk, chunk)
        copies.append(
            pltpu.make_async_copy(weight.at[inner], held_weight.at[inner], sems.at[index])
        )
    for copy in (first, second, *copies):
        copy.start()
    first.wait()
    second.wait()
    rows, columns, features = field.shape
    tokens = held_field[...].astype(jnp.float32)[:, split:]
    tokens = tokens.reshape(rows * (columns - split), features)
    project(tokens, held_gain, held_weight, copies, slots)
    copies = [
        pltpu.make_async_copy(slots.at[index], out, sems.at[index])
        for index, out in enumerate(outs)
    ]
    for copy in copies:
        copy.start()
    for copy in copies:
        copy.wait()


def mixed_kernel(split, field, gain, weight, lon_shift, eastern, *refs):
    *outs, slots = refs
    rows, _, features = field.shape
    own = field[...].astype(jnp.float32)[:, :split]
    column = lax.broadcasted_iota(jnp.int32, own.shape, 1)
    tokens = jnp.where(column < column_offset(lon_shift), eastern[...].astype(jnp.float32), own)
    project(tokens.reshape(rows * split, features), gain, weight, [None], slots)
    groups = slots.shape[0]
    for index, out in enumerate(outs):
        first = index // groups * out.shape[1]
        out[...] = slots[index % groups, :, first : first + out.shape[1]]


def gather(head, kept, mixed, held, keys):
    span = held.shape[1]
    start = 0
    for block in kept:
        held[start : start + block.shape[0]] = block[:, head * span : (head + 1) * span]
        start += block.shape[0]
    for block in mixed:
        held[start : start + block.shape[0]] = block[...]
        start += block.shape[0]
    keys[...] = held[:, :LANES].T


def attend(held, keys, attended, scores, weights):
    span = held.shape[1]
    factor = HD ** (-0.5) * 1.4426950408889634
    step = scores[0].shape[0]
    chunk = 16
    steps = held.shape[0] // step

    def score(index, out):
        first = index * step
        queries = pltpu.roll(held[first : first + step].astype(jnp.float32), span - HD, axis=1)
        queries = queries[:, :LANES]
        lane = lax.broadcasted_iota(jnp.int32, queries.shape, 1)
        queries = jnp.where(lane < HD, queries * factor, 0.0).astype(jnp.bfloat16)
        out[...] = jnp.dot(queries, keys[...], preferred_element_type=jnp.float32)

    score(0, scores[0])
    for index in range(steps):
        if index + 1 < steps:
            score(index + 1, scores[(index + 1) % 2])
        now, out = scores[index % 2], weights[index % 2]
        for first in range(0, step, chunk):
            part = now[first : first + chunk]
            top = jnp.max(part, axis=-1, keepdims=True)
            out[first : first + chunk] = jnp.exp2(part - top).astype(jnp.bfloat16)
        values = jnp.dot(out[...], held[:, span - LANES :], preferred_element_type=jnp.float32)
        first = 2 * HD - (span - LANES)
        values = values / values[:, first + HD : first + HD + 1]
        attended[index * step : (index + 1) * step] = pltpu.roll(values, LANES - first, axis=1)


def packed_rows(count):
    part = round_up(-(-count * (HD - LANES // 2) // LANES), SUBLANES)
    return count // 2 + part, part


def pack(rows):
    count = rows.shape[0]
    half = LANES // 2
    rest = HD - half
    part = packed_rows(count)[1]
    lane = lax.broadcasted_iota(jnp.int32, (count // 2, LANES), 1)
    main = jnp.where(lane < half, rows[: count // 2], pltpu.roll(rows[count // 2 :], half, axis=1))
    lane = lax.broadcasted_iota(jnp.int32, (part, LANES), 1)
    rests = jnp.zeros((part, LANES), jnp.float32)
    for index in range(-(-count // part)):
        piece = rows[index * part : (index + 1) * part]
        if piece.shape[0] < part:
            empty = jnp.zeros((part - piece.shape[0], LANES), jnp.float32)
            piece = jnp.concatenate([piece, empty], axis=0)
        turn = (index * rest + half) % LANES
        piece = pltpu.roll(piece, turn, axis=1) if turn else piece
        rests = jnp.where(lane // rest == index, piece, rests)
    return jnp.concatenate([main, rests], axis=0)


def unpack(block, count):
    half = LANES // 2
    rest = HD - half
    part = packed_rows(count)[1]
    main, rests = block[: count // 2], block[count // 2 : count // 2 + part]
    main = jnp.concatenate([main, pltpu.roll(main, half, axis=1)], axis=0)
    pieces = []
    for index in range(-(-count // part)):
        turn = (half - index * rest) % LANES
        piece = pltpu.roll(rests, turn, axis=1) if turn else rests
        pieces.append(piece[: min(part, count - index * part)])
    lane = lax.broadcasted_iota(jnp.int32, main.shape, 1)
    return jnp.where(lane < half, main, jnp.concatenate(pieces, axis=0))


def packed_tokens(count):
    half = LANES // 2
    total, part = packed_rows(count)
    row = lax.broadcasted_iota(jnp.int32, (total, LANES), 0)
    lane = lax.broadcasted_iota(jnp.int32, (total, LANES), 1)
    main = row + jnp.where(lane < half, 0, count // 2)
    rests = row - count // 2 + lane // (HD - half) * part
    return jnp.where(row < count // 2, main, rests)


def attention_kernel(head, groups, *refs):
    kept, mixed = refs[:groups], refs[groups : 2 * groups]
    kept_out, mixed_out, held, keys, attended, *rest = refs[2 * groups :]
    gather(head, kept, mixed, held, keys)
    attend(held, keys, attended, rest[:2], rest[2:])
    start = 0
    for blocks, out in ((kept, kept_out), (mixed, mixed_out)):
        packed = []
        for block in blocks:
            packed.append(pack(attended[start : start + block.shape[0]]))
            start += block.shape[0]
        out[...] = jnp.concatenate(packed, axis=0).astype(jnp.bfloat16)


def select_kernel(split, count, groups, lon_shift, mixed, western, *refs):
    kept, outs = refs[:-groups], refs[-groups:]
    taken = lax.rem(packed_tokens(count), split) < column_offset(lon_shift)
    own, west = mixed[...].astype(jnp.float32), western[...].astype(jnp.float32)
    rests = [rest[...].astype(jnp.float32) for rest in kept]
    size = own.shape[0] // groups
    for group, out in enumerate(outs):
        rows = slice(group * size, (group + 1) * size)
        pieces = [jnp.where(taken, west[rows], own[rows])]
        for rest in rests:
            part = rest.shape[0] // groups
            pieces.append(rest[group * part : (group + 1) * part])
        out[...] = jnp.concatenate(pieces, axis=0).astype(jnp.bfloat16)


def projected(blocks, first, count, weight, shape):
    total = packed_rows(count)[0]
    columns = [unpack(block[first : first + total], count) for block in blocks]
    attended = jnp.concatenate(columns, axis=1).astype(jnp.bfloat16)
    return jnp.dot(attended, weight[...], preferred_element_type=jnp.float32).reshape(shape)


def first_output_kernel(split, groups, field, weight, *refs):
    *blocks, out, second, first = refs
    features = field.shape[2]
    for slot in range(groups):
        group = lax.rem(lax.axis_index("tok") + slot, groups)
        for head, ordered in enumerate((first, second)):
            at = pl.multiple_of((group * HEADS // groups + head) * HD, 16)
            ordered[slot * LANES : slot * LANES + HD] = weight[pl.ds(at, HD)]
            ordered[slot * LANES + HD : (slot + 1) * LANES] = jnp.zeros(
                (LANES - HD, features), jnp.bfloat16
            )
    rows, columns, _ = field.shape
    kept_count, mixed_count = rows * (columns - split), rows * split
    blocks = [block[...].astype(jnp.float32) for block in blocks]
    tokens = field[...].astype(jnp.float32)
    at = packed_rows(mixed_count)[0]
    shape = (rows, split, features)
    left = tokens[:, :split] + projected(blocks, 0, mixed_count, first, shape)
    shape = (rows, columns - split, features)
    right = tokens[:, split:] + projected(blocks, at, kept_count, first, shape)
    at += packed_rows(kept_count)[0]
    right += projected(blocks, at, kept_count, second, shape)
    out[...] = jnp.concatenate([left, right], axis=1)


def second_output_kernel(split, partial, weight, *refs):
    *blocks, out = refs
    rows, _, features = partial.shape
    blocks = [block[...].astype(jnp.float32) for block in blocks]
    tokens = partial[...]
    left = projected(blocks, 0, rows * split, weight, (rows, split, features))
    out[...] = jnp.concatenate(
        [tokens[:, :split] + left, tokens[:, split:]], axis=1
    ).astype(jnp.bfloat16)


def whole(count):
    return [pl.BlockSpec(memory_space=pltpu.VMEM)] * count


def shards(field_tokens, lon_shift, norm_gain, qkv_weight, out_weight):
    _, rows, columns, features = field_tokens.shape
    groups = lax.axis_size("tok")
    local = HEADS // groups
    width = local * HD
    span = round_up(3 * HD + 1, LANES)
    split = round_up(columns // 2, SUBLANES)
    field = field_tokens[0]
    smem = pl.BlockSpec(memory_space=pltpu.SMEM)
    kept_count, mixed_count = rows * (columns - split), rows * split

    def limit(size):
        return pltpu.CompilerParams(vmem_limit_bytes=size * MIB)

    def projection(kernel, count, parts, specs, out_specs, held, params, *operands):
        block = jax.ShapeDtypeStruct((count, local * span // parts), jnp.bfloat16)
        return pl.pallas_call(
            functools.partial(kernel, split),
            out_shape=[block] * (parts * groups),
            in_specs=specs,
            out_specs=out_specs,
            scratch_shapes=[
                pltpu.VMEM((groups, count, local * span), jnp.bfloat16),
                *held,
            ],
            compiler_params=params,
            cost_estimate=pl.CostEstimate(
                flops=2 * count * features * 3 * HEADS * HD,
                bytes_accessed=2 * features * (3 * HEADS * HD + 2 * count),
                transcendentals=0,
            ),
        )(*operands)

    def spread(blocks, sign):
        arrived = list(blocks)
        for distance in sorted(range(1, groups), key=lambda step: step * (step - groups)):
            arrived[distance] = shifted(blocks[distance], "tok", sign * distance)
        return arrived

    eastern = shifted(field[:, :split], "win", -LAT_WINDOWS)
    hbm = pl.BlockSpec(memory_space=pltpu.HBM)
    operands = (field, norm_gain, qkv_weight)
    held = [
        pltpu.VMEM(qkv_weight.shape, qkv_weight.dtype),
        pltpu.SemaphoreType.DMA((CHUNKS + 2,)),
        pltpu.VMEM(field.shape, field.dtype),
        pltpu.VMEM(norm_gain.shape, norm_gain.dtype),
    ]
    kept = projection(
        kept_kernel, kept_count, 1, [hbm] * 3, [hbm] * groups, held, limit(60), *operands
    )
    kept = spread(kept, 1)
    specs = [*whole(3), smem, *whole(1)]
    operands += (lon_shift, eastern)
    mixed = projection(
        mixed_kernel, mixed_count, local, specs, whole(local * groups), [], limit(48), *operands
    )
    first_mixed = spread(after(mixed[:groups], [None, *kept[1:]]), 1)
    second_mixed = spread(after(mixed[groups:], [None, *first_mixed[1:]]), 1)

    total = groups * rows * columns
    step = total // 5
    mixed_packed, kept_packed = packed_rows(mixed_count)[0], packed_rows(kept_count)[0]

    def block(count):
        return jax.ShapeDtypeStruct((count, LANES), jnp.bfloat16)

    def attention(head, *blocks):
        return pl.pallas_call(
            functools.partial(attention_kernel, head, groups),
            out_shape=[block(groups * kept_packed), block(groups * mixed_packed)],
            in_specs=whole(len(blocks)),
            out_specs=whole(2),
            scratch_shapes=[
                pltpu.VMEM((total, span), jnp.bfloat16),
                pltpu.VMEM((LANES, total), jnp.bfloat16),
                pltpu.VMEM((total, LANES), jnp.float32),
                pltpu.VMEM((step, total), jnp.float32),
                pltpu.VMEM((step, total), jnp.float32),
                pltpu.VMEM((step, total), jnp.bfloat16),
                pltpu.VMEM((step, total), jnp.bfloat16),
            ],
            compiler_params=limit(32),
            cost_estimate=pl.CostEstimate(
                flops=4 * total * total * span,
                bytes_accessed=2 * total * (span + LANES),
                transcendentals=total * total,
            ),
        )(*blocks)

    def back(mixed_values, *kept_values):
        western = shifted(mixed_values, "win", LAT_WINDOWS)
        selected = pl.pallas_call(
            functools.partial(select_kernel, split, mixed_count, groups),
            out_shape=[block(mixed_packed + len(kept_values) * kept_packed)] * groups,
            in_specs=[smem] + whole(2 + len(kept_values)),
            out_specs=whole(groups),
            compiler_params=limit(16),
            cost_estimate=pl.CostEstimate(
                flops=total * LANES * 20, bytes_accessed=8 * total * LANES, transcendentals=0
            ),
        )(lon_shift, mixed_values, western, *kept_values)
        return spread(selected, -1)

    first_kept_values, first_mixed_values = attention(0, *kept, *first_mixed)
    second_kept_values, second_mixed_values = attention(1, *kept, *second_mixed)
    first = back(first_mixed_values, first_kept_values, second_kept_values)
    second = back(second_mixed_values)

    cost = pl.CostEstimate(
        flops=2 * rows * columns * groups * LANES * features,
        bytes_accessed=features * (HEADS * HD + 6 * rows * columns),
        transcendentals=0,
    )
    ordered = (groups * LANES, features)
    partial, weight = pl.pallas_call(
        functools.partial(first_output_kernel, split, groups),
        out_shape=[
            jax.ShapeDtypeStruct(field.shape, jnp.float32),
            jax.ShapeDtypeStruct(ordered, jnp.bfloat16),
        ],
        in_specs=whole(2 + groups),
        out_specs=whole(2),
        scratch_shapes=[pltpu.VMEM(ordered, jnp.bfloat16)],
        compiler_params=limit(24),
        cost_estimate=cost,
    )(field, out_weight, *first)
    result = pl.pallas_call(
        functools.partial(second_output_kernel, split),
        out_shape=jax.ShapeDtypeStruct(field.shape, jnp.bfloat16),
        in_specs=whole(2 + groups),
        out_specs=pl.BlockSpec(memory_space=pltpu.VMEM),
        compiler_params=limit(24),
        cost_estimate=cost,
    )(partial, weight, *second)
    return result[None]


def solution(mesh):
    placed = (P("win", "tok", None, None), P(), P(), P(), P())
    return jax.shard_map(
        shards, mesh=mesh, in_specs=placed, out_specs=P("win", "tok", None, None), check_vma=False
    )
```

```python
import functools

import jax
import jax.numpy as jnp
from jax import lax
from jax.experimental import pallas as pl
from jax.experimental.pallas import tpu as pltpu
from jax.sharding import PartitionSpec as P

HEADS = 8
HD = 80
LAT_WINDOWS = 4
LANES = 128
SUBLANES = 8
MIB = 1024 * 1024
CHUNKS = 5
MAX_STEP = 320


def round_up(value, unit):
    return -(-value // unit) * unit


def shifted(block, axis, distance):
    count = lax.axis_size(axis)
    return lax.ppermute(block, axis, [(i, (i + distance) % count) for i in range(count)])


def after(blocks, arrived):
    return [
        block if other is None else lax.optimization_barrier((block, other))[0]
        for block, other in zip(blocks, arrived)
    ]


def column_offset(lon_shift):
    return lon_shift[lax.rem(lax.axis_index("win"), LAT_WINDOWS)]


def project(tokens, gain, weight, copies, slots):
    groups = slots.shape[0]
    local = HEADS // groups
    count, features = tokens.shape
    span = slots.shape[2] // local
    factor = lax.rsqrt(jnp.mean(tokens * tokens, axis=-1, keepdims=True) + 1e-06)
    normed = (tokens * factor * gain[...].reshape(1, features)).astype(jnp.bfloat16)
    chunk = features // len(copies)
    qkv = None
    for index, copy in enumerate(copies):
        if copy is not None:
            copy.wait()
        inner = slice(index * chunk, (index + 1) * chunk)
        share = jnp.dot(normed[:, inner], weight[inner], preferred_element_type=jnp.float32)
        qkv = share if qkv is None else qkv + share
    qkv = qkv.astype(jnp.bfloat16)
    tail = jnp.ones((count, span - 3 * HD), jnp.bfloat16)
    place = lax.axis_index("tok")
    for group in range(groups):
        slot = lax.rem(group - place + groups, groups)
        columns = []
        for head in range(group * local, (group + 1) * local):
            columns += [
                qkv[:, (kind * HEADS + head) * HD : (kind * HEADS + head + 1) * HD]
                for kind in (1, 0, 2)
            ] + [tail]
        slots[slot] = jnp.concatenate(columns, axis=1)


def kept_kernel(split, field, gain, weight, *refs):
    *outs, slots, held_weight, sems, held_field, held_gain = refs
    first = pltpu.make_async_copy(field, held_field, sems.at[CHUNKS])
    second = pltpu.make_async_copy(gain, held_gain, sems.at[CHUNKS + 1])
    chunk = weight.shape[0] // CHUNKS
    copies = []
    for index in range(CHUNKS):
        inner = pl.ds(index * chunk, chunk)
        copies.append(
            pltpu.make_async_copy(weight.at[inner], held_weight.at[inner], sems.at[index])
        )
    for copy in (first, second, *copies):
        copy.start()
    first.wait()
    second.wait()
    rows, columns, features = field.shape
    tokens = held_field[...].astype(jnp.float32)[:, split:]
    tokens = tokens.reshape(rows * (columns - split), features)
    project(tokens, held_gain, held_weight, copies, slots)
    copies = [
        pltpu.make_async_copy(slots.at[index], out, sems.at[index])
        for index, out in enumerate(outs)
    ]
    for copy in copies:
        copy.start()
    for copy in copies:
        copy.wait()


def mixed_kernel(split, field, gain, weight, lon_shift, eastern, *refs):
    *outs, slots = refs
    rows, _, features = field.shape
    own = field[...].astype(jnp.float32)[:, :split]
    column = lax.broadcasted_iota(jnp.int32, own.shape, 1)
    tokens = jnp.where(column < column_offset(lon_shift), eastern[...].astype(jnp.float32), own)
    project(tokens.reshape(rows * split, features), gain, weight, [None], slots)
    groups = slots.shape[0]
    for index, out in enumerate(outs):
        first = index // groups * out.shape[1]
        out[...] = slots[index % groups, :, first : first + out.shape[1]]


FACTOR = HD ** (-0.5) * 1.4426950408889634
CHUNK = 16


def step_of(count):
    return max(step for step in range(CHUNK, MAX_STEP + 1, CHUNK) if count % step == 0)


def gather(head, kept, mixed, held, keys):
    span = held.shape[1]
    start = 0
    for block in kept:
        held[start : start + block.shape[0]] = block[:, head * span : (head + 1) * span]
        start += block.shape[0]
    for block in mixed:
        held[start : start + block.shape[0]] = block[...]
        start += block.shape[0]
    keys[...] = held[:, :LANES].T


def queries_of(held, first, count):
    queries = pltpu.roll(held[first : first + count].astype(jnp.float32), held.shape[1] - HD, axis=1)
    queries = queries[:, :LANES]
    lane = lax.broadcasted_iota(jnp.int32, queries.shape, 1)
    return jnp.where(lane < HD, queries, 0.0).astype(jnp.bfloat16)


def scaled(values, span):
    first = 2 * HD - (span - LANES)
    values = values / values[:, first + HD : first + HD + 1]
    return pltpu.roll(values, LANES - first, axis=1)


def attend(queries, sources, scores, weights, finish):
    count = queries.shape[0]
    step = step_of(count)
    span = queries.shape[1]

    def score(index):
        block = queries_of(queries, index * step, step)
        start = 0
        for _, keys in sources:
            columns = slice(start, start + keys.shape[1])
            scores[index % 2][:step, columns] = jnp.dot(
                block, keys[...], preferred_element_type=jnp.float32
            )
            start += round_up(keys.shape[1], LANES)

    score(0)
    for index in range(count // step):
        if (index + 1) * step < count:
            score(index + 1)
        now, out = scores[index % 2], weights[index % 2]
        spots, start = [], 0
        for held, keys in sources:
            spots.append((held, slice(start, start + keys.shape[1])))
            start += round_up(keys.shape[1], LANES)
        finish(index * step, step, now, out, spots)


def top_of(now, rows, spots):
    tops = [jnp.max(now[rows, columns], axis=-1, keepdims=True) for _, columns in spots]
    return functools.reduce(jnp.maximum, tops)


def weigh(now, out, rows, spots, top):
    for _, columns in spots:
        out[rows, columns] = jnp.exp2((now[rows, columns] - top) * FACTOR).astype(jnp.bfloat16)


def summed(out, step, spots):
    shares = [
        jnp.dot(
            out[:step, columns],
            held[:, held.shape[1] - LANES :],
            preferred_element_type=jnp.float32,
        )
        for held, columns in spots
    ]
    return functools.reduce(jnp.add, shares)


def chunks(step):
    return [slice(first, first + CHUNK) for first in range(0, step, CHUNK)]


def finish_whole(attended, base, span):
    def finish(first, step, now, out, spots):
        for rows in chunks(step):
            weigh(now, out, rows, spots, top_of(now, rows, spots))
        attended[base + first : base + first + step] = scaled(summed(out, step, spots), span)

    return finish


def finish_early(sums, tops):
    def finish(first, step, now, out, spots):
        for rows in chunks(step):
            top = top_of(now, rows, spots)
            weigh(now, out, rows, spots, top)
            tops[first + rows.start : first + rows.stop] = jnp.broadcast_to(top, (CHUNK, LANES))
        sums[first : first + step] = summed(out, step, spots)

    return finish


def finish_late(attended, sums, tops, span):
    def finish(first, step, now, out, spots):
        shrinks = []
        for rows in chunks(step):
            before = tops[first + rows.start : first + rows.stop]
            top = jnp.maximum(top_of(now, rows, spots), before[:, :1])
            weigh(now, out, rows, spots, top)
            shrinks.append(jnp.exp2((before - top) * FACTOR))
        shrink = jnp.concatenate(shrinks, axis=0)
        values = summed(out, step, spots) + sums[first : first + step] * shrink
        attended[first : first + step] = scaled(values, span)

    return finish


def packed_rows(count):
    part = round_up(-(-count * (HD - LANES // 2) // LANES), SUBLANES)
    return count // 2 + part, part


def pack(rows):
    count = rows.shape[0]
    half = LANES // 2
    rest = HD - half
    part = packed_rows(count)[1]
    lane = lax.broadcasted_iota(jnp.int32, (count // 2, LANES), 1)
    main = jnp.where(lane < half, rows[: count // 2], pltpu.roll(rows[count // 2 :], half, axis=1))
    lane = lax.broadcasted_iota(jnp.int32, (part, LANES), 1)
    rests = jnp.zeros((part, LANES), jnp.float32)
    for index in range(-(-count // part)):
        piece = rows[index * part : (index + 1) * part]
        if piece.shape[0] < part:
            empty = jnp.zeros((part - piece.shape[0], LANES), jnp.float32)
            piece = jnp.concatenate([piece, empty], axis=0)
        turn = (index * rest + half) % LANES
        piece = pltpu.roll(piece, turn, axis=1) if turn else piece
        rests = jnp.where(lane // rest == index, piece, rests)
    return jnp.concatenate([main, rests], axis=0)


def unpack(block, count):
    half = LANES // 2
    rest = HD - half
    part = packed_rows(count)[1]
    main, rests = block[: count // 2], block[count // 2 : count // 2 + part]
    main = jnp.concatenate([main, pltpu.roll(main, half, axis=1)], axis=0)
    pieces = []
    for index in range(-(-count // part)):
        turn = (half - index * rest) % LANES
        piece = pltpu.roll(rests, turn, axis=1) if turn else rests
        pieces.append(piece[: min(part, count - index * part)])
    lane = lax.broadcasted_iota(jnp.int32, main.shape, 1)
    return jnp.where(lane < half, main, jnp.concatenate(pieces, axis=0))


def packed_tokens(count):
    half = LANES // 2
    total, part = packed_rows(count)
    row = lax.broadcasted_iota(jnp.int32, (total, LANES), 0)
    lane = lax.broadcasted_iota(jnp.int32, (total, LANES), 1)
    main = row + jnp.where(lane < half, 0, count // 2)
    rests = row - count // 2 + lane // (HD - half) * part
    return jnp.where(row < count // 2, main, rests)


def pack_all(attended, kept_count, mixed_count, kept_out, mixed_out):
    start = 0
    for count, out in ((kept_count, kept_out), (mixed_count, mixed_out)):
        size = packed_rows(count)[0]
        packed = []
        for _ in range(out.shape[0] // size):
            packed.append(pack(attended[start : start + count]))
            start += count
        out[...] = jnp.concatenate(packed, axis=0).astype(jnp.bfloat16)


def first_head_kernel(groups, *refs):
    kept, mixed = refs[:groups], refs[groups : 2 * groups]
    kept_out, mixed_out, held, keys, attended, *rest = refs[2 * groups :]
    gather(0, kept, mixed, held, keys)
    finish = finish_whole(attended, 0, held.shape[1])
    attend(held, [(held, keys)], rest[:2], rest[2:], finish)
    pack_all(attended, kept[0].shape[0], mixed[0].shape[0], kept_out, mixed_out)


def early_kernel(groups, early, *refs):
    kept, mixed = refs[:groups], refs[groups : groups + early]
    sums, tops, held, keys, *rest = refs[groups + early :]
    gather(1, kept, mixed, held, keys)
    attend(held, [(held, keys)], rest[:2], rest[2:], finish_early(sums, tops))


def late_kernel(kept_count, sums, tops, early_held, early_keys, *refs):
    *mixed, kept_out, mixed_out, held, keys, attended, s0, s1, w0, w1 = refs
    gather(1, [], mixed, held, keys)
    span = held.shape[1]
    early = early_held.shape[0]
    attend(
        early_held, [(held, keys)], (s0, s1), (w0, w1), finish_late(attended, sums, tops, span)
    )
    both = [(early_held, early_keys), (held, keys)]
    attend(held, both, (s0, s1), (w0, w1), finish_whole(attended, early, span))
    pack_all(attended, kept_count, mixed[0].shape[0], kept_out, mixed_out)


def select_kernel(split, count, groups, lon_shift, mixed, western, *refs):
    kept, outs = refs[:-groups], refs[-groups:]
    taken = lax.rem(packed_tokens(count), split) < column_offset(lon_shift)
    own, west = mixed[...].astype(jnp.float32), western[...].astype(jnp.float32)
    rests = [rest[...].astype(jnp.float32) for rest in kept]
    size = own.shape[0] // groups
    for group, out in enumerate(outs):
        rows = slice(group * size, (group + 1) * size)
        pieces = [jnp.where(taken, west[rows], own[rows])]
        for rest in rests:
            part = rest.shape[0] // groups
            pieces.append(rest[group * part : (group + 1) * part])
        out[...] = jnp.concatenate(pieces, axis=0).astype(jnp.bfloat16)


def projected(blocks, first, count, weight, shape):
    total = packed_rows(count)[0]
    columns = [unpack(block[first : first + total], count) for block in blocks]
    attended = jnp.concatenate(columns, axis=1).astype(jnp.bfloat16)
    return jnp.dot(attended, weight[...], preferred_element_type=jnp.float32).reshape(shape)


def first_output_kernel(split, groups, field, weight, *refs):
    *blocks, out, second, first = refs
    features = field.shape[2]
    for slot in range(groups):
        group = lax.rem(lax.axis_index("tok") + slot, groups)
        for head, ordered in enumerate((first, second)):
            at = pl.multiple_of((group * HEADS // groups + head) * HD, 16)
            ordered[slot * LANES : slot * LANES + HD] = weight[pl.ds(at, HD)]
            ordered[slot * LANES + HD : (slot + 1) * LANES] = jnp.zeros(
                (LANES - HD, features), jnp.bfloat16
            )
    rows, columns, _ = field.shape
    kept_count, mixed_count = rows * (columns - split), rows * split
    blocks = [block[...].astype(jnp.float32) for block in blocks]
    tokens = field[...].astype(jnp.float32)
    at = packed_rows(mixed_count)[0]
    shape = (rows, split, features)
    left = tokens[:, :split] + projected(blocks, 0, mixed_count, first, shape)
    shape = (rows, columns - split, features)
    right = tokens[:, split:] + projected(blocks, at, kept_count, first, shape)
    at += packed_rows(kept_count)[0]
    right += projected(blocks, at, kept_count, second, shape)
    out[...] = jnp.concatenate([left, right], axis=1)


def second_output_kernel(split, partial, weight, *refs):
    *blocks, out = refs
    rows, _, features = partial.shape
    blocks = [block[...].astype(jnp.float32) for block in blocks]
    tokens = partial[...]
    left = projected(blocks, 0, rows * split, weight, (rows, split, features))
    out[...] = jnp.concatenate(
        [tokens[:, :split] + left, tokens[:, split:]], axis=1
    ).astype(jnp.bfloat16)


def whole(count):
    return [pl.BlockSpec(memory_space=pltpu.VMEM)] * count


def shards(field_tokens, lon_shift, norm_gain, qkv_weight, out_weight):
    _, rows, columns, features = field_tokens.shape
    groups = lax.axis_size("tok")
    local = HEADS // groups
    width = local * HD
    span = round_up(3 * HD + 1, LANES)
    split = round_up(columns // 2, SUBLANES)
    field = field_tokens[0]
    smem = pl.BlockSpec(memory_space=pltpu.SMEM)
    kept_count, mixed_count = rows * (columns - split), rows * split

    def limit(size):
        return pltpu.CompilerParams(vmem_limit_bytes=size * MIB)

    def projection(kernel, count, parts, specs, out_specs, held, params, *operands):
        block = jax.ShapeDtypeStruct((count, local * span // parts), jnp.bfloat16)
        return pl.pallas_call(
            functools.partial(kernel, split),
            out_shape=[block] * (parts * groups),
            in_specs=specs,
            out_specs=out_specs,
            scratch_shapes=[
                pltpu.VMEM((groups, count, local * span), jnp.bfloat16),
                *held,
            ],
            compiler_params=params,
            cost_estimate=pl.CostEstimate(
                flops=2 * count * features * 3 * HEADS * HD,
                bytes_accessed=2 * features * (3 * HEADS * HD + 2 * count),
                transcendentals=0,
            ),
        )(*operands)

    def spread(blocks, sign):
        arrived = list(blocks)
        for distance in sorted(range(1, groups), key=lambda step: step * (step - groups)):
            arrived[distance] = shifted(blocks[distance], "tok", sign * distance)
        return arrived

    eastern = shifted(field[:, :split], "win", -LAT_WINDOWS)
    hbm = pl.BlockSpec(memory_space=pltpu.HBM)
    operands = (field, norm_gain, qkv_weight)
    held = [
        pltpu.VMEM(qkv_weight.shape, qkv_weight.dtype),
        pltpu.SemaphoreType.DMA((CHUNKS + 2,)),
        pltpu.VMEM(field.shape, field.dtype),
        pltpu.VMEM(norm_gain.shape, norm_gain.dtype),
    ]
    kept = projection(
        kept_kernel, kept_count, 1, [hbm] * 3, [hbm] * groups, held, limit(60), *operands
    )
    kept = spread(kept, 1)
    specs = [*whole(3), smem, *whole(1)]
    operands += (lon_shift, eastern)
    mixed = projection(
        mixed_kernel, mixed_count, local, specs, whole(local * groups), [], limit(48), *operands
    )
    first_mixed = spread(after(mixed[:groups], [None, *kept[1:]]), 1)
    second_mixed = spread(after(mixed[groups:], [None, *first_mixed[1:]]), 1)

    total = groups * rows * columns
    ahead = max(groups // 2, 1)
    early = groups * kept_count + ahead * mixed_count
    mixed_packed, kept_packed = packed_rows(mixed_count)[0], packed_rows(kept_count)[0]

    def block(count):
        return jax.ShapeDtypeStruct((count, LANES), jnp.bfloat16)

    def rows_of(count, lanes, dtype):
        return jax.ShapeDtypeStruct((count, lanes), dtype)

    def gathered(count):
        return [rows_of(count, span, jnp.bfloat16), rows_of(LANES, count, jnp.bfloat16)]

    def attention(kernel, out_shape, held, scores, pairs, *blocks):
        scratch = [pltpu.VMEM(leaf.shape, leaf.dtype) for leaf in held]
        scratch += [pltpu.VMEM(scores, jnp.float32)] * 2 + [pltpu.VMEM(scores, jnp.bfloat16)] * 2
        return pl.pallas_call(
            kernel,
            out_shape=out_shape,
            in_specs=whole(len(blocks)),
            out_specs=whole(len(out_shape)),
            scratch_shapes=scratch,
            compiler_params=limit(32),
            cost_estimate=pl.CostEstimate(
                flops=4 * pairs * span,
                bytes_accessed=2 * total * (span + LANES),
                transcendentals=pairs,
            ),
        )(*blocks)

    values = [block(groups * kept_packed), block(groups * mixed_packed)]
    attended = rows_of(total, LANES, jnp.float32)
    wide = round_up(early, LANES) + round_up(total - early, LANES)
    first_kept_values, first_mixed_values = attention(
        functools.partial(first_head_kernel, groups),
        values,
        [*gathered(total), attended],
        (MAX_STEP, total),
        total * total,
        *kept,
        *first_mixed,
    )
    partial = attention(
        functools.partial(early_kernel, groups, ahead),
        [rows_of(early, LANES, jnp.float32)] * 2 + gathered(early),
        [],
        (MAX_STEP, early),
        early * early,
        *kept,
        *second_mixed[:ahead],
    )
    second_kept_values, second_mixed_values = attention(
        functools.partial(late_kernel, kept_count),
        values,
        [*gathered(total - early), attended],
        (MAX_STEP, wide),
        total * total - early * early,
        *partial,
        *second_mixed[ahead:],
    )
    def back(mixed_values, *kept_values):
        western = shifted(mixed_values, "win", LAT_WINDOWS)
        selected = pl.pallas_call(
            functools.partial(select_kernel, split, mixed_count, groups),
            out_shape=[block(mixed_packed + len(kept_values) * kept_packed)] * groups,
            in_specs=[smem] + whole(2 + len(kept_values)),
            out_specs=whole(groups),
            compiler_params=limit(16),
            cost_estimate=pl.CostEstimate(
                flops=total * LANES * 20, bytes_accessed=8 * total * LANES, transcendentals=0
            ),
        )(lon_shift, mixed_values, western, *kept_values)
        return spread(selected, -1)

    first = back(first_mixed_values, first_kept_values, second_kept_values)
    second = back(second_mixed_values)

    cost = pl.CostEstimate(
        flops=2 * rows * columns * groups * LANES * features,
        bytes_accessed=features * (HEADS * HD + 6 * rows * columns),
        transcendentals=0,
    )
    ordered = (groups * LANES, features)
    partial, weight = pl.pallas_call(
        functools.partial(first_output_kernel, split, groups),
        out_shape=[
            jax.ShapeDtypeStruct(field.shape, jnp.float32),
            jax.ShapeDtypeStruct(ordered, jnp.bfloat16),
        ],
        in_specs=whole(2 + groups),
        out_specs=whole(2),
        scratch_shapes=[pltpu.VMEM(ordered, jnp.bfloat16)],
        compiler_params=limit(24),
        cost_estimate=cost,
    )(field, out_weight, *first)
    result = pl.pallas_call(
        functools.partial(second_output_kernel, split),
        out_shape=jax.ShapeDtypeStruct(field.shape, jnp.bfloat16),
        in_specs=whole(2 + groups),
        out_specs=pl.BlockSpec(memory_space=pltpu.VMEM),
        compiler_params=limit(24),
        cost_estimate=cost,
    )(partial, weight, *second)
    return result[None]


def solution(mesh):
    placed = (P("win", "tok", None, None), P(), P(), P(), P())
    return jax.shard_map(
        shards, mesh=mesh, in_specs=placed, out_specs=P("win", "tok", None, None), check_vma=False
    )
```

```python
import functools

import jax
import jax.numpy as jnp
from jax import lax
from jax.experimental import pallas as pl
from jax.experimental.pallas import tpu as pltpu
from jax.sharding import PartitionSpec as P

HEADS = 8
HD = 80
LAT_WINDOWS = 4
LANES = 128
SUBLANES = 8
MIB = 1024 * 1024
CHUNKS = 5
COPIES = 4


def round_up(value, unit):
    return -(-value // unit) * unit


def shifted(block, axis, distance):
    count = lax.axis_size(axis)
    return lax.ppermute(block, axis, [(i, (i + distance) % count) for i in range(count)])


def after(blocks, arrived):
    return [
        block if other is None else lax.optimization_barrier((block, other))[0]
        for block, other in zip(blocks, arrived)
    ]


def column_offset(lon_shift):
    return lon_shift[lax.rem(lax.axis_index("win"), LAT_WINDOWS)]


def project(tokens, gain, weight, copies, slots):
    groups = slots.shape[0]
    local = HEADS // groups
    count, features = tokens.shape
    span = slots.shape[2] // local
    factor = lax.rsqrt(jnp.mean(tokens * tokens, axis=-1, keepdims=True) + 1e-06)
    normed = (tokens * factor * gain[...].reshape(1, features)).astype(jnp.bfloat16)
    chunk = features // len(copies)
    qkv = None
    for index, copy in enumerate(copies):
        for piece in copy:
            piece.wait()
        inner = slice(index * chunk, (index + 1) * chunk)
        share = jnp.dot(normed[:, inner], weight[inner], preferred_element_type=jnp.float32)
        qkv = share if qkv is None else qkv + share
    qkv = qkv.astype(jnp.bfloat16)
    tail = jnp.ones((count, span - 3 * HD), jnp.bfloat16)
    place = lax.axis_index("tok")
    for group in range(groups):
        slot = lax.rem(group - place + groups, groups)
        columns = []
        for head in range(group * local, (group + 1) * local):
            columns += [
                qkv[:, (kind * HEADS + head) * HD : (kind * HEADS + head + 1) * HD]
                for kind in (1, 0, 2)
            ] + [tail]
        slots[slot] = jnp.concatenate(columns, axis=1)


def kept_kernel(split, field, gain, weight, *refs):
    *outs, slots, held_weight, sems, held_field, held_gain = refs
    total = CHUNKS * COPIES
    first = pltpu.make_async_copy(field, held_field, sems.at[total])
    second = pltpu.make_async_copy(gain, held_gain, sems.at[total + 1])
    chunk = weight.shape[0] // total
    pieces = []
    for index in range(total):
        inner = pl.ds(index * chunk, chunk)
        pieces.append(
            pltpu.make_async_copy(weight.at[inner], held_weight.at[inner], sems.at[index])
        )
    for copy in (first, second, *pieces):
        copy.start()
    copies = [pieces[index : index + COPIES] for index in range(0, total, COPIES)]
    first.wait()
    second.wait()
    rows, columns, features = field.shape
    tokens = held_field[...].astype(jnp.float32)[:, split:]
    tokens = tokens.reshape(rows * (columns - split), features)
    project(tokens, held_gain, held_weight, copies, slots)
    copies = [
        pltpu.make_async_copy(slots.at[index], out, sems.at[index])
        for index, out in enumerate(outs)
    ]
    for copy in copies:
        copy.start()
    for copy in copies:
        copy.wait()


def mixed_kernel(split, field, gain, weight, lon_shift, eastern, *refs):
    *outs, slots = refs
    rows, _, features = field.shape
    own = field[...].astype(jnp.float32)[:, :split]
    column = lax.broadcasted_iota(jnp.int32, own.shape, 1)
    tokens = jnp.where(column < column_offset(lon_shift), eastern[...].astype(jnp.float32), own)
    project(tokens.reshape(rows * split, features), gain, weight, [[]], slots)
    groups = slots.shape[0]
    for index, out in enumerate(outs):
        first = index // groups * out.shape[1]
        out[...] = slots[index % groups, :, first : first + out.shape[1]]


def gather(head, kept, mixed, held, keys):
    span = held.shape[1]
    start = 0
    for block in kept:
        held[start : start + block.shape[0]] = block[:, head * span : (head + 1) * span]
        start += block.shape[0]
    for block in mixed:
        held[start : start + block.shape[0]] = block[...]
        start += block.shape[0]
    keys[...] = held[:, :LANES].T


def attend(held, keys, attended, scores, weights):
    span = held.shape[1]
    factor = HD ** (-0.5) * 1.4426950408889634
    step = scores[0].shape[0]
    chunk = 16
    steps = held.shape[0] // step

    def score(index, out):
        first = index * step
        queries = pltpu.roll(held[first : first + step].astype(jnp.float32), span - HD, axis=1)
        queries = queries[:, :LANES]
        lane = lax.broadcasted_iota(jnp.int32, queries.shape, 1)
        queries = jnp.where(lane < HD, queries, 0.0).astype(jnp.bfloat16)
        out[...] = jnp.dot(queries, keys[...], preferred_element_type=jnp.float32)

    score(0, scores[0])
    for index in range(steps):
        if index + 1 < steps:
            score(index + 1, scores[(index + 1) % 2])
        now, out = scores[index % 2], weights[index % 2]
        for first in range(0, step, chunk):
            part = now[first : first + chunk]
            top = jnp.max(part, axis=-1, keepdims=True)
            out[first : first + chunk] = jnp.exp2((part - top) * factor).astype(jnp.bfloat16)
        values = jnp.dot(out[...], held[:, span - LANES :], preferred_element_type=jnp.float32)
        first = 2 * HD - (span - LANES)
        values = values / values[:, first + HD : first + HD + 1]
        attended[index * step : (index + 1) * step] = pltpu.roll(values, LANES - first, axis=1)


def packed_rows(count):
    part = round_up(-(-count * (HD - LANES // 2) // LANES), SUBLANES)
    return count // 2 + part, part


def pack(rows):
    count = rows.shape[0]
    half = LANES // 2
    rest = HD - half
    part = packed_rows(count)[1]
    lane = lax.broadcasted_iota(jnp.int32, (count // 2, LANES), 1)
    main = jnp.where(lane < half, rows[: count // 2], pltpu.roll(rows[count // 2 :], half, axis=1))
    lane = lax.broadcasted_iota(jnp.int32, (part, LANES), 1)
    rests = jnp.zeros((part, LANES), jnp.float32)
    for index in range(-(-count // part)):
        piece = rows[index * part : (index + 1) * part]
        if piece.shape[0] < part:
            empty = jnp.zeros((part - piece.shape[0], LANES), jnp.float32)
            piece = jnp.concatenate([piece, empty], axis=0)
        turn = (index * rest + half) % LANES
        piece = pltpu.roll(piece, turn, axis=1) if turn else piece
        rests = jnp.where(lane // rest == index, piece, rests)
    return jnp.concatenate([main, rests], axis=0)


def unpack(block, count):
    half = LANES // 2
    rest = HD - half
    part = packed_rows(count)[1]
    main, rests = block[: count // 2], block[count // 2 : count // 2 + part]
    main = jnp.concatenate([main, pltpu.roll(main, half, axis=1)], axis=0)
    pieces = []
    for index in range(-(-count // part)):
        turn = (half - index * rest) % LANES
        piece = pltpu.roll(rests, turn, axis=1) if turn else rests
        pieces.append(piece[: min(part, count - index * part)])
    lane = lax.broadcasted_iota(jnp.int32, main.shape, 1)
    return jnp.where(lane < half, main, jnp.concatenate(pieces, axis=0))


def packed_tokens(count):
    half = LANES // 2
    total, part = packed_rows(count)
    row = lax.broadcasted_iota(jnp.int32, (total, LANES), 0)
    lane = lax.broadcasted_iota(jnp.int32, (total, LANES), 1)
    main = row + jnp.where(lane < half, 0, count // 2)
    rests = row - count // 2 + lane // (HD - half) * part
    return jnp.where(row < count // 2, main, rests)


def attention_kernel(head, groups, *refs):
    kept, mixed = refs[:groups], refs[groups : 2 * groups]
    kept_out, mixed_out, held, keys, attended, *rest = refs[2 * groups :]
    gather(head, kept, mixed, held, keys)
    attend(held, keys, attended, rest[:2], rest[2:])
    start = 0
    for blocks, out in ((kept, kept_out), (mixed, mixed_out)):
        packed = []
        for block in blocks:
            packed.append(pack(attended[start : start + block.shape[0]]))
            start += block.shape[0]
        out[...] = jnp.concatenate(packed, axis=0).astype(jnp.bfloat16)


def select_kernel(split, count, groups, lon_shift, mixed, western, *refs):
    kept, outs = refs[:-groups], refs[-groups:]
    taken = lax.rem(packed_tokens(count), split) < column_offset(lon_shift)
    own, west = mixed[...].astype(jnp.float32), western[...].astype(jnp.float32)
    rests = [rest[...].astype(jnp.float32) for rest in kept]
    size = own.shape[0] // groups
    for group, out in enumerate(outs):
        rows = slice(group * size, (group + 1) * size)
        pieces = [jnp.where(taken, west[rows], own[rows])]
        for rest in rests:
            part = rest.shape[0] // groups
            pieces.append(rest[group * part : (group + 1) * part])
        out[...] = jnp.concatenate(pieces, axis=0).astype(jnp.bfloat16)


def projected(blocks, first, count, weight, shape):
    total = packed_rows(count)[0]
    columns = [unpack(block[first : first + total], count) for block in blocks]
    attended = jnp.concatenate(columns, axis=1).astype(jnp.bfloat16)
    return jnp.dot(attended, weight[...], preferred_element_type=jnp.float32).reshape(shape)


def first_output_kernel(split, groups, field, weight, *refs):
    *blocks, out, second, first = refs
    features = field.shape[2]
    for slot in range(groups):
        group = lax.rem(lax.axis_index("tok") + slot, groups)
        for head, ordered in enumerate((first, second)):
            at = pl.multiple_of((group * HEADS // groups + head) * HD, 16)
            ordered[slot * LANES : slot * LANES + HD] = weight[pl.ds(at, HD)]
            ordered[slot * LANES + HD : (slot + 1) * LANES] = jnp.zeros(
                (LANES - HD, features), jnp.bfloat16
            )
    rows, columns, _ = field.shape
    kept_count, mixed_count = rows * (columns - split), rows * split
    blocks = [block[...].astype(jnp.float32) for block in blocks]
    tokens = field[...].astype(jnp.float32)
    at = packed_rows(mixed_count)[0]
    shape = (rows, split, features)
    left = tokens[:, :split] + projected(blocks, 0, mixed_count, first, shape)
    shape = (rows, columns - split, features)
    right = tokens[:, split:] + projected(blocks, at, kept_count, first, shape)
    at += packed_rows(kept_count)[0]
    right += projected(blocks, at, kept_count, second, shape)
    out[...] = jnp.concatenate([left, right], axis=1)


def second_output_kernel(split, partial, weight, *refs):
    *blocks, out = refs
    rows, _, features = partial.shape
    blocks = [block[...].astype(jnp.float32) for block in blocks]
    tokens = partial[...]
    left = projected(blocks, 0, rows * split, weight, (rows, split, features))
    out[...] = jnp.concatenate(
        [tokens[:, :split] + left, tokens[:, split:]], axis=1
    ).astype(jnp.bfloat16)


def whole(count):
    return [pl.BlockSpec(memory_space=pltpu.VMEM)] * count


def shards(field_tokens, lon_shift, norm_gain, qkv_weight, out_weight):
    _, rows, columns, features = field_tokens.shape
    groups = lax.axis_size("tok")
    local = HEADS // groups
    width = local * HD
    span = round_up(3 * HD + 1, LANES)
    split = round_up(columns // 2, SUBLANES)
    field = field_tokens[0]
    smem = pl.BlockSpec(memory_space=pltpu.SMEM)
    kept_count, mixed_count = rows * (columns - split), rows * split

    def limit(size):
        return pltpu.CompilerParams(vmem_limit_bytes=size * MIB)

    def projection(kernel, count, parts, specs, out_specs, held, params, *operands):
        block = jax.ShapeDtypeStruct((count, local * span // parts), jnp.bfloat16)
        return pl.pallas_call(
            functools.partial(kernel, split),
            out_shape=[block] * (parts * groups),
            in_specs=specs,
            out_specs=out_specs,
            scratch_shapes=[
                pltpu.VMEM((groups, count, local * span), jnp.bfloat16),
                *held,
            ],
            compiler_params=params,
            cost_estimate=pl.CostEstimate(
                flops=2 * count * features * 3 * HEADS * HD,
                bytes_accessed=2 * features * (3 * HEADS * HD + 2 * count),
                transcendentals=0,
            ),
        )(*operands)

    def spread(blocks, sign):
        arrived = list(blocks)
        for distance in sorted(range(1, groups), key=lambda step: step * (step - groups)):
            arrived[distance] = shifted(blocks[distance], "tok", sign * distance)
        return arrived

    eastern = shifted(field[:, :split], "win", -LAT_WINDOWS)
    hbm = pl.BlockSpec(memory_space=pltpu.HBM)
    operands = (field, norm_gain, qkv_weight)
    held = [
        pltpu.VMEM(qkv_weight.shape, qkv_weight.dtype),
        pltpu.SemaphoreType.DMA((CHUNKS * COPIES + 2,)),
        pltpu.VMEM(field.shape, field.dtype),
        pltpu.VMEM(norm_gain.shape, norm_gain.dtype),
    ]
    kept = projection(
        kept_kernel, kept_count, 1, [hbm] * 3, [hbm] * groups, held, limit(60), *operands
    )
    kept = spread(kept, 1)
    specs = [*whole(3), smem, *whole(1)]
    operands += (lon_shift, eastern)
    mixed = projection(
        mixed_kernel, mixed_count, local, specs, whole(local * groups), [], limit(48), *operands
    )
    first_mixed = spread(after(mixed[:groups], [None, *kept[1:]]), 1)
    second_mixed = spread(after(mixed[groups:], [None, *first_mixed[1:]]), 1)

    total = groups * rows * columns
    mixed_packed, kept_packed = packed_rows(mixed_count)[0], packed_rows(kept_count)[0]

    def block(count):
        return jax.ShapeDtypeStruct((count, LANES), jnp.bfloat16)

    def attention(head, step, *blocks):
        return pl.pallas_call(
            functools.partial(attention_kernel, head, groups),
            out_shape=[block(groups * kept_packed), block(groups * mixed_packed)],
            in_specs=whole(len(blocks)),
            out_specs=whole(2),
            scratch_shapes=[
                pltpu.VMEM((total, span), jnp.bfloat16),
                pltpu.VMEM((LANES, total), jnp.bfloat16),
                pltpu.VMEM((total, LANES), jnp.float32),
                pltpu.VMEM((step, total), jnp.float32),
                pltpu.VMEM((step, total), jnp.float32),
                pltpu.VMEM((step, total), jnp.bfloat16),
                pltpu.VMEM((step, total), jnp.bfloat16),
            ],
            compiler_params=limit(32),
            cost_estimate=pl.CostEstimate(
                flops=4 * total * total * span,
                bytes_accessed=2 * total * (span + LANES),
                transcendentals=total * total,
            ),
        )(*blocks)

    def back(mixed_values, *kept_values):
        western = shifted(mixed_values, "win", LAT_WINDOWS)
        selected = pl.pallas_call(
            functools.partial(select_kernel, split, mixed_count, groups),
            out_shape=[block(mixed_packed + len(kept_values) * kept_packed)] * groups,
            in_specs=[smem] + whole(2 + len(kept_values)),
            out_specs=whole(groups),
            compiler_params=limit(16),
            cost_estimate=pl.CostEstimate(
                flops=total * LANES * 20, bytes_accessed=8 * total * LANES, transcendentals=0
            ),
        )(lon_shift, mixed_values, western, *kept_values)
        return spread(selected, -1)

    first_kept_values, first_mixed_values = attention(0, total // 10, *kept, *first_mixed)
    second_kept_values, second_mixed_values = attention(1, total // 4, *kept, *second_mixed)
    first = back(first_mixed_values, first_kept_values, second_kept_values)
    second = back(second_mixed_values)

    cost = pl.CostEstimate(
        flops=2 * rows * columns * groups * LANES * features,
        bytes_accessed=features * (HEADS * HD + 6 * rows * columns),
        transcendentals=0,
    )
    ordered = (groups * LANES, features)
    partial, weight = pl.pallas_call(
        functools.partial(first_output_kernel, split, groups),
        out_shape=[
            jax.ShapeDtypeStruct(field.shape, jnp.float32),
            jax.ShapeDtypeStruct(ordered, jnp.bfloat16),
        ],
        in_specs=whole(2 + groups),
        out_specs=whole(2),
        scratch_shapes=[pltpu.VMEM(ordered, jnp.bfloat16)],
        compiler_params=limit(24),
        cost_estimate=cost,
    )(field, out_weight, *first)
    result = pl.pallas_call(
        functools.partial(second_output_kernel, split),
        out_shape=jax.ShapeDtypeStruct(field.shape, jnp.bfloat16),
        in_specs=whole(2 + groups),
        out_specs=pl.BlockSpec(memory_space=pltpu.VMEM),
        compiler_params=limit(24),
        cost_estimate=cost,
    )(partial, weight, *second)
    return result[None]


def solution(mesh):
    placed = (P("win", "tok", None, None), P(), P(), P(), P())
    return jax.shard_map(
        shards, mesh=mesh, in_specs=placed, out_specs=P("win", "tok", None, None), check_vma=False
    )
```

```python
import functools

import jax
import jax.numpy as jnp
from jax import lax
from jax.experimental import pallas as pl
from jax.experimental.pallas import tpu as pltpu
from jax.sharding import PartitionSpec as P

HEADS = 8
HD = 80
LAT_WINDOWS = 4
LANES = 128
SUBLANES = 8
MIB = 1024 * 1024
CHUNKS = 5
COPIES = 1


def round_up(value, unit):
    return -(-value // unit) * unit


def shifted(block, axis, distance):
    count = lax.axis_size(axis)
    return lax.ppermute(block, axis, [(i, (i + distance) % count) for i in range(count)])


def after(blocks, arrived):
    return [
        block if other is None else lax.optimization_barrier((block, other))[0]
        for block, other in zip(blocks, arrived)
    ]


def column_offset(lon_shift):
    return lon_shift[lax.rem(lax.axis_index("win"), LAT_WINDOWS)]


SPARE = 2 * LANES - 3 * HD


def dense_rows(count):
    return 2 * count - SPARE


def dense(block):
    count, width = block.shape
    second = block[:, LANES:]
    last = second[count - SPARE :]
    pieces = [last[:, at : at + SPARE] for at in range(0, width - LANES, SPARE)]
    empty = count - SPARE - SPARE * len(pieces)
    if empty:
        pieces.append(jnp.zeros((empty, SPARE), block.dtype))
    filled = jnp.concatenate([second[: count - SPARE], jnp.concatenate(pieces, axis=0)], axis=1)
    return jnp.concatenate([block[:, :LANES], filled], axis=0)


def project(tokens, gain, weight, copies, slots):
    groups = slots.shape[0]
    local = HEADS // groups
    features = tokens.shape[1]
    factor = lax.rsqrt(jnp.mean(tokens * tokens, axis=-1, keepdims=True) + 1e-06)
    normed = (tokens * factor * gain[...].reshape(1, features)).astype(jnp.bfloat16)
    chunk = features // len(copies)
    qkv = None
    for index, copy in enumerate(copies):
        for piece in copy:
            piece.wait()
        inner = slice(index * chunk, (index + 1) * chunk)
        share = jnp.dot(normed[:, inner], weight[inner], preferred_element_type=jnp.float32)
        qkv = share if qkv is None else qkv + share
    qkv = qkv.astype(jnp.bfloat16)
    place = lax.axis_index("tok")
    for group in range(groups):
        slot = lax.rem(group - place + groups, groups)
        blocks = []
        for head in range(group * local, (group + 1) * local):
            columns = [
                qkv[:, (kind * HEADS + head) * HD : (kind * HEADS + head + 1) * HD]
                for kind in (1, 0, 2)
            ]
            blocks.append(dense(jnp.concatenate(columns, axis=1)))
        slots[slot] = jnp.concatenate(blocks, axis=0)


def kept_kernel(split, field, gain, weight, *refs):
    *outs, slots, held_weight, sems, held_field, held_gain = refs
    total = CHUNKS * COPIES
    first = pltpu.make_async_copy(field, held_field, sems.at[total])
    second = pltpu.make_async_copy(gain, held_gain, sems.at[total + 1])
    chunk = weight.shape[0] // total
    pieces = []
    for index in range(total):
        inner = pl.ds(index * chunk, chunk)
        pieces.append(
            pltpu.make_async_copy(weight.at[inner], held_weight.at[inner], sems.at[index])
        )
    for copy in (first, second, *pieces):
        copy.start()
    copies = [pieces[index : index + COPIES] for index in range(0, total, COPIES)]
    first.wait()
    second.wait()
    rows, columns, features = field.shape
    tokens = held_field[...].astype(jnp.float32)[:, split:]
    tokens = tokens.reshape(rows * (columns - split), features)
    project(tokens, held_gain, held_weight, copies, slots)
    copies = [
        pltpu.make_async_copy(slots.at[index], out, sems.at[index])
        for index, out in enumerate(outs)
    ]
    for copy in copies:
        copy.start()
    for copy in copies:
        copy.wait()


def mixed_kernel(split, field, gain, weight, lon_shift, eastern, *refs):
    *outs, slots = refs
    rows, _, features = field.shape
    own = field[...].astype(jnp.float32)[:, :split]
    column = lax.broadcasted_iota(jnp.int32, own.shape, 1)
    tokens = jnp.where(column < column_offset(lon_shift), eastern[...].astype(jnp.float32), own)
    project(tokens.reshape(rows * split, features), gain, weight, [[]], slots)
    groups = slots.shape[0]
    for index, out in enumerate(outs):
        first = index // groups * out.shape[0]
        out[...] = slots[index % groups, first : first + out.shape[0]]


def place_rows(block, first, count, held, start):
    held[start : start + count, :LANES] = block[first : first + count]
    second = block[first + count : first + dense_rows(count)]
    used = LANES - SPARE
    lane = lax.broadcasted_iota(jnp.int32, second.shape, 1)
    ones = jnp.ones(second.shape, second.dtype)
    held[start : start + count - SPARE, LANES:] = jnp.where(lane < used, second, ones)
    pieces = [second[at : at + SPARE, used:] for at in range(0, used, SPARE)]
    pieces.append(jnp.ones((SPARE, SPARE), second.dtype))
    held[start + count - SPARE : start + count, LANES:] = jnp.concatenate(pieces, axis=1)


def gather(head, kept, kept_count, mixed, mixed_count, held, keys):
    start = 0
    for block in kept:
        place_rows(block, head * dense_rows(kept_count), kept_count, held, start)
        start += kept_count
    for block in mixed:
        place_rows(block, 0, mixed_count, held, start)
        start += mixed_count
    keys[...] = held[:, :LANES].T


def attend(held, keys, attended, scores, weights):
    span = held.shape[1]
    factor = HD ** (-0.5) * 1.4426950408889634
    step = scores[0].shape[0]
    chunk = 16
    steps = held.shape[0] // step

    def score(index, out):
        first = index * step
        queries = pltpu.roll(held[first : first + step].astype(jnp.float32), span - HD, axis=1)
        queries = queries[:, :LANES]
        lane = lax.broadcasted_iota(jnp.int32, queries.shape, 1)
        queries = jnp.where(lane < HD, queries, 0.0).astype(jnp.bfloat16)
        out[...] = jnp.dot(queries, keys[...], preferred_element_type=jnp.float32)

    score(0, scores[0])
    for index in range(steps):
        if index + 1 < steps:
            score(index + 1, scores[(index + 1) % 2])
        now, out = scores[index % 2], weights[index % 2]
        for first in range(0, step, chunk):
            part = now[first : first + chunk]
            top = jnp.max(part, axis=-1, keepdims=True)
            out[first : first + chunk] = jnp.exp2((part - top) * factor).astype(jnp.bfloat16)
        values = jnp.dot(out[...], held[:, span - LANES :], preferred_element_type=jnp.float32)
        first = 2 * HD - (span - LANES)
        values = values / values[:, first + HD : first + HD + 1]
        attended[index * step : (index + 1) * step] = pltpu.roll(values, LANES - first, axis=1)


def packed_rows(count):
    part = round_up(-(-count * (HD - LANES // 2) // LANES), SUBLANES)
    return count // 2 + part, part


def pack(rows):
    count = rows.shape[0]
    half = LANES // 2
    rest = HD - half
    part = packed_rows(count)[1]
    lane = lax.broadcasted_iota(jnp.int32, (count // 2, LANES), 1)
    main = jnp.where(lane < half, rows[: count // 2], pltpu.roll(rows[count // 2 :], half, axis=1))
    lane = lax.broadcasted_iota(jnp.int32, (part, LANES), 1)
    rests = jnp.zeros((part, LANES), jnp.float32)
    for index in range(-(-count // part)):
        piece = rows[index * part : (index + 1) * part]
        if piece.shape[0] < part:
            empty = jnp.zeros((part - piece.shape[0], LANES), jnp.float32)
            piece = jnp.concatenate([piece, empty], axis=0)
        turn = (index * rest + half) % LANES
        piece = pltpu.roll(piece, turn, axis=1) if turn else piece
        rests = jnp.where(lane // rest == index, piece, rests)
    return jnp.concatenate([main, rests], axis=0)


def unpack(block, count):
    half = LANES // 2
    rest = HD - half
    part = packed_rows(count)[1]
    main, rests = block[: count // 2], block[count // 2 : count // 2 + part]
    main = jnp.concatenate([main, pltpu.roll(main, half, axis=1)], axis=0)
    pieces = []
    for index in range(-(-count // part)):
        turn = (half - index * rest) % LANES
        piece = pltpu.roll(rests, turn, axis=1) if turn else rests
        pieces.append(piece[: min(part, count - index * part)])
    lane = lax.broadcasted_iota(jnp.int32, main.shape, 1)
    return jnp.where(lane < half, main, jnp.concatenate(pieces, axis=0))


def packed_tokens(count):
    half = LANES // 2
    total, part = packed_rows(count)
    row = lax.broadcasted_iota(jnp.int32, (total, LANES), 0)
    lane = lax.broadcasted_iota(jnp.int32, (total, LANES), 1)
    main = row + jnp.where(lane < half, 0, count // 2)
    rests = row - count // 2 + lane // (HD - half) * part
    return jnp.where(row < count // 2, main, rests)


def attention_kernel(head, groups, kept_count, mixed_count, *refs):
    kept, mixed = refs[:groups], refs[groups : 2 * groups]
    kept_out, mixed_out, held, keys, attended, *rest = refs[2 * groups :]
    gather(head, kept, kept_count, mixed, mixed_count, held, keys)
    attend(held, keys, attended, rest[:2], rest[2:])
    start = 0
    for count, out in ((kept_count, kept_out), (mixed_count, mixed_out)):
        packed = []
        for _ in range(groups):
            packed.append(pack(attended[start : start + count]))
            start += count
        out[...] = jnp.concatenate(packed, axis=0).astype(jnp.bfloat16)


def select_kernel(split, count, groups, lon_shift, mixed, western, *refs):
    kept, outs = refs[:-groups], refs[-groups:]
    taken = lax.rem(packed_tokens(count), split) < column_offset(lon_shift)
    own, west = mixed[...].astype(jnp.float32), western[...].astype(jnp.float32)
    rests = [rest[...].astype(jnp.float32) for rest in kept]
    size = own.shape[0] // groups
    for group, out in enumerate(outs):
        rows = slice(group * size, (group + 1) * size)
        pieces = [jnp.where(taken, west[rows], own[rows])]
        for rest in rests:
            part = rest.shape[0] // groups
            pieces.append(rest[group * part : (group + 1) * part])
        out[...] = jnp.concatenate(pieces, axis=0).astype(jnp.bfloat16)


def projected(blocks, first, count, weight, shape):
    total = packed_rows(count)[0]
    columns = [unpack(block[first : first + total], count) for block in blocks]
    attended = jnp.concatenate(columns, axis=1).astype(jnp.bfloat16)
    return jnp.dot(attended, weight[...], preferred_element_type=jnp.float32).reshape(shape)


def first_output_kernel(split, groups, field, weight, *refs):
    *blocks, out, second, first = refs
    features = field.shape[2]
    for slot in range(groups):
        group = lax.rem(lax.axis_index("tok") + slot, groups)
        for head, ordered in enumerate((first, second)):
            at = pl.multiple_of((group * HEADS // groups + head) * HD, 16)
            ordered[slot * LANES : slot * LANES + HD] = weight[pl.ds(at, HD)]
            ordered[slot * LANES + HD : (slot + 1) * LANES] = jnp.zeros(
                (LANES - HD, features), jnp.bfloat16
            )
    rows, columns, _ = field.shape
    kept_count, mixed_count = rows * (columns - split), rows * split
    blocks = [block[...].astype(jnp.float32) for block in blocks]
    tokens = field[...].astype(jnp.float32)
    at = packed_rows(mixed_count)[0]
    shape = (rows, split, features)
    left = tokens[:, :split] + projected(blocks, 0, mixed_count, first, shape)
    shape = (rows, columns - split, features)
    right = tokens[:, split:] + projected(blocks, at, kept_count, first, shape)
    at += packed_rows(kept_count)[0]
    right += projected(blocks, at, kept_count, second, shape)
    out[...] = jnp.concatenate([left, right], axis=1)


def second_output_kernel(split, partial, weight, *refs):
    *blocks, out = refs
    rows, _, features = partial.shape
    blocks = [block[...].astype(jnp.float32) for block in blocks]
    tokens = partial[...]
    left = projected(blocks, 0, rows * split, weight, (rows, split, features))
    out[...] = jnp.concatenate(
        [tokens[:, :split] + left, tokens[:, split:]], axis=1
    ).astype(jnp.bfloat16)


def whole(count):
    return [pl.BlockSpec(memory_space=pltpu.VMEM)] * count


def shards(field_tokens, lon_shift, norm_gain, qkv_weight, out_weight):
    _, rows, columns, features = field_tokens.shape
    groups = lax.axis_size("tok")
    local = HEADS // groups
    width = local * HD
    span = round_up(3 * HD + 1, LANES)
    split = round_up(columns // 2, SUBLANES)
    field = field_tokens[0]
    smem = pl.BlockSpec(memory_space=pltpu.SMEM)
    kept_count, mixed_count = rows * (columns - split), rows * split

    def limit(size):
        return pltpu.CompilerParams(vmem_limit_bytes=size * MIB)

    def projection(kernel, count, parts, specs, out_specs, held, params, *operands):
        size = local * dense_rows(count)
        block = jax.ShapeDtypeStruct((size // parts, LANES), jnp.bfloat16)
        return pl.pallas_call(
            functools.partial(kernel, split),
            out_shape=[block] * (parts * groups),
            in_specs=specs,
            out_specs=out_specs,
            scratch_shapes=[
                pltpu.VMEM((groups, size, LANES), jnp.bfloat16),
                *held,
            ],
            compiler_params=params,
            cost_estimate=pl.CostEstimate(
                flops=2 * count * features * 3 * HEADS * HD,
                bytes_accessed=2 * features * (3 * HEADS * HD + 2 * count),
                transcendentals=0,
            ),
        )(*operands)

    def spread(blocks, sign):
        arrived = list(blocks)
        for distance in sorted(range(1, groups), key=lambda step: step * (step - groups)):
            arrived[distance] = shifted(blocks[distance], "tok", sign * distance)
        return arrived

    eastern = shifted(field[:, :split], "win", -LAT_WINDOWS)
    hbm = pl.BlockSpec(memory_space=pltpu.HBM)
    operands = (field, norm_gain, qkv_weight)
    held = [
        pltpu.VMEM(qkv_weight.shape, qkv_weight.dtype),
        pltpu.SemaphoreType.DMA((CHUNKS * COPIES + 2,)),
        pltpu.VMEM(field.shape, field.dtype),
        pltpu.VMEM(norm_gain.shape, norm_gain.dtype),
    ]
    kept = projection(
        kept_kernel, kept_count, 1, [hbm] * 3, [hbm] * groups, held, limit(60), *operands
    )
    kept = spread(kept, 1)
    specs = [*whole(3), smem, *whole(1)]
    operands += (lon_shift, eastern)
    mixed = projection(
        mixed_kernel, mixed_count, local, specs, whole(local * groups), [], limit(48), *operands
    )
    first_mixed = spread(after(mixed[:groups], [None, *kept[1:]]), 1)
    second_mixed = spread(after(mixed[groups:], [None, *first_mixed[1:]]), 1)

    total = groups * rows * columns
    mixed_packed, kept_packed = packed_rows(mixed_count)[0], packed_rows(kept_count)[0]

    def block(count):
        return jax.ShapeDtypeStruct((count, LANES), jnp.bfloat16)

    def attention(head, step, *blocks):
        return pl.pallas_call(
            functools.partial(attention_kernel, head, groups, kept_count, mixed_count),
            out_shape=[block(groups * kept_packed), block(groups * mixed_packed)],
            in_specs=whole(len(blocks)),
            out_specs=whole(2),
            scratch_shapes=[
                pltpu.VMEM((total, span), jnp.bfloat16),
                pltpu.VMEM((LANES, total), jnp.bfloat16),
                pltpu.VMEM((total, LANES), jnp.float32),
                pltpu.VMEM((step, total), jnp.float32),
                pltpu.VMEM((step, total), jnp.float32),
                pltpu.VMEM((step, total), jnp.bfloat16),
                pltpu.VMEM((step, total), jnp.bfloat16),
            ],
            compiler_params=limit(32),
            cost_estimate=pl.CostEstimate(
                flops=4 * total * total * span,
                bytes_accessed=2 * total * (span + LANES),
                transcendentals=total * total,
            ),
        )(*blocks)

    def back(mixed_values, *kept_values):
        western = shifted(mixed_values, "win", LAT_WINDOWS)
        selected = pl.pallas_call(
            functools.partial(select_kernel, split, mixed_count, groups),
            out_shape=[block(mixed_packed + len(kept_values) * kept_packed)] * groups,
            in_specs=[smem] + whole(2 + len(kept_values)),
            out_specs=whole(groups),
            compiler_params=limit(16),
            cost_estimate=pl.CostEstimate(
                flops=total * LANES * 20, bytes_accessed=8 * total * LANES, transcendentals=0
            ),
        )(lon_shift, mixed_values, western, *kept_values)
        return spread(selected, -1)

    first_kept_values, first_mixed_values = attention(0, total // 5, *kept, *first_mixed)
    second_kept_values, second_mixed_values = attention(1, total // 5, *kept, *second_mixed)
    first = back(first_mixed_values, first_kept_values, second_kept_values)
    second = back(second_mixed_values)

    cost = pl.CostEstimate(
        flops=2 * rows * columns * groups * LANES * features,
        bytes_accessed=features * (HEADS * HD + 6 * rows * columns),
        transcendentals=0,
    )
    ordered = (groups * LANES, features)
    partial, weight = pl.pallas_call(
        functools.partial(first_output_kernel, split, groups),
        out_shape=[
            jax.ShapeDtypeStruct(field.shape, jnp.float32),
            jax.ShapeDtypeStruct(ordered, jnp.bfloat16),
        ],
        in_specs=whole(2 + groups),
        out_specs=whole(2),
        scratch_shapes=[pltpu.VMEM(ordered, jnp.bfloat16)],
        compiler_params=limit(24),
        cost_estimate=cost,
    )(field, out_weight, *first)
    result = pl.pallas_call(
        functools.partial(second_output_kernel, split),
        out_shape=jax.ShapeDtypeStruct(field.shape, jnp.bfloat16),
        in_specs=whole(2 + groups),
        out_specs=pl.BlockSpec(memory_space=pltpu.VMEM),
        compiler_params=limit(24),
        cost_estimate=cost,
    )(partial, weight, *second)
    return result[None]


def solution(mesh):
    placed = (P("win", "tok", None, None), P(), P(), P(), P())
    return jax.shard_map(
        shards, mesh=mesh, in_specs=placed, out_specs=P("win", "tok", None, None), check_vma=False
    )
```

```python
import functools

import jax
import jax.numpy as jnp
from jax import lax
from jax.experimental import pallas as pl
from jax.experimental.pallas import tpu as pltpu
from jax.sharding import PartitionSpec as P

HEADS = 8
HD = 80
LAT_WINDOWS = 4
LANES = 128
SUBLANES = 8
MIB = 1024 * 1024
CHUNKS = 5
COPIES = 1


def round_up(value, unit):
    return -(-value // unit) * unit


def shifted(block, axis, distance):
    count = lax.axis_size(axis)
    return lax.ppermute(block, axis, [(i, (i + distance) % count) for i in range(count)])


def travel_order(groups):
    return [0, *range(groups - 1, 0, -1)]


def after(blocks, arrived):
    return [
        block if other is None else lax.optimization_barrier((block, other))[0]
        for block, other in zip(blocks, arrived)
    ]


def column_offset(lon_shift):
    return lon_shift[lax.rem(lax.axis_index("win"), LAT_WINDOWS)]


SPARE = 2 * LANES - 3 * HD


def dense_rows(count):
    return 2 * count - SPARE


def dense(block):
    count, width = block.shape
    second = block[:, LANES:]
    last = second[count - SPARE :]
    pieces = [last[:, at : at + SPARE] for at in range(0, width - LANES, SPARE)]
    empty = count - SPARE - SPARE * len(pieces)
    if empty:
        pieces.append(jnp.zeros((empty, SPARE), block.dtype))
    filled = jnp.concatenate([second[: count - SPARE], jnp.concatenate(pieces, axis=0)], axis=1)
    return jnp.concatenate([block[:, :LANES], filled], axis=0)


def project(tokens, gain, weight, copies, slots):
    groups = slots.shape[0]
    local = HEADS // groups
    features = tokens.shape[1]
    factor = lax.rsqrt(jnp.mean(tokens * tokens, axis=-1, keepdims=True) + 1e-06)
    normed = (tokens * factor * gain[...].reshape(1, features)).astype(jnp.bfloat16)
    chunk = features // len(copies)
    qkv = None
    for index, copy in enumerate(copies):
        for piece in copy:
            piece.wait()
        inner = slice(index * chunk, (index + 1) * chunk)
        share = jnp.dot(normed[:, inner], weight[inner], preferred_element_type=jnp.float32)
        qkv = share if qkv is None else qkv + share
    qkv = qkv.astype(jnp.bfloat16)
    place = lax.axis_index("tok")
    for group in range(groups):
        slot = lax.rem(place - group + groups, groups)
        blocks = []
        for head in range(group * local, (group + 1) * local):
            columns = [
                qkv[:, (kind * HEADS + head) * HD : (kind * HEADS + head + 1) * HD]
                for kind in (1, 0, 2)
            ]
            blocks.append(dense(jnp.concatenate(columns, axis=1)))
        slots[slot] = jnp.concatenate(blocks, axis=0)


def kept_kernel(split, field, gain, weight, *refs):
    *outs, slots, held_weight, sems, held_field, held_gain = refs
    total = CHUNKS * COPIES
    first = pltpu.make_async_copy(field, held_field, sems.at[total])
    second = pltpu.make_async_copy(gain, held_gain, sems.at[total + 1])
    chunk = weight.shape[0] // total
    pieces = []
    for index in range(total):
        inner = pl.ds(index * chunk, chunk)
        pieces.append(
            pltpu.make_async_copy(weight.at[inner], held_weight.at[inner], sems.at[index])
        )
    for copy in (first, second, *pieces):
        copy.start()
    copies = [pieces[index : index + COPIES] for index in range(0, total, COPIES)]
    first.wait()
    second.wait()
    rows, columns, features = field.shape
    tokens = held_field[...].astype(jnp.float32)[:, split:]
    tokens = tokens.reshape(rows * (columns - split), features)
    project(tokens, held_gain, held_weight, copies, slots)
    copies = [
        pltpu.make_async_copy(slots.at[index], out, sems.at[index])
        for index, out in enumerate(outs)
    ]
    for copy in copies:
        copy.start()
    for copy in copies:
        copy.wait()


def mixed_kernel(split, field, gain, weight, lon_shift, eastern, *refs):
    *outs, slots = refs
    rows, _, features = field.shape
    own = field[...].astype(jnp.float32)[:, :split]
    column = lax.broadcasted_iota(jnp.int32, own.shape, 1)
    tokens = jnp.where(column < column_offset(lon_shift), eastern[...].astype(jnp.float32), own)
    project(tokens.reshape(rows * split, features), gain, weight, [[]], slots)
    groups = slots.shape[0]
    for index, out in enumerate(outs):
        first = index // groups * out.shape[0]
        out[...] = slots[index % groups, first : first + out.shape[0]]


def place_rows(block, first, count, held, start):
    held[start : start + count, :LANES] = block[first : first + count]
    second = block[first + count : first + dense_rows(count)]
    used = LANES - SPARE
    lane = lax.broadcasted_iota(jnp.int32, second.shape, 1)
    ones = jnp.ones(second.shape, second.dtype)
    held[start : start + count - SPARE, LANES:] = jnp.where(lane < used, second, ones)
    pieces = [second[at : at + SPARE, used:] for at in range(0, used, SPARE)]
    pieces.append(jnp.ones((SPARE, SPARE), second.dtype))
    held[start + count - SPARE : start + count, LANES:] = jnp.concatenate(pieces, axis=1)


def gather(head, kept, kept_count, mixed, mixed_count, held, keys):
    start = 0
    for block in kept:
        place_rows(block, head * dense_rows(kept_count), kept_count, held, start)
        start += kept_count
    for block in mixed:
        place_rows(block, 0, mixed_count, held, start)
        start += mixed_count
    keys[...] = held[:, :LANES].T


def attend(held, keys, attended, scores, weights):
    span = held.shape[1]
    factor = HD ** (-0.5) * 1.4426950408889634
    step = scores[0].shape[0]
    chunk = 16
    steps = held.shape[0] // step

    def score(index, out):
        first = index * step
        queries = pltpu.roll(held[first : first + step].astype(jnp.float32), span - HD, axis=1)
        queries = queries[:, :LANES]
        lane = lax.broadcasted_iota(jnp.int32, queries.shape, 1)
        queries = jnp.where(lane < HD, queries, 0.0).astype(jnp.bfloat16)
        out[...] = jnp.dot(queries, keys[...], preferred_element_type=jnp.float32)

    score(0, scores[0])
    for index in range(steps):
        if index + 1 < steps:
            score(index + 1, scores[(index + 1) % 2])
        now, out = scores[index % 2], weights[index % 2]
        for first in range(0, step, chunk):
            part = now[first : first + chunk]
            top = jnp.max(part, axis=-1, keepdims=True)
            out[first : first + chunk] = jnp.exp2((part - top) * factor).astype(jnp.bfloat16)
        values = jnp.dot(out[...], held[:, span - LANES :], preferred_element_type=jnp.float32)
        first = 2 * HD - (span - LANES)
        values = values / values[:, first + HD : first + HD + 1]
        attended[index * step : (index + 1) * step] = pltpu.roll(values, LANES - first, axis=1)


def packed_rows(count):
    part = round_up(-(-count * (HD - LANES // 2) // LANES), SUBLANES)
    return count // 2 + part, part


def pack(rows):
    count = rows.shape[0]
    half = LANES // 2
    rest = HD - half
    part = packed_rows(count)[1]
    lane = lax.broadcasted_iota(jnp.int32, (count // 2, LANES), 1)
    main = jnp.where(lane < half, rows[: count // 2], pltpu.roll(rows[count // 2 :], half, axis=1))
    lane = lax.broadcasted_iota(jnp.int32, (part, LANES), 1)
    rests = jnp.zeros((part, LANES), jnp.float32)
    for index in range(-(-count // part)):
        piece = rows[index * part : (index + 1) * part]
        if piece.shape[0] < part:
            empty = jnp.zeros((part - piece.shape[0], LANES), jnp.float32)
            piece = jnp.concatenate([piece, empty], axis=0)
        turn = (index * rest + half) % LANES
        piece = pltpu.roll(piece, turn, axis=1) if turn else piece
        rests = jnp.where(lane // rest == index, piece, rests)
    return jnp.concatenate([main, rests], axis=0)


def unpack(block, count):
    half = LANES // 2
    rest = HD - half
    part = packed_rows(count)[1]
    main, rests = block[: count // 2], block[count // 2 : count // 2 + part]
    main = jnp.concatenate([main, pltpu.roll(main, half, axis=1)], axis=0)
    pieces = []
    for index in range(-(-count // part)):
        turn = (half - index * rest) % LANES
        piece = pltpu.roll(rests, turn, axis=1) if turn else rests
        pieces.append(piece[: min(part, count - index * part)])
    lane = lax.broadcasted_iota(jnp.int32, main.shape, 1)
    return jnp.where(lane < half, main, jnp.concatenate(pieces, axis=0))


def packed_tokens(count):
    half = LANES // 2
    total, part = packed_rows(count)
    row = lax.broadcasted_iota(jnp.int32, (total, LANES), 0)
    lane = lax.broadcasted_iota(jnp.int32, (total, LANES), 1)
    main = row + jnp.where(lane < half, 0, count // 2)
    rests = row - count // 2 + lane // (HD - half) * part
    return jnp.where(row < count // 2, main, rests)


def attention_kernel(head, groups, kept_count, mixed_count, *refs):
    kept, mixed = refs[:groups], refs[groups : 2 * groups]
    kept_out, mixed_out, held, keys, attended, *rest = refs[2 * groups :]
    gather(head, kept, kept_count, mixed, mixed_count, held, keys)
    attend(held, keys, attended, rest[:2], rest[2:])
    start = 0
    for count, out in ((kept_count, kept_out), (mixed_count, mixed_out)):
        packed = []
        for _ in range(groups):
            packed.append(pack(attended[start : start + count]))
            start += count
        out[...] = jnp.concatenate(packed, axis=0).astype(jnp.bfloat16)


def select_kernel(split, count, groups, lon_shift, mixed, western, *refs):
    kept, outs = refs[:-groups], refs[-groups:]
    taken = lax.rem(packed_tokens(count), split) < column_offset(lon_shift)
    own, west = mixed[...].astype(jnp.float32), western[...].astype(jnp.float32)
    rests = [rest[...].astype(jnp.float32) for rest in kept]
    size = own.shape[0] // groups
    for group, out in enumerate(outs):
        rows = slice(group * size, (group + 1) * size)
        pieces = [jnp.where(taken, west[rows], own[rows])]
        for rest in rests:
            part = rest.shape[0] // groups
            pieces.append(rest[group * part : (group + 1) * part])
        out[...] = jnp.concatenate(pieces, axis=0).astype(jnp.bfloat16)


def projected(blocks, first, count, weight, shape):
    total = packed_rows(count)[0]
    columns = [unpack(block[first : first + total], count) for block in blocks]
    attended = jnp.concatenate(columns, axis=1).astype(jnp.bfloat16)
    return jnp.dot(attended, weight[...], preferred_element_type=jnp.float32).reshape(shape)


def first_output_kernel(split, groups, field, weight, *refs):
    *blocks, out, second, first = refs
    features = field.shape[2]
    for slot, distance in enumerate(travel_order(groups)):
        group = lax.rem(lax.axis_index("tok") + distance, groups)
        for head, ordered in enumerate((first, second)):
            at = pl.multiple_of((group * HEADS // groups + head) * HD, 16)
            ordered[slot * LANES : slot * LANES + HD] = weight[pl.ds(at, HD)]
            ordered[slot * LANES + HD : (slot + 1) * LANES] = jnp.zeros(
                (LANES - HD, features), jnp.bfloat16
            )
    rows, columns, _ = field.shape
    kept_count, mixed_count = rows * (columns - split), rows * split
    blocks = [block[...].astype(jnp.float32) for block in blocks]
    tokens = field[...].astype(jnp.float32)
    at = packed_rows(mixed_count)[0]
    shape = (rows, split, features)
    left = tokens[:, :split] + projected(blocks, 0, mixed_count, first, shape)
    shape = (rows, columns - split, features)
    right = tokens[:, split:] + projected(blocks, at, kept_count, first, shape)
    at += packed_rows(kept_count)[0]
    right += projected(blocks, at, kept_count, second, shape)
    out[...] = jnp.concatenate([left, right], axis=1)


def second_output_kernel(split, partial, weight, *refs):
    *blocks, out = refs
    rows, _, features = partial.shape
    blocks = [block[...].astype(jnp.float32) for block in blocks]
    tokens = partial[...]
    left = projected(blocks, 0, rows * split, weight, (rows, split, features))
    out[...] = jnp.concatenate(
        [tokens[:, :split] + left, tokens[:, split:]], axis=1
    ).astype(jnp.bfloat16)


def whole(count):
    return [pl.BlockSpec(memory_space=pltpu.VMEM)] * count


def shards(field_tokens, lon_shift, norm_gain, qkv_weight, out_weight):
    _, rows, columns, features = field_tokens.shape
    groups = lax.axis_size("tok")
    local = HEADS // groups
    width = local * HD
    span = round_up(3 * HD + 1, LANES)
    split = round_up(columns // 2, SUBLANES)
    field = field_tokens[0]
    smem = pl.BlockSpec(memory_space=pltpu.SMEM)
    kept_count, mixed_count = rows * (columns - split), rows * split

    def limit(size):
        return pltpu.CompilerParams(vmem_limit_bytes=size * MIB)

    def projection(kernel, count, parts, specs, out_specs, held, params, *operands):
        size = local * dense_rows(count)
        block = jax.ShapeDtypeStruct((size // parts, LANES), jnp.bfloat16)
        return pl.pallas_call(
            functools.partial(kernel, split),
            out_shape=[block] * (parts * groups),
            in_specs=specs,
            out_specs=out_specs,
            scratch_shapes=[
                pltpu.VMEM((groups, size, LANES), jnp.bfloat16),
                *held,
            ],
            compiler_params=params,
            cost_estimate=pl.CostEstimate(
                flops=2 * count * features * 3 * HEADS * HD,
                bytes_accessed=2 * features * (3 * HEADS * HD + 2 * count),
                transcendentals=0,
            ),
        )(*operands)

    def spread(blocks, sign):
        return [blocks[0]] + [
            shifted(block, "tok", sign * distance)
            for block, distance in zip(blocks[1:], travel_order(groups)[1:])
        ]

    eastern = shifted(field[:, :split], "win", -LAT_WINDOWS)
    hbm = pl.BlockSpec(memory_space=pltpu.HBM)
    operands = (field, norm_gain, qkv_weight)
    held = [
        pltpu.VMEM(qkv_weight.shape, qkv_weight.dtype),
        pltpu.SemaphoreType.DMA((CHUNKS * COPIES + 2,)),
        pltpu.VMEM(field.shape, field.dtype),
        pltpu.VMEM(norm_gain.shape, norm_gain.dtype),
    ]
    kept = projection(
        kept_kernel, kept_count, 1, [hbm] * 3, [hbm] * groups, held, limit(60), *operands
    )
    kept = spread(kept, 1)
    specs = [*whole(3), smem, *whole(1)]
    operands += (lon_shift, eastern)
    mixed = projection(
        mixed_kernel, mixed_count, local, specs, whole(local * groups), [], limit(48), *operands
    )
    first_mixed = spread(after(mixed[:groups], [None, *kept[1:]]), 1)
    second_mixed = spread(after(mixed[groups:], [None, *first_mixed[1:]]), 1)

    total = groups * rows * columns
    mixed_packed, kept_packed = packed_rows(mixed_count)[0], packed_rows(kept_count)[0]

    def block(count):
        return jax.ShapeDtypeStruct((count, LANES), jnp.bfloat16)

    def attention(head, step, *blocks):
        return pl.pallas_call(
            functools.partial(attention_kernel, head, groups, kept_count, mixed_count),
            out_shape=[block(groups * kept_packed), block(groups * mixed_packed)],
            in_specs=whole(len(blocks)),
            out_specs=whole(2),
            scratch_shapes=[
                pltpu.VMEM((total, span), jnp.bfloat16),
                pltpu.VMEM((LANES, total), jnp.bfloat16),
                pltpu.VMEM((total, LANES), jnp.float32),
                pltpu.VMEM((step, total), jnp.float32),
                pltpu.VMEM((step, total), jnp.float32),
                pltpu.VMEM((step, total), jnp.bfloat16),
                pltpu.VMEM((step, total), jnp.bfloat16),
            ],
            compiler_params=limit(32),
            cost_estimate=pl.CostEstimate(
                flops=4 * total * total * span,
                bytes_accessed=2 * total * (span + LANES),
                transcendentals=total * total,
            ),
        )(*blocks)

    def back(mixed_values, *kept_values):
        western = shifted(mixed_values, "win", LAT_WINDOWS)
        selected = pl.pallas_call(
            functools.partial(select_kernel, split, mixed_count, groups),
            out_shape=[block(mixed_packed + len(kept_values) * kept_packed)] * groups,
            in_specs=[smem] + whole(2 + len(kept_values)),
            out_specs=whole(groups),
            compiler_params=limit(16),
            cost_estimate=pl.CostEstimate(
                flops=total * LANES * 20, bytes_accessed=8 * total * LANES, transcendentals=0
            ),
        )(lon_shift, mixed_values, western, *kept_values)
        return spread(selected, -1)

    first_kept_values, first_mixed_values = attention(0, total // 5, *kept, *first_mixed)
    second_kept_values, second_mixed_values = attention(1, total // 5, *kept, *second_mixed)
    first = back(first_mixed_values, first_kept_values, second_kept_values)
    second = back(second_mixed_values)

    cost = pl.CostEstimate(
        flops=2 * rows * columns * groups * LANES * features,
        bytes_accessed=features * (HEADS * HD + 6 * rows * columns),
        transcendentals=0,
    )
    ordered = (groups * LANES, features)
    partial, weight = pl.pallas_call(
        functools.partial(first_output_kernel, split, groups),
        out_shape=[
            jax.ShapeDtypeStruct(field.shape, jnp.float32),
            jax.ShapeDtypeStruct(ordered, jnp.bfloat16),
        ],
        in_specs=whole(2 + groups),
        out_specs=whole(2),
        scratch_shapes=[pltpu.VMEM(ordered, jnp.bfloat16)],
        compiler_params=limit(24),
        cost_estimate=cost,
    )(field, out_weight, *first)
    result = pl.pallas_call(
        functools.partial(second_output_kernel, split),
        out_shape=jax.ShapeDtypeStruct(field.shape, jnp.bfloat16),
        in_specs=whole(2 + groups),
        out_specs=pl.BlockSpec(memory_space=pltpu.VMEM),
        compiler_params=limit(24),
        cost_estimate=cost,
    )(partial, weight, *second)
    return result[None]


def solution(mesh):
    placed = (P("win", "tok", None, None), P(), P(), P(), P())
    return jax.shard_map(
        shards, mesh=mesh, in_specs=placed, out_specs=P("win", "tok", None, None), check_vma=False
    )
```

```python
import functools

import jax
import jax.numpy as jnp
from jax import lax
from jax.experimental import pallas as pl
from jax.experimental.pallas import tpu as pltpu
from jax.sharding import PartitionSpec as P

HEADS = 8
HD = 80
LAT_WINDOWS = 4
LANES = 128
SUBLANES = 8
MIB = 1024 * 1024
CHUNKS = 5
COPIES = 1


def round_up(value, unit):
    return -(-value // unit) * unit


def shifted(block, axis, distance):
    count = lax.axis_size(axis)
    return lax.ppermute(block, axis, [(i, (i + distance) % count) for i in range(count)])


def travel_order(groups):
    return [0, *range(groups - 1, 0, -1)]


def after(blocks, arrived):
    return [
        block if other is None else lax.optimization_barrier((block, other))[0]
        for block, other in zip(blocks, [*arrived, *[None] * len(blocks)])
    ]


def column_offset(lon_shift):
    return lon_shift[lax.rem(lax.axis_index("win"), LAT_WINDOWS)]


SPARE = 2 * LANES - 3 * HD


def dense_rows(count):
    return 2 * count - SPARE


def dense(block):
    count, width = block.shape
    second = block[:, LANES:]
    last = second[count - SPARE :]
    pieces = [last[:, at : at + SPARE] for at in range(0, width - LANES, SPARE)]
    empty = count - SPARE - SPARE * len(pieces)
    if empty:
        pieces.append(jnp.zeros((empty, SPARE), block.dtype))
    filled = jnp.concatenate([second[: count - SPARE], jnp.concatenate(pieces, axis=0)], axis=1)
    return jnp.concatenate([block[:, :LANES], filled], axis=0)


def project(tokens, gain, weight, copies, slots):
    groups = slots.shape[0]
    local = HEADS // groups
    features = tokens.shape[1]
    factor = lax.rsqrt(jnp.mean(tokens * tokens, axis=-1, keepdims=True) + 1e-06)
    normed = (tokens * factor * gain[...].reshape(1, features)).astype(jnp.bfloat16)
    chunk = features // len(copies)
    qkv = None
    for index, copy in enumerate(copies):
        for piece in copy:
            piece.wait()
        inner = slice(index * chunk, (index + 1) * chunk)
        share = jnp.dot(normed[:, inner], weight[inner], preferred_element_type=jnp.float32)
        qkv = share if qkv is None else qkv + share
    qkv = qkv.astype(jnp.bfloat16)
    place = lax.axis_index("tok")
    for group in range(groups):
        slot = lax.rem(place - group + groups, groups)
        blocks = []
        for head in range(group * local, (group + 1) * local):
            columns = [
                qkv[:, (kind * HEADS + head) * HD : (kind * HEADS + head + 1) * HD]
                for kind in (1, 0, 2)
            ]
            blocks.append(dense(jnp.concatenate(columns, axis=1)))
        slots[slot] = jnp.concatenate(blocks, axis=0)


def kept_kernel(split, field, gain, weight, *refs):
    *outs, slots, held_weight, sems, held_field, held_gain = refs
    total = CHUNKS * COPIES
    first = pltpu.make_async_copy(field, held_field, sems.at[total])
    second = pltpu.make_async_copy(gain, held_gain, sems.at[total + 1])
    chunk = weight.shape[0] // total
    pieces = []
    for index in range(total):
        inner = pl.ds(index * chunk, chunk)
        pieces.append(
            pltpu.make_async_copy(weight.at[inner], held_weight.at[inner], sems.at[index])
        )
    for copy in (first, second, *pieces):
        copy.start()
    copies = [pieces[index : index + COPIES] for index in range(0, total, COPIES)]
    first.wait()
    second.wait()
    rows, columns, features = field.shape
    tokens = held_field[...].astype(jnp.float32)[:, split:]
    tokens = tokens.reshape(rows * (columns - split), features)
    project(tokens, held_gain, held_weight, copies, slots)
    copies = [
        pltpu.make_async_copy(slots.at[index], out, sems.at[index])
        for index, out in enumerate(outs)
    ]
    for copy in copies:
        copy.start()
    for copy in copies:
        copy.wait()


def mixed_kernel(split, field, gain, weight, lon_shift, eastern, *refs):
    *outs, slots = refs
    rows, _, features = field.shape
    own = field[...].astype(jnp.float32)[:, :split]
    column = lax.broadcasted_iota(jnp.int32, own.shape, 1)
    tokens = jnp.where(column < column_offset(lon_shift), eastern[...].astype(jnp.float32), own)
    project(tokens.reshape(rows * split, features), gain, weight, [[]], slots)
    groups = slots.shape[0]
    for index, out in enumerate(outs):
        first = index // groups * out.shape[0]
        out[...] = slots[index % groups, first : first + out.shape[0]]


def place_rows(block, first, count, held, start):
    held[start : start + count, :LANES] = block[first : first + count]
    second = block[first + count : first + dense_rows(count)]
    used = LANES - SPARE
    lane = lax.broadcasted_iota(jnp.int32, second.shape, 1)
    ones = jnp.ones(second.shape, second.dtype)
    held[start : start + count - SPARE, LANES:] = jnp.where(lane < used, second, ones)
    pieces = [second[at : at + SPARE, used:] for at in range(0, used, SPARE)]
    pieces.append(jnp.ones((SPARE, SPARE), second.dtype))
    held[start + count - SPARE : start + count, LANES:] = jnp.concatenate(pieces, axis=1)


def gather(head, kept, kept_count, mixed, mixed_count, held, keys):
    start = 0
    for block in kept:
        place_rows(block, head * dense_rows(kept_count), kept_count, held, start)
        start += kept_count
    for block in mixed:
        place_rows(block, 0, mixed_count, held, start)
        start += mixed_count
    keys[...] = held[:, :LANES].T


def attend(held, keys, attended, scores, weights):
    span = held.shape[1]
    factor = HD ** (-0.5) * 1.4426950408889634
    step = scores[0].shape[0]
    chunk = 16
    steps = held.shape[0] // step

    def score(index, out):
        first = index * step
        queries = pltpu.roll(held[first : first + step].astype(jnp.float32), span - HD, axis=1)
        queries = queries[:, :LANES]
        lane = lax.broadcasted_iota(jnp.int32, queries.shape, 1)
        queries = jnp.where(lane < HD, queries, 0.0).astype(jnp.bfloat16)
        out[...] = jnp.dot(queries, keys[...], preferred_element_type=jnp.float32)

    score(0, scores[0])
    for index in range(steps):
        if index + 1 < steps:
            score(index + 1, scores[(index + 1) % 2])
        now, out = scores[index % 2], weights[index % 2]
        for first in range(0, step, chunk):
            part = now[first : first + chunk]
            top = jnp.max(part, axis=-1, keepdims=True)
            out[first : first + chunk] = jnp.exp2((part - top) * factor).astype(jnp.bfloat16)
        values = jnp.dot(out[...], held[:, span - LANES :], preferred_element_type=jnp.float32)
        first = 2 * HD - (span - LANES)
        values = values / values[:, first + HD : first + HD + 1]
        attended[index * step : (index + 1) * step] = pltpu.roll(values, LANES - first, axis=1)


def packed_rows(count):
    part = round_up(-(-count * (HD - LANES // 2) // LANES), SUBLANES)
    return count // 2 + part, part


def pack(rows):
    count = rows.shape[0]
    half = LANES // 2
    rest = HD - half
    part = packed_rows(count)[1]
    lane = lax.broadcasted_iota(jnp.int32, (count // 2, LANES), 1)
    main = jnp.where(lane < half, rows[: count // 2], pltpu.roll(rows[count // 2 :], half, axis=1))
    lane = lax.broadcasted_iota(jnp.int32, (part, LANES), 1)
    rests = jnp.zeros((part, LANES), jnp.float32)
    for index in range(-(-count // part)):
        piece = rows[index * part : (index + 1) * part]
        if piece.shape[0] < part:
            empty = jnp.zeros((part - piece.shape[0], LANES), jnp.float32)
            piece = jnp.concatenate([piece, empty], axis=0)
        turn = (index * rest + half) % LANES
        piece = pltpu.roll(piece, turn, axis=1) if turn else piece
        rests = jnp.where(lane // rest == index, piece, rests)
    return jnp.concatenate([main, rests], axis=0)


def unpack(block, count):
    half = LANES // 2
    rest = HD - half
    part = packed_rows(count)[1]
    main, rests = block[: count // 2], block[count // 2 : count // 2 + part]
    main = jnp.concatenate([main, pltpu.roll(main, half, axis=1)], axis=0)
    pieces = []
    for index in range(-(-count // part)):
        turn = (half - index * rest) % LANES
        piece = pltpu.roll(rests, turn, axis=1) if turn else rests
        pieces.append(piece[: min(part, count - index * part)])
    lane = lax.broadcasted_iota(jnp.int32, main.shape, 1)
    return jnp.where(lane < half, main, jnp.concatenate(pieces, axis=0))


def packed_tokens(count):
    half = LANES // 2
    total, part = packed_rows(count)
    row = lax.broadcasted_iota(jnp.int32, (total, LANES), 0)
    lane = lax.broadcasted_iota(jnp.int32, (total, LANES), 1)
    main = row + jnp.where(lane < half, 0, count // 2)
    rests = row - count // 2 + lane // (HD - half) * part
    return jnp.where(row < count // 2, main, rests)


def attention_kernel(head, groups, kept_count, mixed_count, *refs):
    kept, mixed = refs[:groups], refs[groups : 2 * groups]
    kept_out, mixed_out, held, keys, attended, *rest = refs[2 * groups :]
    gather(head, kept, kept_count, mixed, mixed_count, held, keys)
    attend(held, keys, attended, rest[:2], rest[2:])
    start = 0
    for count, out in ((kept_count, kept_out), (mixed_count, mixed_out)):
        packed = []
        for _ in range(groups):
            packed.append(pack(attended[start : start + count]))
            start += count
        out[...] = jnp.concatenate(packed, axis=0).astype(jnp.bfloat16)


def select_kernel(split, count, groups, lon_shift, mixed, western, *refs):
    kept, outs = refs[:-groups], refs[-groups:]
    taken = lax.rem(packed_tokens(count), split) < column_offset(lon_shift)
    own, west = mixed[...].astype(jnp.float32), western[...].astype(jnp.float32)
    rests = [rest[...].astype(jnp.float32) for rest in kept]
    size = own.shape[0] // groups
    for group, out in enumerate(outs):
        rows = slice(group * size, (group + 1) * size)
        pieces = [jnp.where(taken, west[rows], own[rows])]
        for rest in rests:
            part = rest.shape[0] // groups
            pieces.append(rest[group * part : (group + 1) * part])
        out[...] = jnp.concatenate(pieces, axis=0).astype(jnp.bfloat16)


def projected(blocks, first, count, weight, shape):
    total = packed_rows(count)[0]
    columns = [unpack(block[first : first + total], count) for block in blocks]
    attended = jnp.concatenate(columns, axis=1).astype(jnp.bfloat16)
    return jnp.dot(attended, weight[...], preferred_element_type=jnp.float32).reshape(shape)


def first_output_kernel(split, groups, field, weight, *refs):
    *blocks, out, second, first = refs
    features = field.shape[2]
    for slot, distance in enumerate(travel_order(groups)):
        group = lax.rem(lax.axis_index("tok") + distance, groups)
        for head, ordered in enumerate((first, second)):
            at = pl.multiple_of((group * HEADS // groups + head) * HD, 16)
            ordered[slot * LANES : slot * LANES + HD] = weight[pl.ds(at, HD)]
            ordered[slot * LANES + HD : (slot + 1) * LANES] = jnp.zeros(
                (LANES - HD, features), jnp.bfloat16
            )
    rows, columns, _ = field.shape
    kept_count, mixed_count = rows * (columns - split), rows * split
    blocks = [block[...].astype(jnp.float32) for block in blocks]
    tokens = field[...].astype(jnp.float32)
    at = packed_rows(mixed_count)[0]
    shape = (rows, split, features)
    left = tokens[:, :split] + projected(blocks, 0, mixed_count, first, shape)
    shape = (rows, columns - split, features)
    right = tokens[:, split:] + projected(blocks, at, kept_count, first, shape)
    at += packed_rows(kept_count)[0]
    right += projected(blocks, at, kept_count, second, shape)
    out[...] = jnp.concatenate([left, right], axis=1)


def second_output_kernel(split, partial, weight, *refs):
    *blocks, out = refs
    rows, _, features = partial.shape
    blocks = [block[...].astype(jnp.float32) for block in blocks]
    tokens = partial[...]
    left = projected(blocks, 0, rows * split, weight, (rows, split, features))
    out[...] = jnp.concatenate(
        [tokens[:, :split] + left, tokens[:, split:]], axis=1
    ).astype(jnp.bfloat16)


def whole(count):
    return [pl.BlockSpec(memory_space=pltpu.VMEM)] * count


def shards(field_tokens, lon_shift, norm_gain, qkv_weight, out_weight):
    _, rows, columns, features = field_tokens.shape
    groups = lax.axis_size("tok")
    local = HEADS // groups
    width = local * HD
    span = round_up(3 * HD + 1, LANES)
    split = round_up(columns // 2, SUBLANES)
    field = field_tokens[0]
    smem = pl.BlockSpec(memory_space=pltpu.SMEM)
    kept_count, mixed_count = rows * (columns - split), rows * split

    def limit(size):
        return pltpu.CompilerParams(vmem_limit_bytes=size * MIB)

    def projection(kernel, count, parts, specs, out_specs, held, params, *operands):
        size = local * dense_rows(count)
        block = jax.ShapeDtypeStruct((size // parts, LANES), jnp.bfloat16)
        return pl.pallas_call(
            functools.partial(kernel, split),
            out_shape=[block] * (parts * groups),
            in_specs=specs,
            out_specs=out_specs,
            scratch_shapes=[
                pltpu.VMEM((groups, size, LANES), jnp.bfloat16),
                *held,
            ],
            compiler_params=params,
            cost_estimate=pl.CostEstimate(
                flops=2 * count * features * 3 * HEADS * HD,
                bytes_accessed=2 * features * (3 * HEADS * HD + 2 * count),
                transcendentals=0,
            ),
        )(*operands)

    def spread(blocks, sign):
        return [blocks[0]] + [
            shifted(block, "tok", sign * distance)
            for block, distance in zip(blocks[1:], travel_order(groups)[1:])
        ]

    eastern = shifted(field[:, :split], "win", -LAT_WINDOWS)
    hbm = pl.BlockSpec(memory_space=pltpu.HBM)
    operands = (field, norm_gain, qkv_weight)
    held = [
        pltpu.VMEM(qkv_weight.shape, qkv_weight.dtype),
        pltpu.SemaphoreType.DMA((CHUNKS * COPIES + 2,)),
        pltpu.VMEM(field.shape, field.dtype),
        pltpu.VMEM(norm_gain.shape, norm_gain.dtype),
    ]
    kept = projection(
        kept_kernel, kept_count, 1, [hbm] * 3, [hbm] * groups, held, limit(60), *operands
    )
    kept = spread(kept, 1)
    specs = [*whole(3), smem, *whole(1)]
    operands += (lon_shift, eastern)
    mixed = projection(
        mixed_kernel, mixed_count, local, specs, whole(local * groups), [], limit(48), *operands
    )
    first_mixed = spread(after(mixed[:groups], [None, *kept[1:]]), 1)
    second_mixed = spread(after(mixed[groups:], [None, *first_mixed[1:]]), 1)

    total = groups * rows * columns
    mixed_packed, kept_packed = packed_rows(mixed_count)[0], packed_rows(kept_count)[0]

    def block(count):
        return jax.ShapeDtypeStruct((count, LANES), jnp.bfloat16)

    def attention(head, step, *blocks):
        return pl.pallas_call(
            functools.partial(attention_kernel, head, groups, kept_count, mixed_count),
            out_shape=[block(groups * kept_packed), block(groups * mixed_packed)],
            in_specs=whole(len(blocks)),
            out_specs=whole(2),
            scratch_shapes=[
                pltpu.VMEM((total, span), jnp.bfloat16),
                pltpu.VMEM((LANES, total), jnp.bfloat16),
                pltpu.VMEM((total, LANES), jnp.float32),
                pltpu.VMEM((step, total), jnp.float32),
                pltpu.VMEM((step, total), jnp.float32),
                pltpu.VMEM((step, total), jnp.bfloat16),
                pltpu.VMEM((step, total), jnp.bfloat16),
            ],
            compiler_params=limit(32),
            cost_estimate=pl.CostEstimate(
                flops=4 * total * total * span,
                bytes_accessed=2 * total * (span + LANES),
                transcendentals=total * total,
            ),
        )(*blocks)

    def back(arrived, mixed_values, *kept_values):
        western = shifted(mixed_values, "win", LAT_WINDOWS)
        selected = pl.pallas_call(
            functools.partial(select_kernel, split, mixed_count, groups),
            out_shape=[block(mixed_packed + len(kept_values) * kept_packed)] * groups,
            in_specs=[smem] + whole(2 + len(kept_values)),
            out_specs=whole(groups),
            compiler_params=limit(16),
            cost_estimate=pl.CostEstimate(
                flops=total * LANES * 20, bytes_accessed=8 * total * LANES, transcendentals=0
            ),
        )(lon_shift, mixed_values, western, *kept_values)
        return spread(after(selected, [None, *arrived]), -1)

    first_kept_values, first_mixed_values = attention(0, total // 5, *kept, *first_mixed)
    second_kept_values, second_mixed_values = attention(1, total // 5, *kept, *second_mixed)
    first = back([], first_mixed_values, first_kept_values, second_kept_values)
    second = back(first[1:], second_mixed_values)

    cost = pl.CostEstimate(
        flops=2 * rows * columns * groups * LANES * features,
        bytes_accessed=features * (HEADS * HD + 6 * rows * columns),
        transcendentals=0,
    )
    ordered = (groups * LANES, features)
    partial, weight = pl.pallas_call(
        functools.partial(first_output_kernel, split, groups),
        out_shape=[
            jax.ShapeDtypeStruct(field.shape, jnp.float32),
            jax.ShapeDtypeStruct(ordered, jnp.bfloat16),
        ],
        in_specs=whole(2 + groups),
        out_specs=whole(2),
        scratch_shapes=[pltpu.VMEM(ordered, jnp.bfloat16)],
        compiler_params=limit(24),
        cost_estimate=cost,
    )(field, out_weight, *first)
    result = pl.pallas_call(
        functools.partial(second_output_kernel, split),
        out_shape=jax.ShapeDtypeStruct(field.shape, jnp.bfloat16),
        in_specs=whole(2 + groups),
        out_specs=pl.BlockSpec(memory_space=pltpu.VMEM),
        compiler_params=limit(24),
        cost_estimate=cost,
    )(partial, weight, *second)
    return result[None]


def solution(mesh):
    placed = (P("win", "tok", None, None), P(), P(), P(), P())
    return jax.shard_map(
        shards, mesh=mesh, in_specs=placed, out_specs=P("win", "tok", None, None), check_vma=False
    )
```

```python
import functools

import jax
import jax.numpy as jnp
from jax import lax
from jax.experimental import pallas as pl
from jax.experimental.pallas import tpu as pltpu
from jax.sharding import PartitionSpec as P

HEADS = 8
HD = 80
LAT_WINDOWS = 4
LANES = 128
SUBLANES = 8
MIB = 1024 * 1024
CHUNKS = 5
COPIES = 1


def round_up(value, unit):
    return -(-value // unit) * unit


def shifted(block, axis, distance):
    count = lax.axis_size(axis)
    return lax.ppermute(block, axis, [(i, (i + distance) % count) for i in range(count)])


def travel_order(groups):
    return [0, *range(groups - 1, 0, -1)]


def after(blocks, arrived):
    return [
        block if other is None else lax.optimization_barrier((block, other))[0]
        for block, other in zip(blocks, arrived)
    ]


def column_offset(lon_shift):
    return lon_shift[lax.rem(lax.axis_index("win"), LAT_WINDOWS)]


SPARE = 2 * LANES - 3 * HD


def dense_rows(count):
    return 2 * count - SPARE


def dense(block):
    count, width = block.shape
    second = block[:, LANES:]
    last = second[count - SPARE :]
    pieces = [last[:, at : at + SPARE] for at in range(0, width - LANES, SPARE)]
    empty = count - SPARE - SPARE * len(pieces)
    if empty:
        pieces.append(jnp.zeros((empty, SPARE), block.dtype))
    filled = jnp.concatenate([second[: count - SPARE], jnp.concatenate(pieces, axis=0)], axis=1)
    return jnp.concatenate([block[:, :LANES], filled], axis=0)


def project(tokens, gain, weight, copies, slots):
    groups = slots.shape[0]
    local = HEADS // groups
    features = tokens.shape[1]
    factor = lax.rsqrt(jnp.mean(tokens * tokens, axis=-1, keepdims=True) + 1e-06)
    normed = (tokens * factor * gain[...].reshape(1, features)).astype(jnp.bfloat16)
    chunk = features // len(copies)
    qkv = None
    for index, copy in enumerate(copies):
        for piece in copy:
            piece.wait()
        inner = slice(index * chunk, (index + 1) * chunk)
        share = jnp.dot(normed[:, inner], weight[inner], preferred_element_type=jnp.float32)
        qkv = share if qkv is None else qkv + share
    qkv = qkv.astype(jnp.bfloat16)
    place = lax.axis_index("tok")
    for group in range(groups):
        slot = lax.rem(place - group + groups, groups)
        blocks = []
        for head in range(group * local, (group + 1) * local):
            columns = [
                qkv[:, (kind * HEADS + head) * HD : (kind * HEADS + head + 1) * HD]
                for kind in (1, 0, 2)
            ]
            blocks.append(dense(jnp.concatenate(columns, axis=1)))
        slots[slot] = jnp.concatenate(blocks, axis=0)


def kept_kernel(split, field, gain, weight, *refs):
    *outs, slots, held_weight, sems, held_field, held_gain = refs
    total = CHUNKS * COPIES
    first = pltpu.make_async_copy(field, held_field, sems.at[total])
    second = pltpu.make_async_copy(gain, held_gain, sems.at[total + 1])
    chunk = weight.shape[0] // total
    pieces = []
    for index in range(total):
        inner = pl.ds(index * chunk, chunk)
        pieces.append(
            pltpu.make_async_copy(weight.at[inner], held_weight.at[inner], sems.at[index])
        )
    for copy in (first, second, *pieces):
        copy.start()
    copies = [pieces[index : index + COPIES] for index in range(0, total, COPIES)]
    first.wait()
    second.wait()
    rows, columns, features = field.shape
    tokens = held_field[...].astype(jnp.float32)[:, split:]
    tokens = tokens.reshape(rows * (columns - split), features)
    project(tokens, held_gain, held_weight, copies, slots)
    copies = [
        pltpu.make_async_copy(slots.at[index], out, sems.at[index])
        for index, out in enumerate(outs)
    ]
    for copy in copies:
        copy.start()
    for copy in copies:
        copy.wait()


def mixed_kernel(split, field, gain, weight, lon_shift, eastern, *refs):
    *outs, slots = refs
    rows, _, features = field.shape
    own = field[...].astype(jnp.float32)[:, :split]
    column = lax.broadcasted_iota(jnp.int32, own.shape, 1)
    tokens = jnp.where(column < column_offset(lon_shift), eastern[...].astype(jnp.float32), own)
    project(tokens.reshape(rows * split, features), gain, weight, [[]], slots)
    groups = slots.shape[0]
    for index, out in enumerate(outs):
        first = index // groups * out.shape[0]
        out[...] = slots[index % groups, first : first + out.shape[0]]


def place_rows(block, first, count, held, start):
    held[start : start + count, :LANES] = block[first : first + count]
    second = block[first + count : first + dense_rows(count)]
    used = LANES - SPARE
    lane = lax.broadcasted_iota(jnp.int32, second.shape, 1)
    ones = jnp.ones(second.shape, second.dtype)
    held[start : start + count - SPARE, LANES:] = jnp.where(lane < used, second, ones)
    pieces = [second[at : at + SPARE, used:] for at in range(0, used, SPARE)]
    pieces.append(jnp.ones((SPARE, SPARE), second.dtype))
    held[start + count - SPARE : start + count, LANES:] = jnp.concatenate(pieces, axis=1)


def gather(head, kept, kept_count, mixed, mixed_count, held, keys):
    start = 0
    for block in kept:
        place_rows(block, head * dense_rows(kept_count), kept_count, held, start)
        start += kept_count
    for block in mixed:
        place_rows(block, 0, mixed_count, held, start)
        start += mixed_count
    keys[...] = held[:, :LANES].T


def attend(held, keys, attended, scores, weights):
    span = held.shape[1]
    factor = HD ** (-0.5) * 1.4426950408889634
    step = scores[0].shape[0]
    chunk = 16
    steps = held.shape[0] // step

    def score(index, out):
        first = index * step
        queries = pltpu.roll(held[first : first + step].astype(jnp.float32), span - HD, axis=1)
        queries = queries[:, :LANES]
        lane = lax.broadcasted_iota(jnp.int32, queries.shape, 1)
        queries = jnp.where(lane < HD, queries, 0.0).astype(jnp.bfloat16)
        out[...] = jnp.dot(queries, keys[...], preferred_element_type=jnp.float32)

    score(0, scores[0])
    for index in range(steps):
        if index + 1 < steps:
            score(index + 1, scores[(index + 1) % 2])
        now, out = scores[index % 2], weights[index % 2]
        for first in range(0, step, chunk):
            part = now[first : first + chunk]
            top = jnp.max(part, axis=-1, keepdims=True)
            out[first : first + chunk] = jnp.exp2((part - top) * factor).astype(jnp.bfloat16)
        values = jnp.dot(out[...], held[:, span - LANES :], preferred_element_type=jnp.float32)
        first = 2 * HD - (span - LANES)
        values = values / values[:, first + HD : first + HD + 1]
        attended[index * step : (index + 1) * step] = pltpu.roll(values, LANES - first, axis=1)


def packed_rows(count):
    part = round_up(-(-count * (HD - LANES // 2) // LANES), SUBLANES)
    return count // 2 + part, part


def pack(rows):
    count = rows.shape[0]
    half = LANES // 2
    rest = HD - half
    part = packed_rows(count)[1]
    lane = lax.broadcasted_iota(jnp.int32, (count // 2, LANES), 1)
    main = jnp.where(lane < half, rows[: count // 2], pltpu.roll(rows[count // 2 :], half, axis=1))
    lane = lax.broadcasted_iota(jnp.int32, (part, LANES), 1)
    rests = jnp.zeros((part, LANES), jnp.float32)
    for index in range(-(-count // part)):
        piece = rows[index * part : (index + 1) * part]
        if piece.shape[0] < part:
            empty = jnp.zeros((part - piece.shape[0], LANES), jnp.float32)
            piece = jnp.concatenate([piece, empty], axis=0)
        turn = (index * rest + half) % LANES
        piece = pltpu.roll(piece, turn, axis=1) if turn else piece
        rests = jnp.where(lane // rest == index, piece, rests)
    return jnp.concatenate([main, rests], axis=0)


def unpack(block, count):
    half = LANES // 2
    rest = HD - half
    part = packed_rows(count)[1]
    main, rests = block[: count // 2], block[count // 2 : count // 2 + part]
    main = jnp.concatenate([main, pltpu.roll(main, half, axis=1)], axis=0)
    pieces = []
    for index in range(-(-count // part)):
        turn = (half - index * rest) % LANES
        piece = pltpu.roll(rests, turn, axis=1) if turn else rests
        pieces.append(piece[: min(part, count - index * part)])
    lane = lax.broadcasted_iota(jnp.int32, main.shape, 1)
    return jnp.where(lane < half, main, jnp.concatenate(pieces, axis=0))


def packed_tokens(count):
    half = LANES // 2
    total, part = packed_rows(count)
    row = lax.broadcasted_iota(jnp.int32, (total, LANES), 0)
    lane = lax.broadcasted_iota(jnp.int32, (total, LANES), 1)
    main = row + jnp.where(lane < half, 0, count // 2)
    rests = row - count // 2 + lane // (HD - half) * part
    return jnp.where(row < count // 2, main, rests)


def attention_kernel(head, groups, kept_count, mixed_count, *refs):
    kept, mixed = refs[:groups], refs[groups : 2 * groups]
    *others, held, keys, attended, s0, s1, w0, w1 = refs[2 * groups :]
    gather(head, kept, kept_count, mixed, mixed_count, held, keys)
    attend(held, keys, attended, (s0, s1), (w0, w1))

    def packed(start, count):
        return [pack(attended[start + at * count : start + (at + 1) * count]) for at in range(groups)]

    right, left = packed(0, kept_count), packed(groups * kept_count, mixed_count)
    if head == 0:
        mixed_out, kept_out = others
        kept_out[...] = jnp.concatenate(right, axis=0).astype(jnp.bfloat16)
    else:
        first, mixed_out, *outs = others
        first = first[...].astype(jnp.float32)
        size = packed_rows(kept_count)[0]
        for group, out in enumerate(outs):
            both = [first[group * size : (group + 1) * size], right[group]]
            out[...] = jnp.concatenate(both, axis=0).astype(jnp.bfloat16)
    mixed_out[...] = jnp.concatenate(left, axis=0).astype(jnp.bfloat16)


def select_kernel(split, count, groups, lon_shift, *refs):
    pairs, outs = refs[:-groups], refs[-groups:]
    taken = lax.rem(packed_tokens(count), split) < column_offset(lon_shift)
    values = [ref[...].astype(jnp.float32) for ref in pairs]
    size = values[0].shape[0] // groups
    for group, out in enumerate(outs):
        rows = slice(group * size, (group + 1) * size)
        chosen = [
            jnp.where(taken, west[rows], own[rows])
            for own, west in zip(values[::2], values[1::2])
        ]
        out[...] = jnp.concatenate(chosen, axis=0).astype(jnp.bfloat16)


def projected(blocks, first, count, weight, shape):
    total = packed_rows(count)[0]
    columns = [unpack(block[first : first + total], count) for block in blocks]
    attended = jnp.concatenate(columns, axis=1).astype(jnp.bfloat16)
    return jnp.dot(attended, weight[...], preferred_element_type=jnp.float32).reshape(shape)


def first_output_kernel(split, groups, field, weight, *refs):
    *blocks, out, first, second = refs
    features = field.shape[2]
    for slot, distance in enumerate(travel_order(groups)):
        group = lax.rem(lax.axis_index("tok") + distance, groups)
        for head, ordered in enumerate((first, second)):
            at = pl.multiple_of((group * HEADS // groups + head) * HD, 16)
            ordered[slot * LANES : slot * LANES + HD] = weight[pl.ds(at, HD)]
            ordered[slot * LANES + HD : (slot + 1) * LANES] = jnp.zeros(
                (LANES - HD, features), jnp.bfloat16
            )
    rows, columns, _ = field.shape
    kept_count = rows * (columns - split)
    blocks = [block[...].astype(jnp.float32) for block in blocks]
    tokens = field[...].astype(jnp.float32)
    shape = (rows, columns - split, features)
    right = tokens[:, split:] + projected(blocks, 0, kept_count, first, shape)
    right += projected(blocks, packed_rows(kept_count)[0], kept_count, second, shape)
    out[...] = jnp.concatenate([tokens[:, :split], right], axis=1)


def second_output_kernel(split, partial, first, second, *refs):
    *blocks, out = refs
    rows, _, features = partial.shape
    blocks = [block[...].astype(jnp.float32) for block in blocks]
    tokens = partial[...]
    count, shape = rows * split, (rows, split, features)
    left = tokens[:, :split] + projected(blocks, 0, count, first, shape)
    left += projected(blocks, packed_rows(count)[0], count, second, shape)
    out[...] = jnp.concatenate([left, tokens[:, split:]], axis=1).astype(jnp.bfloat16)


def whole(count):
    return [pl.BlockSpec(memory_space=pltpu.VMEM)] * count


def shards(field_tokens, lon_shift, norm_gain, qkv_weight, out_weight):
    _, rows, columns, features = field_tokens.shape
    groups = lax.axis_size("tok")
    local = HEADS // groups
    width = local * HD
    span = round_up(3 * HD + 1, LANES)
    split = round_up(columns // 2, SUBLANES)
    field = field_tokens[0]
    smem = pl.BlockSpec(memory_space=pltpu.SMEM)
    kept_count, mixed_count = rows * (columns - split), rows * split

    def limit(size):
        return pltpu.CompilerParams(vmem_limit_bytes=size * MIB)

    def projection(kernel, count, parts, specs, out_specs, held, params, *operands):
        size = local * dense_rows(count)
        block = jax.ShapeDtypeStruct((size // parts, LANES), jnp.bfloat16)
        return pl.pallas_call(
            functools.partial(kernel, split),
            out_shape=[block] * (parts * groups),
            in_specs=specs,
            out_specs=out_specs,
            scratch_shapes=[
                pltpu.VMEM((groups, size, LANES), jnp.bfloat16),
                *held,
            ],
            compiler_params=params,
            cost_estimate=pl.CostEstimate(
                flops=2 * count * features * 3 * HEADS * HD,
                bytes_accessed=2 * features * (3 * HEADS * HD + 2 * count),
                transcendentals=0,
            ),
        )(*operands)

    def spread(blocks, sign):
        return [blocks[0]] + [
            shifted(block, "tok", sign * distance)
            for block, distance in zip(blocks[1:], travel_order(groups)[1:])
        ]

    eastern = shifted(field[:, :split], "win", -LAT_WINDOWS)
    hbm = pl.BlockSpec(memory_space=pltpu.HBM)
    operands = (field, norm_gain, qkv_weight)
    held = [
        pltpu.VMEM(qkv_weight.shape, qkv_weight.dtype),
        pltpu.SemaphoreType.DMA((CHUNKS * COPIES + 2,)),
        pltpu.VMEM(field.shape, field.dtype),
        pltpu.VMEM(norm_gain.shape, norm_gain.dtype),
    ]
    kept = projection(
        kept_kernel, kept_count, 1, [hbm] * 3, [hbm] * groups, held, limit(60), *operands
    )
    kept = spread(kept, 1)
    specs = [*whole(3), smem, *whole(1)]
    operands += (lon_shift, eastern)
    mixed = projection(
        mixed_kernel, mixed_count, local, specs, whole(local * groups), [], limit(48), *operands
    )
    first_mixed = spread(after(mixed[:groups], [None, *kept[1:]]), 1)
    second_mixed = spread(after(mixed[groups:], [None, *first_mixed[1:]]), 1)

    total = groups * rows * columns
    mixed_packed, kept_packed = packed_rows(mixed_count)[0], packed_rows(kept_count)[0]

    def block(count):
        return jax.ShapeDtypeStruct((count, LANES), jnp.bfloat16)

    def attention(head, out_shape, *blocks):
        step = total // 5
        return pl.pallas_call(
            functools.partial(attention_kernel, head, groups, kept_count, mixed_count),
            out_shape=out_shape,
            in_specs=whole(len(blocks)),
            out_specs=whole(len(out_shape)),
            scratch_shapes=[
                pltpu.VMEM((total, span), jnp.bfloat16),
                pltpu.VMEM((LANES, total), jnp.bfloat16),
                pltpu.VMEM((total, LANES), jnp.float32),
                pltpu.VMEM((step, total), jnp.float32),
                pltpu.VMEM((step, total), jnp.float32),
                pltpu.VMEM((step, total), jnp.bfloat16),
                pltpu.VMEM((step, total), jnp.bfloat16),
            ],
            compiler_params=limit(32),
            cost_estimate=pl.CostEstimate(
                flops=4 * total * total * span,
                bytes_accessed=2 * total * (span + LANES),
                transcendentals=total * total,
            ),
        )(*blocks)

    values = block(groups * mixed_packed)
    first_values, kept_values = attention(
        0, [values, block(groups * kept_packed)], *kept, *first_mixed
    )
    first_western = shifted(first_values, "win", LAT_WINDOWS)
    second_values, *kept_values = attention(
        1, [values] + [block(2 * kept_packed)] * groups, *kept, *second_mixed, kept_values
    )
    second_western = shifted(second_values, "win", LAT_WINDOWS)
    first = spread(kept_values, -1)
    selected = pl.pallas_call(
        functools.partial(select_kernel, split, mixed_count, groups),
        out_shape=[block(2 * mixed_packed)] * groups,
        in_specs=[smem] + whole(4),
        out_specs=whole(groups),
        compiler_params=limit(16),
        cost_estimate=pl.CostEstimate(
            flops=total * LANES * 20, bytes_accessed=8 * total * LANES, transcendentals=0
        ),
    )(lon_shift, first_values, first_western, second_values, second_western)
    second = spread(selected, -1)

    cost = pl.CostEstimate(
        flops=2 * rows * columns * groups * LANES * features,
        bytes_accessed=features * (HEADS * HD + 6 * rows * columns),
        transcendentals=0,
    )
    ordered = (groups * LANES, features)
    partial, *weights = pl.pallas_call(
        functools.partial(first_output_kernel, split, groups),
        out_shape=[
            jax.ShapeDtypeStruct(field.shape, jnp.float32),
            jax.ShapeDtypeStruct(ordered, jnp.bfloat16),
            jax.ShapeDtypeStruct(ordered, jnp.bfloat16),
        ],
        in_specs=whole(2 + groups),
        out_specs=whole(3),
        compiler_params=limit(24),
        cost_estimate=cost,
    )(field, out_weight, *first)
    result = pl.pallas_call(
        functools.partial(second_output_kernel, split),
        out_shape=jax.ShapeDtypeStruct(field.shape, jnp.bfloat16),
        in_specs=whole(3 + groups),
        out_specs=pl.BlockSpec(memory_space=pltpu.VMEM),
        compiler_params=limit(24),
        cost_estimate=cost,
    )(partial, *weights, *second)
    return result[None]


def solution(mesh):
    placed = (P("win", "tok", None, None), P(), P(), P(), P())
    return jax.shard_map(
        shards, mesh=mesh, in_specs=placed, out_specs=P("win", "tok", None, None), check_vma=False
    )
```

```python
import functools

import jax
import jax.numpy as jnp
from jax import lax
from jax.experimental import pallas as pl
from jax.experimental.pallas import tpu as pltpu
from jax.sharding import PartitionSpec as P

HEADS = 8
HD = 80
LAT_WINDOWS = 4
LANES = 128
SUBLANES = 8
MIB = 1024 * 1024
CHUNKS = 5
COPIES = 1


def round_up(value, unit):
    return -(-value // unit) * unit


def shifted(block, axis, distance):
    count = lax.axis_size(axis)
    return lax.ppermute(block, axis, [(i, (i + distance) % count) for i in range(count)])


def travel_order(groups):
    return [0, *range(groups - 1, 0, -1)]


def after(blocks, arrived):
    return [
        block if other is None else lax.optimization_barrier((block, other))[0]
        for block, other in zip(blocks, arrived)
    ]


def column_offset(lon_shift):
    return lon_shift[lax.rem(lax.axis_index("win"), LAT_WINDOWS)]


SPARE = 2 * LANES - 3 * HD


def dense_rows(count):
    return 2 * count - SPARE


def dense(block):
    count, width = block.shape
    second = block[:, LANES:]
    last = second[count - SPARE :]
    pieces = [last[:, at : at + SPARE] for at in range(0, width - LANES, SPARE)]
    empty = count - SPARE - SPARE * len(pieces)
    if empty:
        pieces.append(jnp.zeros((empty, SPARE), block.dtype))
    filled = jnp.concatenate([second[: count - SPARE], jnp.concatenate(pieces, axis=0)], axis=1)
    return jnp.concatenate([block[:, :LANES], filled], axis=0)


def project(tokens, gain, weight, copies, slots):
    groups = slots.shape[0]
    local = HEADS // groups
    features = tokens.shape[1]
    factor = lax.rsqrt(jnp.mean(tokens * tokens, axis=-1, keepdims=True) + 1e-06)
    normed = (tokens * factor * gain[...].reshape(1, features)).astype(jnp.bfloat16)
    chunk = features // len(copies)
    qkv = None
    for index, copy in enumerate(copies):
        for piece in copy:
            piece.wait()
        inner = slice(index * chunk, (index + 1) * chunk)
        share = jnp.dot(normed[:, inner], weight[inner], preferred_element_type=jnp.float32)
        qkv = share if qkv is None else qkv + share
    qkv = qkv.astype(jnp.bfloat16)
    place = lax.axis_index("tok")
    for group in range(groups):
        slot = lax.rem(place - group + groups, groups)
        blocks = []
        for head in range(group * local, (group + 1) * local):
            columns = [
                qkv[:, (kind * HEADS + head) * HD : (kind * HEADS + head + 1) * HD]
                for kind in (1, 0, 2)
            ]
            blocks.append(dense(jnp.concatenate(columns, axis=1)))
        slots[slot] = jnp.concatenate(blocks, axis=0)


def kept_kernel(split, field, gain, weight, *refs):
    *outs, slots, held_weight, sems, held_field, held_gain = refs
    total = CHUNKS * COPIES
    first = pltpu.make_async_copy(field, held_field, sems.at[total])
    second = pltpu.make_async_copy(gain, held_gain, sems.at[total + 1])
    chunk = weight.shape[0] // total
    pieces = []
    for index in range(total):
        inner = pl.ds(index * chunk, chunk)
        pieces.append(
            pltpu.make_async_copy(weight.at[inner], held_weight.at[inner], sems.at[index])
        )
    for copy in (first, second, *pieces):
        copy.start()
    copies = [pieces[index : index + COPIES] for index in range(0, total, COPIES)]
    first.wait()
    second.wait()
    rows, columns, features = field.shape
    tokens = held_field[...].astype(jnp.float32)[:, split:]
    tokens = tokens.reshape(rows * (columns - split), features)
    project(tokens, held_gain, held_weight, copies, slots)
    copies = [
        pltpu.make_async_copy(slots.at[index], out, sems.at[index])
        for index, out in enumerate(outs)
    ]
    for copy in copies:
        copy.start()
    for copy in copies:
        copy.wait()


def mixed_kernel(split, field, gain, weight, lon_shift, eastern, *refs):
    *outs, slots = refs
    rows, _, features = field.shape
    own = field[...].astype(jnp.float32)[:, :split]
    column = lax.broadcasted_iota(jnp.int32, own.shape, 1)
    tokens = jnp.where(column < column_offset(lon_shift), eastern[...].astype(jnp.float32), own)
    project(tokens.reshape(rows * split, features), gain, weight, [[]], slots)
    groups = slots.shape[0]
    for index, out in enumerate(outs):
        first = index // groups * out.shape[0]
        out[...] = slots[index % groups, first : first + out.shape[0]]


def place_rows(block, first, count, held, start):
    held[start : start + count, :LANES] = block[first : first + count]
    second = block[first + count : first + dense_rows(count)]
    used = LANES - SPARE
    lane = lax.broadcasted_iota(jnp.int32, second.shape, 1)
    ones = jnp.ones(second.shape, second.dtype)
    held[start : start + count - SPARE, LANES:] = jnp.where(lane < used, second, ones)
    pieces = [second[at : at + SPARE, used:] for at in range(0, used, SPARE)]
    pieces.append(jnp.ones((SPARE, SPARE), second.dtype))
    held[start + count - SPARE : start + count, LANES:] = jnp.concatenate(pieces, axis=1)


def gather(head, kept, kept_count, mixed, mixed_count, held, keys):
    start = 0
    for block in kept:
        place_rows(block, head * dense_rows(kept_count), kept_count, held, start)
        start += kept_count
    for block in mixed:
        place_rows(block, 0, mixed_count, held, start)
        start += mixed_count
    keys[...] = held[:, :LANES].T


def attend(held, keys, attended, scores, weights):
    span = held.shape[1]
    factor = HD ** (-0.5) * 1.4426950408889634
    step = scores[0].shape[0]
    chunk = 16
    steps = held.shape[0] // step

    def score(index, out):
        first = index * step
        queries = pltpu.roll(held[first : first + step].astype(jnp.float32), span - HD, axis=1)
        queries = queries[:, :LANES]
        lane = lax.broadcasted_iota(jnp.int32, queries.shape, 1)
        queries = jnp.where(lane < HD, queries, 0.0).astype(jnp.bfloat16)
        out[...] = jnp.dot(queries, keys[...], preferred_element_type=jnp.float32)

    score(0, scores[0])
    for index in range(steps):
        if index + 1 < steps:
            score(index + 1, scores[(index + 1) % 2])
        now, out = scores[index % 2], weights[index % 2]
        for first in range(0, step, chunk):
            part = now[first : first + chunk]
            top = jnp.max(part, axis=-1, keepdims=True)
            out[first : first + chunk] = jnp.exp2((part - top) * factor).astype(jnp.bfloat16)
        values = jnp.dot(out[...], held[:, span - LANES :], preferred_element_type=jnp.float32)
        first = 2 * HD - (span - LANES)
        values = values / values[:, first + HD : first + HD + 1]
        attended[index * step : (index + 1) * step] = pltpu.roll(values, LANES - first, axis=1)


def packed_rows(count):
    part = round_up(-(-count * (HD - LANES // 2) // LANES), SUBLANES)
    return count // 2 + part, part


def pack(rows):
    count = rows.shape[0]
    half = LANES // 2
    rest = HD - half
    part = packed_rows(count)[1]
    lane = lax.broadcasted_iota(jnp.int32, (count // 2, LANES), 1)
    main = jnp.where(lane < half, rows[: count // 2], pltpu.roll(rows[count // 2 :], half, axis=1))
    lane = lax.broadcasted_iota(jnp.int32, (part, LANES), 1)
    rests = jnp.zeros((part, LANES), jnp.float32)
    for index in range(-(-count // part)):
        piece = rows[index * part : (index + 1) * part]
        if piece.shape[0] < part:
            empty = jnp.zeros((part - piece.shape[0], LANES), jnp.float32)
            piece = jnp.concatenate([piece, empty], axis=0)
        turn = (index * rest + half) % LANES
        piece = pltpu.roll(piece, turn, axis=1) if turn else piece
        rests = jnp.where(lane // rest == index, piece, rests)
    return jnp.concatenate([main, rests], axis=0)


def unpack(block, count):
    half = LANES // 2
    rest = HD - half
    part = packed_rows(count)[1]
    main, rests = block[: count // 2], block[count // 2 : count // 2 + part]
    main = jnp.concatenate([main, pltpu.roll(main, half, axis=1)], axis=0)
    pieces = []
    for index in range(-(-count // part)):
        turn = (half - index * rest) % LANES
        piece = pltpu.roll(rests, turn, axis=1) if turn else rests
        pieces.append(piece[: min(part, count - index * part)])
    lane = lax.broadcasted_iota(jnp.int32, main.shape, 1)
    return jnp.where(lane < half, main, jnp.concatenate(pieces, axis=0))


def packed_tokens(count):
    half = LANES // 2
    total, part = packed_rows(count)
    row = lax.broadcasted_iota(jnp.int32, (total, LANES), 0)
    lane = lax.broadcasted_iota(jnp.int32, (total, LANES), 1)
    main = row + jnp.where(lane < half, 0, count // 2)
    rests = row - count // 2 + lane // (HD - half) * part
    return jnp.where(row < count // 2, main, rests)


def attention_kernel(head, groups, kept_count, mixed_count, *refs):
    kept, mixed = refs[:groups], refs[groups : 2 * groups]
    *others, held, keys, attended, s0, s1, w0, w1 = refs[2 * groups :]
    gather(head, kept, kept_count, mixed, mixed_count, held, keys)
    attend(held, keys, attended, (s0, s1), (w0, w1))

    def packed(start, count):
        return [pack(attended[start + at * count : start + (at + 1) * count]) for at in range(groups)]

    right, left = packed(0, kept_count), packed(groups * kept_count, mixed_count)
    if head == 0:
        mixed_out, kept_out = others
        kept_out[...] = jnp.concatenate(right, axis=0).astype(jnp.bfloat16)
    else:
        first, mixed_out, *outs = others
        first = first[...].astype(jnp.float32)
        size = packed_rows(kept_count)[0]
        for group, out in enumerate(outs):
            both = [first[group * size : (group + 1) * size], right[group]]
            out[...] = jnp.concatenate(both, axis=0).astype(jnp.bfloat16)
    mixed_out[...] = jnp.concatenate(left, axis=0).astype(jnp.bfloat16)


def select_kernel(split, count, groups, lon_shift, *refs):
    pairs, outs = refs[:-groups], refs[-groups:]
    taken = lax.rem(packed_tokens(count), split) < column_offset(lon_shift)
    values = [ref[...].astype(jnp.float32) for ref in pairs]
    size = values[0].shape[0] // groups
    for group, out in enumerate(outs):
        rows = slice(group * size, (group + 1) * size)
        chosen = [
            jnp.where(taken, west[rows], own[rows])
            for own, west in zip(values[::2], values[1::2])
        ]
        out[...] = jnp.concatenate(chosen, axis=0).astype(jnp.bfloat16)


def projected(blocks, first, count, weight, shape):
    total = packed_rows(count)[0]
    columns = [unpack(block[first : first + total], count) for block in blocks]
    attended = jnp.concatenate(columns, axis=1).astype(jnp.bfloat16)
    return jnp.dot(attended, weight[...], preferred_element_type=jnp.float32).reshape(shape)


def first_output_kernel(split, groups, field, weight, *refs):
    *blocks, out, first, second = refs
    features = field.shape[2]
    for slot, distance in enumerate(travel_order(groups)):
        group = lax.rem(lax.axis_index("tok") + distance, groups)
        for head, ordered in enumerate((first, second)):
            at = pl.multiple_of((group * HEADS // groups + head) * HD, 16)
            ordered[slot * LANES : slot * LANES + HD] = weight[pl.ds(at, HD)]
            ordered[slot * LANES + HD : (slot + 1) * LANES] = jnp.zeros(
                (LANES - HD, features), jnp.bfloat16
            )
    rows, columns, _ = field.shape
    kept_count = rows * (columns - split)
    blocks = [block[...].astype(jnp.float32) for block in blocks]
    tokens = field[...].astype(jnp.float32)
    shape = (rows, columns - split, features)
    right = tokens[:, split:] + projected(blocks, 0, kept_count, first, shape)
    right += projected(blocks, packed_rows(kept_count)[0], kept_count, second, shape)
    out[...] = jnp.concatenate([tokens[:, :split], right], axis=1)


def second_output_kernel(split, partial, first, second, *refs):
    *blocks, out, held, sems = refs
    rows, _, features = partial.shape
    blocks = [block[...].astype(jnp.float32) for block in blocks]
    count, shape = rows * split, (rows, split, features)
    left = projected(blocks, 0, count, first, shape)
    left += projected(blocks, packed_rows(count)[0], count, second, shape)
    copies = []
    for start, size in ((0, rows // 2), (rows // 2, rows - rows // 2)):
        end = start + size
        tokens = partial[start:end]
        held[start:end] = jnp.concatenate(
            [tokens[:, :split] + left[start:end], tokens[:, split:]], axis=1
        ).astype(jnp.bfloat16)
        part = pl.ds(start, size)
        copies.append(pltpu.make_async_copy(held.at[part], out.at[part], sems.at[len(copies)]))
        copies[-1].start()
    for copy in copies:
        copy.wait()


def whole(count):
    return [pl.BlockSpec(memory_space=pltpu.VMEM)] * count


def shards(field_tokens, lon_shift, norm_gain, qkv_weight, out_weight):
    _, rows, columns, features = field_tokens.shape
    groups = lax.axis_size("tok")
    local = HEADS // groups
    width = local * HD
    span = round_up(3 * HD + 1, LANES)
    split = round_up(columns // 2, SUBLANES)
    field = field_tokens[0]
    smem = pl.BlockSpec(memory_space=pltpu.SMEM)
    kept_count, mixed_count = rows * (columns - split), rows * split

    def limit(size):
        return pltpu.CompilerParams(vmem_limit_bytes=size * MIB)

    def projection(kernel, count, parts, specs, out_specs, held, params, *operands):
        size = local * dense_rows(count)
        block = jax.ShapeDtypeStruct((size // parts, LANES), jnp.bfloat16)
        return pl.pallas_call(
            functools.partial(kernel, split),
            out_shape=[block] * (parts * groups),
            in_specs=specs,
            out_specs=out_specs,
            scratch_shapes=[
                pltpu.VMEM((groups, size, LANES), jnp.bfloat16),
                *held,
            ],
            compiler_params=params,
            cost_estimate=pl.CostEstimate(
                flops=2 * count * features * 3 * HEADS * HD,
                bytes_accessed=2 * features * (3 * HEADS * HD + 2 * count),
                transcendentals=0,
            ),
        )(*operands)

    def spread(blocks, sign):
        return [blocks[0]] + [
            shifted(block, "tok", sign * distance)
            for block, distance in zip(blocks[1:], travel_order(groups)[1:])
        ]

    eastern = shifted(field[:, :split], "win", -LAT_WINDOWS)
    hbm = pl.BlockSpec(memory_space=pltpu.HBM)
    operands = (field, norm_gain, qkv_weight)
    held = [
        pltpu.VMEM(qkv_weight.shape, qkv_weight.dtype),
        pltpu.SemaphoreType.DMA((CHUNKS * COPIES + 2,)),
        pltpu.VMEM(field.shape, field.dtype),
        pltpu.VMEM(norm_gain.shape, norm_gain.dtype),
    ]
    kept = projection(
        kept_kernel, kept_count, 1, [hbm] * 3, [hbm] * groups, held, limit(60), *operands
    )
    kept = spread(kept, 1)
    specs = [*whole(3), smem, *whole(1)]
    operands += (lon_shift, eastern)
    mixed = projection(
        mixed_kernel, mixed_count, local, specs, whole(local * groups), [], limit(48), *operands
    )
    first_mixed = spread(after(mixed[:groups], [None, *kept[1:]]), 1)
    second_mixed = spread(after(mixed[groups:], [None, *first_mixed[1:]]), 1)

    total = groups * rows * columns
    mixed_packed, kept_packed = packed_rows(mixed_count)[0], packed_rows(kept_count)[0]

    def block(count):
        return jax.ShapeDtypeStruct((count, LANES), jnp.bfloat16)

    def attention(head, out_shape, *blocks):
        step = total // 5
        return pl.pallas_call(
            functools.partial(attention_kernel, head, groups, kept_count, mixed_count),
            out_shape=out_shape,
            in_specs=whole(len(blocks)),
            out_specs=whole(len(out_shape)),
            scratch_shapes=[
                pltpu.VMEM((total, span), jnp.bfloat16),
                pltpu.VMEM((LANES, total), jnp.bfloat16),
                pltpu.VMEM((total, LANES), jnp.float32),
                pltpu.VMEM((step, total), jnp.float32),
                pltpu.VMEM((step, total), jnp.float32),
                pltpu.VMEM((step, total), jnp.bfloat16),
                pltpu.VMEM((step, total), jnp.bfloat16),
            ],
            compiler_params=limit(32),
            cost_estimate=pl.CostEstimate(
                flops=4 * total * total * span,
                bytes_accessed=2 * total * (span + LANES),
                transcendentals=total * total,
            ),
        )(*blocks)

    values = block(groups * mixed_packed)
    first_values, kept_values = attention(
        0, [values, block(groups * kept_packed)], *kept, *first_mixed
    )
    first_western = shifted(first_values, "win", LAT_WINDOWS)
    second_values, *kept_values = attention(
        1, [values] + [block(2 * kept_packed)] * groups, *kept, *second_mixed, kept_values
    )
    second_western = shifted(second_values, "win", LAT_WINDOWS)
    first = spread(kept_values, -1)
    selected = pl.pallas_call(
        functools.partial(select_kernel, split, mixed_count, groups),
        out_shape=[block(2 * mixed_packed)] * groups,
        in_specs=[smem] + whole(4),
        out_specs=whole(groups),
        compiler_params=limit(16),
        cost_estimate=pl.CostEstimate(
            flops=total * LANES * 20, bytes_accessed=8 * total * LANES, transcendentals=0
        ),
    )(lon_shift, first_values, first_western, second_values, second_western)
    second = spread(selected, -1)

    cost = pl.CostEstimate(
        flops=2 * rows * columns * groups * LANES * features,
        bytes_accessed=features * (HEADS * HD + 6 * rows * columns),
        transcendentals=0,
    )
    ordered = (groups * LANES, features)
    partial, *weights = pl.pallas_call(
        functools.partial(first_output_kernel, split, groups),
        out_shape=[
            jax.ShapeDtypeStruct(field.shape, jnp.float32),
            jax.ShapeDtypeStruct(ordered, jnp.bfloat16),
            jax.ShapeDtypeStruct(ordered, jnp.bfloat16),
        ],
        in_specs=whole(2 + groups),
        out_specs=whole(3),
        compiler_params=limit(24),
        cost_estimate=cost,
    )(field, out_weight, *first)
    result = pl.pallas_call(
        functools.partial(second_output_kernel, split),
        out_shape=jax.ShapeDtypeStruct(field.shape, jnp.bfloat16),
        in_specs=whole(3 + groups),
        out_specs=hbm,
        scratch_shapes=[
            pltpu.VMEM(field.shape, jnp.bfloat16),
            pltpu.SemaphoreType.DMA((2,)),
        ],
        compiler_params=limit(24),
        cost_estimate=cost,
    )(partial, *weights, *second)
    return result[None]


def solution(mesh):
    placed = (P("win", "tok", None, None), P(), P(), P(), P())
    return jax.shard_map(
        shards, mesh=mesh, in_specs=placed, out_specs=P("win", "tok", None, None), check_vma=False
    )
```
